512 devices in a mesh: grp: 16 (over y, z_hi), dev: 32 (over x, z_lo, core).
Axes of the slice: x: 4, y: 8, z: 8 (z_hi: 2, z_lo: 4; z = z_hi * 4 + z_lo), core: 2. Of those that a mesh axis runs over, the one named last changes fastest.
Arguments:
- acts: bfloat16 [262144, 1024], P(('grp', 'dev')), may hold values from -48 to 48
- out_grads: bfloat16 [262144, 1024], P(('grp', 'dev')), may hold values from -0.01171875 to 0.01171875
- old_act_factor: float32 [1024, 1024], P('dev'), may hold values from -3 to 3
- old_grad_factor: float32 [1024, 1024], P('dev'), may hold values from -3 to 3
- act_basis: bfloat16 [1024, 1024], P('dev'), may hold values from -0.1875 to 0.1875
- grad_basis: bfloat16 [1024, 1024], P('dev'), may hold values from -0.1875 to 0.1875
- act_eigs: float32 [1024], P('dev'), may hold values from 0.3 to 3
- grad_eigs: float32 [1024], replicated, may hold values from 0.3 to 3
- sample_index: int32 [1024], P(('grp', 'dev')), may hold values from 0 to 511
Outputs:
- precond: float32 [1024, 1024], P('dev')
- act_factor: float32 [1024, 1024], P('dev')
- grad_factor: float32 [1024, 1024], P('dev')
The draws below stay inside these ranges and needn't reach their ends.
Inputs may be any that keep to these rules, and one draw needn't show every extreme that they name: `sample_index`: every entry indexes a token of the device that holds the entry.
All inputs are finite; a program needn't handle non-finite values.
Results may differ from the reference program's by a relative error of at most 0.0059.
Values may be sent and summed in bfloat16 or wider, within the bound.
A program may use at most 64 MiB of HBM per device.

```python
import math
import jax
import jax.numpy as jnp
from jax import lax

D = 1024
TOK_DEV = 512
SAMPLES = 2
TOKENS = 262144
NSAMP = 1024
N_GRP = 16
N_DEV = 32


def plant(values, own_key, low, high):
    extent = values.shape
    spot = [jax.random.randint(jax.random.fold_in(own_key, axis), (), 0, extent[axis]) for axis in range(len(extent))]
    values = values.at[tuple(spot)].set(low)
    longest = extent.index(max(extent))
    spot[longest] = (spot[longest] + 1) % extent[longest]
    return values.at[tuple(spot)].set(high)


def raised(drawn, rng, source, target, parts, factor):
    def block_of(axis_at):
        return (jnp.arange(drawn.shape[axis_at]) // (drawn.shape[axis_at] // parts)).reshape((-1,) + (1,) * (drawn.ndim - 1 - axis_at))

    one_side = jax.random.permutation(rng, parts)[block_of(target)]
    second = (block_of(target) + parts // 2) % parts
    return jnp.where((block_of(source) == one_side) | (block_of(source) == second), factor * drawn, drawn)


def block_levels(rng, extent, shards, low, top_value):
    factor_of = 1.0
    for axis_at, blocks in shards:
        steps = jax.random.uniform(jax.random.fold_in(jax.random.fold_in(rng, 6), axis_at), (blocks,), jnp.float32, low / len(shards), top_value / len(shards))
        factor_of = factor_of * jnp.repeat(jnp.exp(steps), extent[axis_at] // blocks).reshape((-1,) + (1,) * (len(extent) - 1 - axis_at))
    return factor_of


def centred(key, dims, spread, most, split=(), kind=jnp.bfloat16):
    array = jax.random.normal(key, dims, jnp.float32) * spread
    if len(split) > 0:
        array = block_levels(key, dims, split, -0.22, 0.18) * array
    return jnp.clip(array, min=-most, max=most).astype(kind)


def heavy_noise(own_key, extent, scale, reach, split, heavy, kind=jnp.bfloat16):
    result = scale * jax.random.normal(own_key, extent, jnp.float32)
    if split:
        result = result * block_levels(own_key, extent, split, -0.22, 0.18)
    return jnp.clip(raised(result, jax.random.fold_in(own_key, 3), *heavy), -reach, reach).astype(kind)


def setup_inputs(seed: int = 0) -> dict:
    key_of = jax.random.split(jax.random.key(seed), 10)
    acts = heavy_noise(key_of[0], (TOKENS, D), 2.0, 48.0, ((0, 512),), (0, 1, 512, 6.0))
    out_grads = centred(key_of[1], (TOKENS, D), (TOKENS ** -0.5), 0.01171875, ((0, 512),))
    old_act_factor = centred(key_of[2], (D, D), 0.5, 3.0, ((0, 32),), jnp.float32)
    old_grad_factor = centred(key_of[3], (D, D), 0.5, 3.0, ((0, 32),), jnp.float32)
    act_basis = centred(key_of[4], (D, D), D ** -0.5, 0.1875, ((0, 32),))
    grad_basis = centred(key_of[5], (D, D), D ** -0.5, 0.1875, ((0, 32),))
    act_eigs = jnp.clip(jnp.exp(math.log(3.0) - 2.3025851 * jax.random.uniform(key_of[6], (D,), jnp.float32) ** block_levels(key_of[6], (D,), ((0, 32),), -0.2, 0.2)), 0.3, 3.0)
    grad_eigs = jnp.clip(jnp.exp(jax.random.uniform(key_of[7], (D,), jnp.float32, math.log(0.3), math.log(3.0))), 0.3, 3.0)
    sample_index = plant(jax.random.randint(key_of[8], (NSAMP,), 0, TOK_DEV), jax.random.fold_in(key_of[8], 1), 0, TOK_DEV - 1).astype(jnp.int32)
    return {"acts": acts, "out_grads": out_grads, "old_act_factor": old_act_factor, "old_grad_factor": old_grad_factor, "act_basis": act_basis, "grad_basis": grad_basis, "act_eigs": act_eigs, "grad_eigs": grad_eigs, "sample_index": sample_index}


def reference(acts, out_grads, old_act_factor, old_grad_factor, act_basis, grad_basis, act_eigs, grad_eigs, sample_index):
    device_count = N_GRP * N_DEV
    act_blocks = acts.reshape(device_count, TOK_DEV, D)
    grad_blocks = out_grads.reshape(device_count, TOK_DEV, D)
    basis_wide = act_basis.astype(jnp.float32)

    def add_term(running, pair):
        act_one, grad_one = pair
        proj = jnp.dot(act_one.astype(jnp.float32), basis_wide, precision=lax.Precision.HIGHEST).astype(jnp.bfloat16)
        term = jnp.dot(proj.astype(jnp.float32).T, grad_one.astype(jnp.float32), precision=lax.Precision.HIGHEST)
        return running + term, None

    rotated_sum, unused = lax.scan(add_term, jnp.zeros((D, D), jnp.float32), (act_blocks, grad_blocks))
    rotated = rotated_sum.astype(jnp.bfloat16)

    picked = sample_index.reshape(device_count, SAMPLES).astype(jnp.int32)
    owners = jnp.arange(device_count, dtype=jnp.int32)[:, None]
    picked_acts = act_blocks[owners, picked].reshape(NSAMP, D)
    picked_grads = grad_blocks[owners, picked].reshape(NSAMP, D)
    act_stat = jnp.dot(picked_acts.T, picked_acts, preferred_element_type=jnp.float32)
    grad_stat = jnp.dot(picked_grads.T, picked_grads, preferred_element_type=jnp.float32)
    act_factor = 0.75 * old_act_factor + (0.25 / NSAMP) * act_stat
    grad_factor = 0.75 * old_grad_factor + (0.25 * TOKENS / NSAMP) * grad_stat

    turned = jnp.dot(rotated, grad_basis, preferred_element_type=jnp.float32)
    scaled = (turned / (act_eigs[:, None] * grad_eigs[None, :] + 0.1)).astype(jnp.bfloat16)
    restored = jnp.dot(scaled, grad_basis.T, preferred_element_type=jnp.float32).astype(jnp.bfloat16)
    precond = jnp.dot(act_basis, restored, preferred_element_type=jnp.float32)
    return precond, act_factor, grad_factor
```

```python
import functools

import jax
import jax.numpy as jnp
from jax import lax
from jax.experimental import pallas as pl
from jax.experimental.pallas import tpu as pltpu
from jax.sharding import PartitionSpec as P

NX, NY, NZ, ZL = 4, 8, 8, 4
D, TOK = 1024, 512
HALF = D // 2
CHUNKS, CW = 4, 256
BF, F32 = jnp.bfloat16, jnp.float32
DX = (1, 3, 2)
DY = (1, 7, 2, 6, 3, 5, 4)
DZ = (1, 7, 2, 6, 3, 5, 4)
DZL = (1, 7, 2)
DXC = tuple((dx, dc) for dx in (0, 1, 3, 2) for dc in (0, 1) if (dx, dc) != (0, 0))


def dot(left, right, dims=(((1,), (0,)), ((), ()))):
    return lax.dot_general(left, right, dims, preferred_element_type=F32)


def kernel(
    idx_hbm, acts_ref, grads_ref, a_hbm, b_ref, aeig_hbm, geig_hbm,
    out_ref,
    idx_ref, a_ref, aeig_ref, geig_ref,
    acts_v, grads_v, aperm, abuf, projt,
    tbuf, sendx1, recvx1, sendx2, recvx2, sendz, recvz, sendy, recvy,
    bcol, tsend, trecv, rbuf, obuf,
    picks, pbuf, pwide, xbuf, sfull, ssend, srecv, szsend, szrecv, sout,
    lsem, ssem, rsem,
):
    grp, dev = lax.axis_index("grp"), lax.axis_index("dev")
    y, zh = grp // 2, grp % 2
    x, zl, c = dev // 8, (dev // 2) % 4, dev % 2
    z = zh * ZL + zl

    def at(px, py, pz, pc):
        return {"grp": py * 2 + pz // ZL, "dev": px * 8 + (pz % ZL) * 2 + pc}

    def to_x(step):
        return at((x + step) % NX, y, z, c)

    def to_y(step):
        return at(x, (y + step) % NY, z, c)

    def to_z(step):
        return at(x, y, (z + step) % NZ, c)

    def to_xc(step):
        return at((x + step[0]) % NX, y, z, (c + step[1]) % 2)

    sibling = at(x, y, z, 1 - c)
    slot_z = (z % ZL) * 2 + z // ZL

    counter = [0]
    pending = []

    def send(moves, like):
        n = counter[0]
        counter[0] += 1

        def copy(src, dst, target):
            return pltpu.make_async_remote_copy(
                src_ref=src, dst_ref=dst, send_sem=ssem.at[n], recv_sem=rsem.at[n],
                device_id=target, device_id_type=pl.DeviceIdType.MESH,
            )

        for move in moves:
            copy(*move).start()
        whole = copy(like, like, sibling)
        pending.append(whole)
        return whole

    def gather(ref, targets, like):
        return send([(ref, ref, target) for target in targets], like)

    def drain():
        for copy in pending:
            copy.wait_send()
        pending.clear()

    all_x = [to_x(s) for s in DX]
    all_y = [to_y(s) for s in DY]
    all_z = [to_z(s) for s in DZ]
    all_zl = [to_z(s) for s in DZL]
    all_xc = [to_xc(s) for s in DXC]
    x_up, x_down, x_far = (x + 1) % NX, (x + 3) % NX, (x + 2) % NX
    zl_up, zl_down = (zl + 1) % ZL, (zl + 3) % ZL

    barrier = pltpu.get_barrier_semaphore()
    partners = all_xc + all_y + all_z
    for partner in partners:
        pl.semaphore_signal(
            barrier, inc=1, device_id=partner, device_id_type=pl.DeviceIdType.MESH
        )

    own = [
        pltpu.make_async_copy(src, dst, lsem.at[i])
        for i, (src, dst) in enumerate((
            (a_hbm, a_ref), (idx_hbm, idx_ref), (acts_ref, acts_v.at[0]), (grads_ref, grads_v.at[0]),
            (aeig_hbm, aeig_ref),
            (geig_hbm.at[:, pl.ds(pl.multiple_of(y * 128, 128), 128)], geig_ref),
        ))
    ]
    own_basis = [
        pltpu.make_async_copy(
            b_ref.at[:, pl.ds(pl.multiple_of(y * 128, 128), 128)], bcol.at[x, zl, c], lsem.at[6]
        )
    ]
    for copy in own + own_basis:
        copy.start()

    own[0].wait()
    lane_block = lax.broadcasted_iota(jnp.int32, (32, 128), 1) // 32
    for m in range(4):
        u = a_ref[:, 256 * m:256 * m + 128].astype(F32)
        v = a_ref[:, 256 * m + 128:256 * m + 256].astype(F32)
        even = jnp.where(
            lane_block == 0, u,
            jnp.where(lane_block == 1, pltpu.roll(u, 96, 1),
                      jnp.where(lane_block == 2, pltpu.roll(v, 64, 1), pltpu.roll(v, 32, 1))),
        )
        odd = jnp.where(
            lane_block == 0, pltpu.roll(u, 96, 1),
            jnp.where(lane_block == 1, pltpu.roll(u, 64, 1),
                      jnp.where(lane_block == 2, pltpu.roll(v, 32, 1), v)),
        )
        cols = slice(128 * (m % 2), 128 * (m % 2) + 128)
        aperm[0, m // 2, :, cols] = even.astype(BF)
        aperm[1, m // 2, :, cols] = odd.astype(BF)
    my_rows = pl.ds(pl.multiple_of(c * 32, 32), 32)
    abuf[:, x, zl, my_rows, :] = aperm[c]
    pl.semaphore_wait(barrier, len(partners))

    mine = abuf.at[:, x, zl, my_rows, :]
    a_sib = send([(aperm.at[1 - c], mine, sibling)], mine)
    acts_sib = send([(acts_ref, acts_v.at[1], sibling)], acts_v.at[1])
    grads_sib = send([(grads_ref, grads_v.at[1], sibling)], grads_v.at[1])

    a_sib.wait_recv()
    az1 = gather(abuf.at[0, x, zl], all_zl, abuf.at[0, 0, pl.ds(0, 3)])
    ax1 = gather(abuf.at[1, x, zl], all_x, abuf.at[0, 0, pl.ds(0, 3)])

    for copy in own[1:]:
        copy.wait()
    row = lax.broadcasted_iota(jnp.int32, (16, TOK), 0)
    col = lax.broadcasted_iota(jnp.int32, (16, TOK), 1)
    wanted = jnp.where(row == 0, idx_ref[0, 0], jnp.where(row == 1, idx_ref[0, 1], -1))
    hot = jnp.where(col == wanted, 1.0, 0.0).astype(BF)
    for i, source in enumerate((acts_v, grads_v)):
        rows = dot(hot, source[0])
        for s in range(2):
            for k in range(8):
                picks[i, s * 8 + k:s * 8 + k + 1, :] = rows[s:s + 1, 128 * k:128 * k + 128]
    pbuf[c, x, zl] = picks[...].astype(BF)
    pz = gather(pbuf.at[c, x, zl], all_zl, pbuf.at[0, 0, pl.ds(0, 3)])
    for copy in own_basis:
        copy.wait()
    bz = gather(bcol.at[x, zl, c], all_zl, bcol.at[0, pl.ds(0, 3), 0])

    az1.wait_recv()
    mine = abuf.at[0, x]
    ax2 = [send([(mine, mine, to_x(s))], mine) for s in (1, 3)]
    ax1.wait_recv()
    mine = abuf.at[1, :, zl]
    az2 = [send([(mine, mine, to_z(s))], mine) for s in (1, 7)]
    pz.wait_recv()
    px = gather(pbuf.at[c, x], all_x, pbuf.at[0, pl.ds(0, 3)])
    bz.wait_recv()
    bx = gather(bcol.at[x, :, c], all_x, bcol.at[pl.ds(0, 3), :, 0])

    a3 = []
    for block, target, copy in (
        (abuf.at[0, x_down, pl.ds(0, 2)], to_x(1), ax2[0]),
        (abuf.at[0, x_up, pl.ds(2, 2)], to_x(3), ax2[1]),
        (abuf.at[1, pl.ds(0, 2), zl_down], to_z(1), az2[0]),
        (abuf.at[1, pl.ds(2, 2), zl_up], to_z(7), az2[1]),
    ):
        copy.wait_recv()
        a3.append(send([(block, block, target)], block))

    acts_sib.wait_recv()
    for copy in a3:
        copy.wait_recv()

    for slot in range(2):
        for t in range(2):
            tokens = acts_v[slot, 256 * t:256 * t + 256, :]
            for h in range(2):
                proj = dot(tokens, abuf[h].reshape(D, 256)).astype(BF)
                projt[256 * h:256 * h + 256, slot * TOK + 256 * t:slot * TOK + 256 * t + 256] = proj.T

    grads_sib.wait_recv()
    r1, r2 = {}, {}

    def forward(j):
        r1[j][0].wait_recv()
        sendx2[j, 0] = (tbuf[j, x_up, 0:64, :] + recvx1[j, 0, 0].astype(F32)).astype(BF)
        up = send([(sendx2.at[j, 0], recvx2.at[j, 0], to_x(1))], recvx2.at[j, 0])
        r1[j][1].wait_recv()
        sendx2[j, 1] = (tbuf[j, x_down, 64:128, :] + recvx1[j, 1, 0].astype(F32)).astype(BF)
        down = send([(sendx2.at[j, 1], recvx2.at[j, 1], to_x(3))], recvx2.at[j, 1])
        r2[j] = (up, down)

    for j in range(CHUNKS):
        cols = slice(CW * j, CW * j + CW)
        term = dot(projt[:, 0:TOK], grads_v[0, :, cols])
        term = term + dot(projt[:, TOK:], grads_v[1, :, cols])
        tbuf[j] = term.reshape(NX, 128, CW)
        sendx1[j, 0, 0] = tbuf[j, x_far, 0:64, :].astype(BF)
        sendx1[j, 0, 1] = tbuf[j, x_up, 64:128, :].astype(BF)
        sendx1[j, 1, 0] = tbuf[j, x_far, 64:128, :].astype(BF)
        sendx1[j, 1, 1] = tbuf[j, x_down, 0:64, :].astype(BF)
        r1[j] = [
            send([(sendx1.at[j, i], recvx1.at[j, i], to_x(s))], recvx1.at[j, i])
            for i, s in enumerate((1, 3))
        ]
        if j > 1:
            forward(j - 2)
    forward(CHUNKS - 2)
    forward(CHUNKS - 1)

    px.wait_recv()
    psib = gather(pbuf.at[c], [sibling], pbuf.at[c])
    bx.wait_recv()
    bsib = gather(bcol.at[:, :, c], [sibling], bcol.at[:, :, c])

    psib.wait_recv()
    for i in range(2):
        pwide[...] = pbuf[:, :, :, i].reshape(2 * NX * ZL * 16, 128).astype(F32)
        for k in range(8):
            part = jnp.concatenate(
                [pwide[pl.ds(s * 8 + k, 2 * NX * ZL, stride=16), :] for s in range(2)], axis=0
            )
            xbuf[k] = part.astype(BF)
        wide = jnp.concatenate([xbuf[k] for k in range(8)], axis=1)
        sfull[...] = dot(xbuf[dev // 4], wide, (((0,), (0,)), ((), ())))
        rows = sfull[pl.ds(pl.multiple_of((dev % 4) * 32, 32), 32), :]
        for k in range(8):
            ssend[k, i] = rows[:, 128 * k:128 * k + 128].astype(BF)
    sy = send([(ssend.at[(y + s) % NY], srecv.at[i], to_y(s)) for i, s in enumerate(DY)], srecv)

    rz, ry = {}, {}

    def sum_x(j):
        r2[j][0].wait_recv()
        r2[j][1].wait_recv()
        top = tbuf[j, x, 0:64, :] + recvx1[j, 1, 1].astype(F32) + recvx2[j, 0].astype(F32)
        low = tbuf[j, x, 64:128, :] + recvx1[j, 0, 1].astype(F32) + recvx2[j, 1].astype(F32)
        sendz[j, 0:4] = top.astype(BF).reshape(4, 16, CW)
        sendz[j, 4:8] = low.astype(BF).reshape(4, 16, CW)
        moves = []
        for i, s in enumerate(DZ):
            to = (z + s) % NZ
            moves.append((sendz.at[j, (to % ZL) * 2 + to // ZL], recvz.at[j, i], to_z(s)))
        rz[j] = send(moves, recvz.at[j])

    def sum_z(j):
        rz[j].wait_recv()
        total = sendz[j, slot_z].astype(F32)
        for i in range(len(DZ)):
            total = total + recvz[j, i].astype(F32)
        sendy[j] = total.astype(BF)
        ry[j] = send(
            [(sendy.at[j], recvy.at[j, i], to_y(s)) for i, s in enumerate(DY)], recvy.at[j]
        )

    sum_x(0)
    for j in range(1, CHUNKS):
        sum_x(j)
        sum_z(j - 1)
    sum_z(CHUNKS - 1)

    sy.wait_recv()
    stat = ssend[y].astype(F32)
    for i in range(len(DY)):
        stat = stat + srecv[i].astype(F32)
    szsend[...] = stat
    sz = send([(szsend, szrecv, to_z(4))], szrecv)
    sz.wait_recv()
    sout[y] = (szsend[...] + szrecv[...]).astype(BF)
    so = gather(sout.at[y], all_y, sout.at[pl.ds(0, 7)])

    lane = lax.broadcasted_iota(jnp.int32, (16, 32), 1)
    sub = lax.broadcasted_iota(jnp.int32, (16, 32), 0)
    eigs = jnp.sum(
        jnp.where(lane == sub + 16 * zh, aeig_ref[...], 0.0), axis=1, keepdims=True
    )
    divisor = eigs * geig_ref[...] + 0.1
    bsib.wait_recv()
    basis = bcol[...].reshape(D, 128)
    parts = []
    for j in range(CHUNKS):
        ry[j].wait_recv()
        total = sendy[j].astype(F32)
        for i in range(len(DY)):
            total = total + recvy[j, i].astype(F32)
        parts.append(total.astype(BF))
    turned = dot(jnp.concatenate(parts, axis=1), basis)
    scaled = (turned / divisor).astype(BF)
    partial = dot(scaled, basis, (((1,), (1,)), ((), ())))
    for k in range(8):
        tsend[k] = partial[:, 128 * k:128 * k + 128]
    ty = send([(tsend.at[(y + s) % NY], trecv.at[i], to_y(s)) for i, s in enumerate(DY)], trecv)
    ty.wait_recv()
    restored = tsend[y]
    for i in range(len(DY)):
        restored = restored + trecv[i]
    rbuf[c * NX + x, slot_z] = restored.astype(BF)
    mine = rbuf.at[c * NX + x]
    rzg = gather(mine.at[slot_z], all_z, rbuf.at[0, pl.ds(0, 7)])
    rzg.wait_recv()
    rxc = gather(mine, all_xc, rbuf.at[pl.ds(0, 7)])

    so.wait_recv()
    for i in range(2):
        for k in range(8):
            out_ref[1 + i, :, 128 * k:128 * k + 128] = sout[k, i]
    rxc.wait_recv()
    total = jnp.zeros((32, 128), F32)
    for half in range(2):
        for h in range(2):
            total = total + dot(aperm[half, h], rbuf[half * NX + 2 * h:half * NX + 2 * h + 2].reshape(256, 128))
    obuf[y] = total.astype(BF)
    po = gather(obuf.at[y], all_y, obuf.at[pl.ds(0, 7)])

    drain()

    po.wait_recv()
    for k in range(8):
        out_ref[0, :, 128 * k:128 * k + 128] = obuf[k]


def finish(result_ref, old_act_ref, old_grad_ref, pre_ref, act_ref, grad_ref, *, act_scale, grad_scale):
    pre_ref[...] = result_ref[0].astype(F32)
    act_ref[...] = 0.75 * old_act_ref[...] + act_scale * result_ref[1].astype(F32)
    grad_ref[...] = 0.75 * old_grad_ref[...] + grad_scale * result_ref[2].astype(F32)


def local(
    acts,
    out_grads,
    old_act_factor,
    old_grad_factor,
    act_basis,
    grad_basis,
    act_eigs,
    grad_eigs,
    sample_index,
):
    vmem = pl.BlockSpec(memory_space=pltpu.VMEM)
    hbm = pl.BlockSpec(memory_space=pl.ANY)
    copies = 64
    result = pl.pallas_call(
        kernel,
        out_shape=jax.ShapeDtypeStruct((3, 32, D), BF),
        in_specs=[hbm] * 7,
        out_specs=vmem,
        scratch_shapes=[
            pltpu.SMEM((1, 2), jnp.int32),
            pltpu.VMEM((32, D), BF),
            pltpu.VMEM((1, 32), F32),
            pltpu.VMEM((1, 128), F32),
            pltpu.VMEM((2, TOK, D), BF),
            pltpu.VMEM((2, TOK, D), BF),
            pltpu.VMEM((2, 2, 32, 256), BF),
            pltpu.VMEM((2, NX, ZL, 64, 256), BF),
            pltpu.VMEM((HALF, 2 * TOK), BF),
            pltpu.VMEM((CHUNKS, NX, 128, CW), F32),
            pltpu.VMEM((CHUNKS, 2, 2, 64, CW), BF),
            pltpu.VMEM((CHUNKS, 2, 2, 64, CW), BF),
            pltpu.VMEM((CHUNKS, 2, 64, CW), BF),
            pltpu.VMEM((CHUNKS, 2, 64, CW), BF),
            pltpu.VMEM((CHUNKS, NZ, 16, CW), BF),
            pltpu.VMEM((CHUNKS, 7, 16, CW), BF),
            pltpu.VMEM((CHUNKS, 16, CW), BF),
            pltpu.VMEM((CHUNKS, 7, 16, CW), BF),
            pltpu.VMEM((NX, ZL, 2, 32, 128), BF),
            pltpu.VMEM((NY, 16, 128), F32),
            pltpu.VMEM((7, 16, 128), F32),
            pltpu.VMEM((2 * NX, NZ, 16, 128), BF),
            pltpu.VMEM((NY, 32, 128), BF),
            pltpu.VMEM((2, 16, 128), F32),
            pltpu.VMEM((2, NX, ZL, 2, 16, 128), BF),
            pltpu.VMEM((2 * NX * ZL * 16, 128), F32),
            pltpu.VMEM((8, 64, 128), BF),
            pltpu.VMEM((128, D), F32),
            pltpu.VMEM((NY, 2, 32, 128), BF),
            pltpu.VMEM((7, 2, 32, 128), BF),
            pltpu.VMEM((2, 32, 128), F32),
            pltpu.VMEM((2, 32, 128), F32),
            pltpu.VMEM((NY, 2, 32, 128), BF),
            pltpu.SemaphoreType.DMA((7,)),
            pltpu.SemaphoreType.DMA((copies,)),
            pltpu.SemaphoreType.DMA((copies,)),
        ],
        compiler_params=pltpu.CompilerParams(
            collective_id=0, has_side_effects=True, vmem_limit_bytes=63 * 1024 * 1024
        ),
        cost_estimate=pl.CostEstimate(
            flops=4 * TOK * D * D, bytes_accessed=4 * TOK * D, transcendentals=0
        ),
    )(
        sample_index.reshape(1, 2), acts, out_grads, act_basis, grad_basis,
        act_eigs.reshape(1, 32), grad_eigs.reshape(1, D),
    )
    device_count = lax.axis_size("grp") * lax.axis_size("dev")
    total_samples = device_count * sample_index.shape[0]
    total_tokens = device_count * acts.shape[0]
    return pl.pallas_call(
        functools.partial(
            finish,
            act_scale=0.25 / total_samples,
            grad_scale=0.25 * total_tokens / total_samples,
        ),
        out_shape=(jax.ShapeDtypeStruct((32, D), F32),) * 3,
        in_specs=[vmem] * 3,
        out_specs=(vmem,) * 3,
    )(result, old_act_factor, old_grad_factor)


def solution(mesh):
    return jax.shard_map(
        local,
        mesh=mesh,
        in_specs=(
            P(("grp", "dev"), None),
            P(("grp", "dev"), None),
            P("dev", None),
            P("dev", None),
            P("dev", None),
            P("dev", None),
            P("dev"),
            P(),
            P(("grp", "dev")),
        ),
        out_specs=(P("dev", None), P("dev", None), P("dev", None)),
        check_vma=False,
    )
```

```python
import functools

import jax
import jax.numpy as jnp
from jax import lax
from jax.experimental import pallas as pl
from jax.experimental.pallas import tpu as pltpu
from jax.sharding import PartitionSpec as P

NX, NY, NZ, ZL = 4, 8, 8, 4
D, TOK = 1024, 512
HALF = D // 2
CHUNKS, CW = 4, 256
BF, F32 = jnp.bfloat16, jnp.float32
DX = (2, 1, 3)
DY = (4, 3, 5, 2, 6, 1, 7)
DZ = (4, 3, 5, 2, 6, 1, 7)
DZL = (2, 1, 7)
DXC = tuple((dx, dc) for dx in (2, 1, 3, 0) for dc in (1, 0) if (dx, dc) != (0, 0))
NT = (((1,), (1,)), ((), ()))


def dot(left, right, dims=(((1,), (0,)), ((), ()))):
    return lax.dot_general(left, right, dims, preferred_element_type=F32)


def column(row):
    sub = lax.broadcasted_iota(jnp.int32, (128, 128), 0)
    lane = lax.broadcasted_iota(jnp.int32, (128, 128), 1)
    return jnp.sum(jnp.where(sub == lane, row, 0.0), axis=1, keepdims=True)


def kernel(
    idx_hbm, acts_hbm, grads_hbm, a_hbm, b_hbm, aeig_hbm, geig_hbm,
    out_ref,
    idx_ref, a_ref, aeig_ref, geig_ref,
    acts_v, acts_sv, grads_v, actst, abuf, bbuf,
    tbuf, sendx1, recvx1, sendx2, recvx2, sendz, recvz, sendy, recvy,
    gbuf, recip, qbuf,
    shifted, picks, pbuf, pwide, xbuf, sfull, ssend, srecv, szsend, szrecv, sout,
    lsem, ssem, rsem,
):
    grp, dev = lax.axis_index("grp"), lax.axis_index("dev")
    y, zh = grp // 2, grp % 2
    x, zl, c = dev // 8, (dev // 2) % 4, dev % 2
    z = zh * ZL + zl

    def at(px, py, pz, pc):
        return {"grp": py * 2 + pz // ZL, "dev": px * 8 + (pz % ZL) * 2 + pc}

    def to_x(step):
        return at((x + step) % NX, y, z, c)

    def to_y(step):
        return at(x, (y + step) % NY, z, c)

    def to_z(step):
        return at(x, y, (z + step) % NZ, c)

    def to_xc(step):
        return at((x + step[0]) % NX, y, z, (c + step[1]) % 2)

    sibling = at(x, y, z, 1 - c)

    counter = [0]
    pending = []

    def send(moves, like):
        n = counter[0]
        counter[0] += 1

        def copy(src, dst, target):
            return pltpu.make_async_remote_copy(
                src_ref=src, dst_ref=dst, send_sem=ssem.at[n], recv_sem=rsem.at[n],
                device_id=target, device_id_type=pl.DeviceIdType.MESH,
            )

        for move in moves:
            copy(*move).start()
        whole = copy(like, like, sibling)
        pending.append(whole)
        return whole

    def gather(ref, targets, like):
        return send([(ref, ref, target) for target in targets], like)

    def drain():
        for copy in pending:
            copy.wait_send()
        pending.clear()

    all_x = [to_x(s) for s in DX]
    all_y = [to_y(s) for s in DY]
    all_z = [to_z(s) for s in DZ]
    all_zl = [to_z(s) for s in DZL]
    all_xc = [to_xc(s) for s in DXC]
    x_up, x_down, x_far = (x + 1) % NX, (x + 3) % NX, (x + 2) % NX

    barrier = pltpu.get_barrier_semaphore()
    partners = all_xc + all_y + all_z
    for partner in partners:
        pl.semaphore_signal(
            barrier, inc=1, device_id=partner, device_id_type=pl.DeviceIdType.MESH
        )

    my_rows = pl.ds(pl.multiple_of(c * 32, 32), 32)
    my_cols = pl.ds(pl.multiple_of(y * 128, 128), 128)

    def half(ref, side):
        return ref.at[:, pl.ds(pl.multiple_of(side * HALF, HALF), HALF)]

    def quarter(ref, side, h):
        return ref.at[:, pl.ds(pl.multiple_of(side * HALF + h * 256, 256), 256)]

    moves = [
        (acts_hbm, acts_v), (grads_hbm, grads_v.at[0]), (idx_hbm, idx_ref),
        (aeig_hbm, aeig_ref), (geig_hbm.at[:, my_cols], geig_ref), (a_hbm, a_ref),
        (b_hbm.at[pl.ds(0, 16), my_cols], pbuf.at[x, zl, c, 3]),
        (b_hbm.at[pl.ds(16, 16), my_cols], pbuf.at[x, zl, c, 4]),
    ]
    for source, whole in ((a_hbm, abuf), (b_hbm, bbuf)):
        for h in range(2):
            moves.append((quarter(source, c, h), whole.at[2 * c + h, x, zl, my_rows]))
    own = [pltpu.make_async_copy(src, dst, lsem.at[i]) for i, (src, dst) in enumerate(moves)]
    for copy in own:
        copy.start()

    own[0].wait()
    mine = acts_v[:, pl.ds(pl.multiple_of(c * HALF, HALF), HALF)]
    for k in range(2):
        for t in range(2):
            actst[256 * k:256 * k + 256, 256 * t:256 * t + 256] = (
                mine[256 * t:256 * t + 256, 256 * k:256 * k + 256].T
            )

    pl.semaphore_wait(barrier, len(partners))

    acts_sib = send([(half(acts_hbm, 1 - c), acts_sv, sibling)], acts_sv)
    grads_sib = send([(grads_hbm, grads_v.at[1], sibling)], grads_v.at[1])
    basis_sib = []
    for source, whole in ((a_hbm, abuf), (b_hbm, bbuf)):
        basis_sib.append(send(
            [
                (quarter(source, 1 - c, h), whole.at[2 * (1 - c) + h, x, zl, my_rows], sibling)
                for h in range(2)
            ],
            whole.at[pl.ds(0, 2), 0, 0, pl.ds(0, 32)],
        ))

    def term(slot, j):
        part = dot(
            actst[:, slot * TOK:slot * TOK + TOK], grads_v[slot, :, CW * j:CW * j + CW]
        )
        return part.reshape(NX, 128, CW)

    for copy in own[1:]:
        copy.wait()
    for j in range(CHUNKS):
        tbuf[j] = term(0, j)

    row = lax.broadcasted_iota(jnp.int32, (16, TOK), 0)
    col = lax.broadcasted_iota(jnp.int32, (16, TOK), 1)
    wanted = jnp.where(row == 0, idx_ref[0, 0], jnp.where(row == 1, idx_ref[0, 1], -1))
    hot = jnp.where(col == wanted, 1.0, 0.0).astype(BF)
    for i, source in enumerate((acts_v[...], grads_v[0])):
        rows = dot(hot, source)
        for s in range(2):
            for k in range(8):
                picks[i, s * 8 + k:s * 8 + k + 1, :] = rows[s:s + 1, 128 * k:128 * k + 128]
    shifted[...] = jnp.zeros((8, 128), F32)
    shifted[0:1, 0:32] = aeig_ref[...]
    eigs = pltpu.roll(shifted[...], (dev % 4) * 32, 1)[0:1, :]
    high = eigs.astype(BF).astype(F32)
    middle = (eigs - high).astype(BF).astype(F32)
    picks[2] = jnp.zeros((16, 128), F32)
    picks[2, 0:1, :] = high
    picks[2, 1:2, :] = middle
    picks[2, 2:3, :] = eigs - high - middle
    pbuf[x, zl, c, 0:3] = picks[...].astype(BF)
    pz = gather(pbuf.at[x, zl, c], all_zl, pbuf.at[0, pl.ds(0, 3), 0])

    def first(whole):
        return (
            gather(whole.at[2 * c, x, zl], all_zl, whole.at[0, 0, pl.ds(0, 3)]),
            gather(whole.at[2 * c + 1, x, zl], all_x, whole.at[0, 0, pl.ds(0, 3)]),
        )

    def second(whole, stage):
        stage[0].wait_recv()
        over_x = gather(whole.at[2 * c, x], all_x, whole.at[0, pl.ds(0, 3)])
        stage[1].wait_recv()
        over_z = gather(whole.at[2 * c + 1, :, zl], all_zl, whole.at[0, pl.ds(0, 3)])
        return over_x, over_z

    def third(whole, stage):
        for copy in stage:
            copy.wait_recv()
        mine = whole.at[pl.ds(2 * c, 2)]
        return gather(mine, [sibling], mine)

    basis_sib[0].wait_recv()
    a_first = first(abuf)
    basis_sib[1].wait_recv()
    b_first = first(bbuf)

    acts_sib.wait_recv()
    for k in range(2):
        for t in range(2):
            actst[256 * k:256 * k + 256, TOK + 256 * t:TOK + 256 * t + 256] = (
                acts_sv[256 * t:256 * t + 256, 256 * k:256 * k + 256].T
            )
    grads_sib.wait_recv()
    r1, r2 = {}, {}

    def forward(j):
        r1[j][0].wait_recv()
        sendx2[j, 0] = (tbuf[j, x_up, 0:64, :] + recvx1[j, 0, 0].astype(F32)).astype(BF)
        up = send([(sendx2.at[j, 0], recvx2.at[j, 0], to_x(1))], recvx2.at[j, 0])
        r1[j][1].wait_recv()
        sendx2[j, 1] = (tbuf[j, x_down, 64:128, :] + recvx1[j, 1, 0].astype(F32)).astype(BF)
        down = send([(sendx2.at[j, 1], recvx2.at[j, 1], to_x(3))], recvx2.at[j, 1])
        r2[j] = (up, down)

    for j in range(CHUNKS):
        tbuf[j] = tbuf[j] + term(1, j)
        sendx1[j, 0, 0] = tbuf[j, x_far, 0:64, :].astype(BF)
        sendx1[j, 0, 1] = tbuf[j, x_up, 64:128, :].astype(BF)
        sendx1[j, 1, 0] = tbuf[j, x_far, 64:128, :].astype(BF)
        sendx1[j, 1, 1] = tbuf[j, x_down, 0:64, :].astype(BF)
        r1[j] = [
            send([(sendx1.at[j, i], recvx1.at[j, i], to_x(s))], recvx1.at[j, i])
            for i, s in enumerate((1, 3))
        ]
        if j > 1:
            forward(j - 2)
    pz.wait_recv()
    px = gather(pbuf.at[x, :, c], all_x, pbuf.at[pl.ds(0, 3), :, 0])
    forward(CHUNKS - 2)
    forward(CHUNKS - 1)
    a_second = second(abuf, a_first)

    rz, ry = {}, {}

    def sum_x(j):
        r2[j][0].wait_recv()
        r2[j][1].wait_recv()
        top = tbuf[j, x, 0:64, :] + recvx1[j, 1, 1].astype(F32) + recvx2[j, 0].astype(F32)
        low = tbuf[j, x, 64:128, :] + recvx1[j, 0, 1].astype(F32) + recvx2[j, 1].astype(F32)
        sendz[j, 0:4] = top.astype(BF).reshape(4, 16, CW)
        sendz[j, 4:8] = low.astype(BF).reshape(4, 16, CW)
        rz[j] = send(
            [(sendz.at[j, (z + s) % NZ], recvz.at[j, i], to_z(s)) for i, s in enumerate(DZ)],
            recvz.at[j],
        )

    def sum_z(j):
        rz[j].wait_recv()
        total = sendz[j, z].astype(F32)
        for i in range(len(DZ)):
            total = total + recvz[j, i].astype(F32)
        sendy[j] = total.astype(BF)
        ry[j] = send(
            [(sendy.at[j], recvy.at[j, i], to_y(s)) for i, s in enumerate(DY)], recvy.at[j]
        )

    sum_x(0)
    for j in range(1, CHUNKS):
        sum_x(j)
        sum_z(j - 1)
    px.wait_recv()
    psib = gather(pbuf.at[:, :, c], [sibling], pbuf.at[:, :, c])
    sum_z(CHUNKS - 1)
    b_second = second(bbuf, b_first)

    psib.wait_recv()
    for i in range(2):
        pwide[...] = pbuf[:, :, :, i].reshape(2 * NX * ZL * 16, 128).astype(F32)
        for k in range(8):
            part = jnp.concatenate(
                [pwide[pl.ds(s * 8 + k, 2 * NX * ZL, stride=16), :] for s in range(2)], axis=0
            )
            xbuf[k] = part.astype(BF)
        wide = jnp.concatenate([xbuf[k] for k in range(8)], axis=1)
        sfull[...] = dot(xbuf[dev // 4], wide, (((0,), (0,)), ((), ())))
        rows = sfull[pl.ds(pl.multiple_of((dev % 4) * 32, 32), 32), :]
        for k in range(8):
            ssend[k, i] = rows[:, 128 * k:128 * k + 128].astype(BF)
    sy = send([(ssend.at[(y + s) % NY], srecv.at[i], to_y(s)) for i, s in enumerate(DY)], srecv)

    high_parts, low_parts = [], []
    for j in range(CHUNKS):
        ry[j].wait_recv()
        total = sendy[j].astype(F32)
        for i in range(len(DY)):
            total = total + recvy[j, i].astype(F32)
        high_parts.append(total.astype(BF))
        low_parts.append((total - total.astype(BF).astype(F32)).astype(BF))
    columns = pbuf[:, :, :, 3:5].reshape(D, 128)
    product = dot(
        jnp.concatenate(
            [jnp.concatenate(high_parts, axis=1), jnp.concatenate(low_parts, axis=1)], axis=0
        ),
        columns,
    )
    gbuf[c * NX + x, z] = (product[0:16] + product[16:32]).astype(BF)
    mine = gbuf.at[c * NX + x]
    gz = gather(mine.at[z], all_z, gbuf.at[0, pl.ds(0, 7)])

    geig = column(geig_ref[...])
    for m in range(8):
        block = pbuf[m // 2, 2 * (m % 2):2 * (m % 2) + 2, :, 2].astype(F32)
        block = block[0, 0] + block[0, 1] + block[1, 0] + block[1, 1]
        eig_row = block[0:1] + block[1:2] + block[2:3]
        recip[:, 128 * m:128 * m + 128] = 1.0 / (geig * eig_row + 0.1)

    gz.wait_recv()
    gxc = gather(mine, all_xc, gbuf.at[pl.ds(0, 7)])
    a_third = third(abuf, a_second)

    sy.wait_recv()
    stat = ssend[y].astype(F32)
    for i in range(len(DY)):
        stat = stat + srecv[i].astype(F32)
    szsend[...] = stat
    sz = send([(szsend, szrecv, to_z(4))], szrecv)

    gxc.wait_recv()
    turned = gbuf[...].reshape(D, 128).T
    a_third.wait_recv()
    total = jnp.zeros((32, 128), F32)
    for q in range(4):
        cols = slice(256 * q, 256 * q + 256)
        scaled = (dot(turned, abuf[q].reshape(D, 256)) * recip[:, cols]).astype(BF)
        total = total + dot(a_ref[:, cols], scaled, NT)
    qbuf[y] = total.astype(BF)
    qy = gather(qbuf.at[y], all_y, qbuf.at[pl.ds(0, 7)])
    b_third = third(bbuf, b_second)

    sz.wait_recv()
    sout[y] = (szsend[...] + szrecv[...]).astype(BF)
    so = gather(sout.at[y], all_y, sout.at[pl.ds(0, 7)])
    drain()

    qy.wait_recv()
    left = jnp.concatenate([qbuf[k] for k in range(8)], axis=1)
    b_third.wait_recv()
    total = dot(left[:, 0:256], bbuf[0].reshape(D, 256), NT)
    for q in range(1, 4):
        total = total + dot(left[:, 256 * q:256 * q + 256], bbuf[q].reshape(D, 256), NT)
    out_ref[0] = total
    so.wait_recv()
    for i in range(2):
        for k in range(8):
            out_ref[1 + i, :, 128 * k:128 * k + 128] = sout[k, i].astype(F32)


def finish(result_ref, old_act_ref, old_grad_ref, pre_ref, act_ref, grad_ref, *, act_scale, grad_scale):
    pre_ref[...] = result_ref[0]
    act_ref[...] = 0.75 * old_act_ref[...] + act_scale * result_ref[1]
    grad_ref[...] = 0.75 * old_grad_ref[...] + grad_scale * result_ref[2]


def local(
    acts,
    out_grads,
    old_act_factor,
    old_grad_factor,
    act_basis,
    grad_basis,
    act_eigs,
    grad_eigs,
    sample_index,
):
    vmem = pl.BlockSpec(memory_space=pltpu.VMEM)
    hbm = pl.BlockSpec(memory_space=pl.ANY)
    copies = 72
    result = pl.pallas_call(
        kernel,
        out_shape=jax.ShapeDtypeStruct((3, 32, D), F32),
        in_specs=[hbm] * 7,
        out_specs=vmem,
        scratch_shapes=[
            pltpu.SMEM((1, 2), jnp.int32),
            pltpu.VMEM((32, D), BF),
            pltpu.VMEM((1, 32), F32),
            pltpu.VMEM((1, 128), F32),
            pltpu.VMEM((TOK, D), BF),
            pltpu.VMEM((TOK, HALF), BF),
            pltpu.VMEM((2, TOK, D), BF),
            pltpu.VMEM((HALF, 2 * TOK), BF),
            pltpu.VMEM((4, NX, ZL, 64, 256), BF),
            pltpu.VMEM((4, NX, ZL, 64, 256), BF),
            pltpu.VMEM((CHUNKS, NX, 128, CW), F32),
            pltpu.VMEM((CHUNKS, 2, 2, 64, CW), BF),
            pltpu.VMEM((CHUNKS, 2, 2, 64, CW), BF),
            pltpu.VMEM((CHUNKS, 2, 64, CW), BF),
            pltpu.VMEM((CHUNKS, 2, 64, CW), BF),
            pltpu.VMEM((CHUNKS, NZ, 16, CW), BF),
            pltpu.VMEM((CHUNKS, 7, 16, CW), BF),
            pltpu.VMEM((CHUNKS, 16, CW), BF),
            pltpu.VMEM((CHUNKS, 7, 16, CW), BF),
            pltpu.VMEM((2 * NX, NZ, 16, 128), BF),
            pltpu.VMEM((128, D), F32),
            pltpu.VMEM((NY, 32, 128), BF),
            pltpu.VMEM((8, 128), F32),
            pltpu.VMEM((3, 16, 128), F32),
            pltpu.VMEM((NX, ZL, 2, 5, 16, 128), BF),
            pltpu.VMEM((2 * NX * ZL * 16, 128), F32),
            pltpu.VMEM((8, 64, 128), BF),
            pltpu.VMEM((128, D), F32),
            pltpu.VMEM((NY, 2, 32, 128), BF),
            pltpu.VMEM((7, 2, 32, 128), BF),
            pltpu.VMEM((2, 32, 128), F32),
            pltpu.VMEM((2, 32, 128), F32),
            pltpu.VMEM((NY, 2, 32, 128), BF),
            pltpu.SemaphoreType.DMA((12,)),
            pltpu.SemaphoreType.DMA((copies,)),
            pltpu.SemaphoreType.DMA((copies,)),
        ],
        compiler_params=pltpu.CompilerParams(
            collective_id=0, has_side_effects=True, vmem_limit_bytes=63 * 1024 * 1024
        ),
        cost_estimate=pl.CostEstimate(
            flops=4 * TOK * D * D, bytes_accessed=4 * TOK * D, transcendentals=0
        ),
    )(
        sample_index.reshape(1, 2), acts, out_grads, act_basis, grad_basis,
        act_eigs.reshape(1, 32), grad_eigs.reshape(1, D),
    )
    device_count = lax.axis_size("grp") * lax.axis_size("dev")
    total_samples = device_count * sample_index.shape[0]
    total_tokens = device_count * acts.shape[0]
    return pl.pallas_call(
        functools.partial(
            finish,
            act_scale=0.25 / total_samples,
            grad_scale=0.25 * total_tokens / total_samples,
        ),
        out_shape=(jax.ShapeDtypeStruct((32, D), F32),) * 3,
        in_specs=[vmem] * 3,
        out_specs=(vmem,) * 3,
    )(result, old_act_factor, old_grad_factor)


def solution(mesh):
    return jax.shard_map(
        local,
        mesh=mesh,
        in_specs=(
            P(("grp", "dev"), None),
            P(("grp", "dev"), None),
            P("dev", None),
            P("dev", None),
            P("dev", None),
            P("dev", None),
            P("dev"),
            P(),
            P(("grp", "dev")),
        ),
        out_specs=(P("dev", None), P("dev", None), P("dev", None)),
        check_vma=False,
    )
```

```python
import functools

import jax
import jax.numpy as jnp
from jax import lax
from jax.experimental import pallas as pl
from jax.experimental.pallas import tpu as pltpu
from jax.sharding import PartitionSpec as P

NX, NY, NZ, ZL = 4, 8, 8, 4
D, TOK = 1024, 512
HALF = D // 2
CHUNKS, CW = 4, 256
BF, F32 = jnp.bfloat16, jnp.float32
DX = (2, 1, 3)
DY = (4, 3, 5, 2, 6, 1, 7)
DZ = (4, 3, 5, 2, 6, 1, 7)
DZL = (2, 1, 7)
DXC = tuple((dx, dc) for dx in (2, 1, 3, 0) for dc in (1, 0) if (dx, dc) != (0, 0))
NT = (((1,), (1,)), ((), ()))


def dot(left, right, dims=(((1,), (0,)), ((), ()))):
    return lax.dot_general(left, right, dims, preferred_element_type=F32)


def column(row):
    sub = lax.broadcasted_iota(jnp.int32, (128, 128), 0)
    lane = lax.broadcasted_iota(jnp.int32, (128, 128), 1)
    return jnp.sum(jnp.where(sub == lane, row, 0.0), axis=1, keepdims=True)


def kernel(
    idx_hbm, acts_hbm, grads_hbm, a_hbm, b_hbm, aeig_hbm, geig_hbm,
    out_ref,
    idx_ref, a_ref, aeig_ref, geig_ref,
    acts_v, acts_sv, grads_v, actst, abuf, bbuf,
    tbuf, sendx1, recvx1, sendx2, recvx2, sendz, recvz, sendy, recvy,
    gbuf, recip, qbuf,
    shifted, parts, ebuf, picks, pbuf, pwide, xbuf, sfull, ssend, srecv, szsend, szrecv, sout,
    lsem, ssem, rsem,
):
    grp, dev = lax.axis_index("grp"), lax.axis_index("dev")
    y, zh = grp // 2, grp % 2
    x, zl, c = dev // 8, (dev // 2) % 4, dev % 2
    z = zh * ZL + zl

    def at(px, py, pz, pc):
        return {"grp": py * 2 + pz // ZL, "dev": px * 8 + (pz % ZL) * 2 + pc}

    def to_x(step):
        return at((x + step) % NX, y, z, c)

    def to_y(step):
        return at(x, (y + step) % NY, z, c)

    def to_z(step):
        return at(x, y, (z + step) % NZ, c)

    def to_xc(step):
        return at((x + step[0]) % NX, y, z, (c + step[1]) % 2)

    sibling = at(x, y, z, 1 - c)

    counter = [0]
    pending = []

    def send(moves, like):
        n = counter[0]
        counter[0] += 1

        def copy(src, dst, target):
            return pltpu.make_async_remote_copy(
                src_ref=src, dst_ref=dst, send_sem=ssem.at[n], recv_sem=rsem.at[n],
                device_id=target, device_id_type=pl.DeviceIdType.MESH,
            )

        for move in moves:
            copy(*move).start()
        whole = copy(like, like, sibling)
        pending.append(whole)
        return whole

    def gather(ref, targets, like):
        return send([(ref, ref, target) for target in targets], like)

    def drain():
        for copy in pending:
            copy.wait_send()
        pending.clear()

    all_x = [to_x(s) for s in DX]
    all_y = [to_y(s) for s in DY]
    all_z = [to_z(s) for s in DZ]
    all_zl = [to_z(s) for s in DZL]
    all_xc = [to_xc(s) for s in DXC]
    x_up, x_down, x_far = (x + 1) % NX, (x + 3) % NX, (x + 2) % NX

    barrier = pltpu.get_barrier_semaphore()
    partners = all_xc + all_y + all_z
    for partner in partners:
        pl.semaphore_signal(
            barrier, inc=1, device_id=partner, device_id_type=pl.DeviceIdType.MESH
        )

    my_rows = pl.ds(pl.multiple_of(c * 32, 32), 32)
    my_cols = pl.ds(pl.multiple_of(y * 128, 128), 128)

    def half(ref, side):
        return ref.at[:, pl.ds(pl.multiple_of(side * HALF, HALF), HALF)]

    def quarter(ref, side, h):
        return ref.at[:, pl.ds(pl.multiple_of(side * HALF + h * 256, 256), 256)]

    moves = [
        (aeig_hbm, aeig_ref),
        (b_hbm.at[pl.ds(0, 16), my_cols], ebuf.at[x, zl, c, 1]),
        (b_hbm.at[pl.ds(16, 16), my_cols], ebuf.at[x, zl, c, 2]),
        (acts_hbm, acts_v), (grads_hbm, grads_v.at[0]), (idx_hbm, idx_ref),
        (geig_hbm.at[:, my_cols], geig_ref), (a_hbm, a_ref),
    ]
    for source, whole in ((a_hbm, abuf), (b_hbm, bbuf)):
        for h in range(2):
            moves.append((quarter(source, c, h), whole.at[2 * c + h, x, zl, my_rows]))
    own = [pltpu.make_async_copy(src, dst, lsem.at[i]) for i, (src, dst) in enumerate(moves)]
    for copy in own:
        copy.start()

    own[0].wait()
    shifted[...] = jnp.zeros((8, 128), F32)
    shifted[0:1, 0:32] = aeig_ref[...]
    eigs = pltpu.roll(shifted[...], (dev % 4) * 32, 1)[0:1, :]
    high = eigs.astype(BF).astype(F32)
    middle = (eigs - high).astype(BF).astype(F32)
    parts[...] = jnp.zeros((16, 128), F32)
    parts[0:1, :] = high
    parts[1:2, :] = middle
    parts[2:3, :] = eigs - high - middle
    ebuf[x, zl, c, 0] = parts[...].astype(BF)
    for copy in own[1:3]:
        copy.wait()

    pl.semaphore_wait(barrier, len(partners))

    basis_sib = []
    for source, whole in ((a_hbm, abuf), (b_hbm, bbuf)):
        basis_sib.append(send(
            [
                (quarter(source, 1 - c, h), whole.at[2 * (1 - c) + h, x, zl, my_rows], sibling)
                for h in range(2)
            ],
            whole.at[pl.ds(0, 2), 0, 0, pl.ds(0, 32)],
        ))

    acts_sib = send([(half(acts_hbm, 1 - c), acts_sv, sibling)], acts_sv)
    grads_sib = send([(grads_hbm, grads_v.at[1], sibling)], grads_v.at[1])
    ez = gather(ebuf.at[x, zl, c], all_zl, ebuf.at[0, pl.ds(0, 3), 0])

    own[3].wait()
    mine = acts_v[:, pl.ds(pl.multiple_of(c * HALF, HALF), HALF)]
    for k in range(2):
        for t in range(2):
            actst[256 * k:256 * k + 256, 256 * t:256 * t + 256] = (
                mine[256 * t:256 * t + 256, 256 * k:256 * k + 256].T
            )

    def term(slot, j):
        part = dot(
            actst[:, slot * TOK:slot * TOK + TOK], grads_v[slot, :, CW * j:CW * j + CW]
        )
        return part.reshape(NX, 128, CW)

    for copy in own[4:]:
        copy.wait()
    for j in range(CHUNKS):
        tbuf[j] = term(0, j)

    def first(whole):
        return (
            gather(whole.at[2 * c, x, zl], all_zl, whole.at[0, 0, pl.ds(0, 3)]),
            gather(whole.at[2 * c + 1, x, zl], all_x, whole.at[0, 0, pl.ds(0, 3)]),
        )

    def second_x(whole, stage):
        stage[0].wait_recv()
        return gather(whole.at[2 * c, x], all_x, whole.at[0, pl.ds(0, 3)])

    def second_z(whole, stage):
        stage[1].wait_recv()
        return gather(whole.at[2 * c + 1, :, zl], all_zl, whole.at[0, pl.ds(0, 3)])

    def third(whole, stage):
        for copy in stage:
            copy.wait_recv()
        mine = whole.at[pl.ds(2 * c, 2)]
        return gather(mine, [sibling], mine)

    basis_sib[0].wait_recv()
    a_first = first(abuf)
    basis_sib[1].wait_recv()
    b_first = first(bbuf)
    ez.wait_recv()
    ex = gather(ebuf.at[x, :, c], all_x, ebuf.at[pl.ds(0, 3), :, 0])

    acts_sib.wait_recv()
    for k in range(2):
        for t in range(2):
            actst[256 * k:256 * k + 256, TOK + 256 * t:TOK + 256 * t + 256] = (
                acts_sv[256 * t:256 * t + 256, 256 * k:256 * k + 256].T
            )
    grads_sib.wait_recv()
    r1, r2 = {}, {}

    def forward(j):
        r1[j][0].wait_recv()
        sendx2[j, 0] = (tbuf[j, x_up, 0:64, :] + recvx1[j, 0, 0].astype(F32)).astype(BF)
        up = send([(sendx2.at[j, 0], recvx2.at[j, 0], to_x(1))], recvx2.at[j, 0])
        r1[j][1].wait_recv()
        sendx2[j, 1] = (tbuf[j, x_down, 64:128, :] + recvx1[j, 1, 0].astype(F32)).astype(BF)
        down = send([(sendx2.at[j, 1], recvx2.at[j, 1], to_x(3))], recvx2.at[j, 1])
        r2[j] = (up, down)

    for j in range(CHUNKS):
        tbuf[j] = tbuf[j] + term(1, j)
        sendx1[j, 0, 0] = tbuf[j, x_far, 0:64, :].astype(BF)
        sendx1[j, 0, 1] = tbuf[j, x_up, 64:128, :].astype(BF)
        sendx1[j, 1, 0] = tbuf[j, x_far, 64:128, :].astype(BF)
        sendx1[j, 1, 1] = tbuf[j, x_down, 0:64, :].astype(BF)
        r1[j] = [
            send([(sendx1.at[j, i], recvx1.at[j, i], to_x(s))], recvx1.at[j, i])
            for i, s in enumerate((1, 3))
        ]
    a_over_z = second_z(abuf, a_first)

    row = lax.broadcasted_iota(jnp.int32, (16, TOK), 0)
    col = lax.broadcasted_iota(jnp.int32, (16, TOK), 1)
    wanted = jnp.where(row == 0, idx_ref[0, 0], jnp.where(row == 1, idx_ref[0, 1], -1))
    hot = jnp.where(col == wanted, 1.0, 0.0).astype(BF)
    for i, source in enumerate((acts_v[...], grads_v[0])):
        rows = dot(hot, source)
        for s in range(2):
            for k in range(8):
                picks[i, s * 8 + k:s * 8 + k + 1, :] = rows[s:s + 1, 128 * k:128 * k + 128]
    pbuf[x, zl, c] = picks[...].astype(BF)
    pz = gather(pbuf.at[x, zl, c], all_zl, pbuf.at[0, pl.ds(0, 3), 0])

    for j in range(CHUNKS):
        forward(j)
    ex.wait_recv()
    esib = gather(ebuf.at[:, :, c], [sibling], ebuf.at[:, :, c])
    pz.wait_recv()
    px = gather(pbuf.at[x, :, c], all_x, pbuf.at[pl.ds(0, 3), :, 0])
    a_over_x = second_x(abuf, a_first)

    rz, ry = {}, {}

    def sum_x(j):
        r2[j][0].wait_recv()
        r2[j][1].wait_recv()
        top = tbuf[j, x, 0:64, :] + recvx1[j, 1, 1].astype(F32) + recvx2[j, 0].astype(F32)
        low = tbuf[j, x, 64:128, :] + recvx1[j, 0, 1].astype(F32) + recvx2[j, 1].astype(F32)
        sendz[j, 0:4] = top.astype(BF).reshape(4, 16, CW)
        sendz[j, 4:8] = low.astype(BF).reshape(4, 16, CW)
        rz[j] = send(
            [(sendz.at[j, (z + s) % NZ], recvz.at[j, i], to_z(s)) for i, s in enumerate(DZ)],
            recvz.at[j],
        )

    def sum_z(j):
        rz[j].wait_recv()
        total = sendz[j, z].astype(F32)
        for i in range(len(DZ)):
            total = total + recvz[j, i].astype(F32)
        sendy[j] = total.astype(BF)
        ry[j] = send(
            [(sendy.at[j], recvy.at[j, i], to_y(s)) for i, s in enumerate(DY)], recvy.at[j]
        )

    sum_x(0)
    for j in range(1, CHUNKS):
        sum_x(j)
        sum_z(j - 1)
    sum_z(CHUNKS - 1)
    px.wait_recv()
    psib = gather(pbuf.at[:, :, c], [sibling], pbuf.at[:, :, c])
    b_over_x = second_x(bbuf, b_first)

    psib.wait_recv()
    for i in range(2):
        pwide[...] = pbuf[:, :, :, i].reshape(2 * NX * ZL * 16, 128).astype(F32)
        for k in range(8):
            part = jnp.concatenate(
                [pwide[pl.ds(s * 8 + k, 2 * NX * ZL, stride=16), :] for s in range(2)], axis=0
            )
            xbuf[k] = part.astype(BF)
        wide = jnp.concatenate([xbuf[k] for k in range(8)], axis=1)
        sfull[...] = dot(xbuf[dev // 4], wide, (((0,), (0,)), ((), ())))
        rows = sfull[pl.ds(pl.multiple_of((dev % 4) * 32, 32), 32), :]
        for k in range(8):
            ssend[k, i] = rows[:, 128 * k:128 * k + 128].astype(BF)
    sy = send([(ssend.at[(y + s) % NY], srecv.at[i], to_y(s)) for i, s in enumerate(DY)], srecv)

    high_parts, low_parts = [], []
    for j in range(CHUNKS):
        ry[j].wait_recv()
        total = sendy[j].astype(F32)
        for i in range(len(DY)):
            total = total + recvy[j, i].astype(F32)
        high_parts.append(total.astype(BF))
        low_parts.append((total - total.astype(BF).astype(F32)).astype(BF))
    esib.wait_recv()
    columns = ebuf[:, :, :, 1:3].reshape(D, 128)
    product = dot(
        jnp.concatenate(
            [jnp.concatenate(high_parts, axis=1), jnp.concatenate(low_parts, axis=1)], axis=0
        ),
        columns,
    )
    gbuf[c * NX + x, z] = (product[0:16] + product[16:32]).astype(BF)
    mine = gbuf.at[c * NX + x]
    gz = gather(mine.at[z], all_z, gbuf.at[0, pl.ds(0, 7)])
    b_over_z = second_z(bbuf, b_first)

    geig = column(geig_ref[...])
    for m in range(8):
        block = ebuf[m // 2, 2 * (m % 2):2 * (m % 2) + 2, :, 0].astype(F32)
        block = block[0, 0] + block[0, 1] + block[1, 0] + block[1, 1]
        eig_row = block[0:1] + block[1:2] + block[2:3]
        recip[:, 128 * m:128 * m + 128] = 1.0 / (geig * eig_row + 0.1)

    gz.wait_recv()
    gxc = gather(mine, all_xc, gbuf.at[pl.ds(0, 7)])
    a_third = third(abuf, (a_over_x, a_over_z))

    sy.wait_recv()
    stat = ssend[y].astype(F32)
    for i in range(len(DY)):
        stat = stat + srecv[i].astype(F32)
    szsend[...] = stat
    sz = send([(szsend, szrecv, to_z(4))], szrecv)

    gxc.wait_recv()
    turned = gbuf[...].reshape(D, 128).T
    a_third.wait_recv()
    total = jnp.zeros((32, 128), F32)
    for q in range(4):
        cols = slice(256 * q, 256 * q + 256)
        scaled = (dot(turned, abuf[q].reshape(D, 256)) * recip[:, cols]).astype(BF)
        total = total + dot(a_ref[:, cols], scaled, NT)
    qbuf[y] = total.astype(BF)
    qy = gather(qbuf.at[y], all_y, qbuf.at[pl.ds(0, 7)])
    b_third = third(bbuf, (b_over_x, b_over_z))

    sz.wait_recv()
    sout[y] = (szsend[...] + szrecv[...]).astype(BF)
    so = gather(sout.at[y], all_y, sout.at[pl.ds(0, 7)])
    drain()

    qy.wait_recv()
    left = jnp.concatenate([qbuf[k] for k in range(8)], axis=1)
    b_third.wait_recv()
    total = dot(left[:, 0:256], bbuf[0].reshape(D, 256), NT)
    for q in range(1, 4):
        total = total + dot(left[:, 256 * q:256 * q + 256], bbuf[q].reshape(D, 256), NT)
    out_ref[0] = total
    so.wait_recv()
    for i in range(2):
        for k in range(8):
            out_ref[1 + i, :, 128 * k:128 * k + 128] = sout[k, i].astype(F32)


def finish(result_ref, old_act_ref, old_grad_ref, pre_ref, act_ref, grad_ref, *, act_scale, grad_scale):
    pre_ref[...] = result_ref[0]
    act_ref[...] = 0.75 * old_act_ref[...] + act_scale * result_ref[1]
    grad_ref[...] = 0.75 * old_grad_ref[...] + grad_scale * result_ref[2]


def local(
    acts,
    out_grads,
    old_act_factor,
    old_grad_factor,
    act_basis,
    grad_basis,
    act_eigs,
    grad_eigs,
    sample_index,
):
    vmem = pl.BlockSpec(memory_space=pltpu.VMEM)
    hbm = pl.BlockSpec(memory_space=pl.ANY)
    copies = 72
    result = pl.pallas_call(
        kernel,
        out_shape=jax.ShapeDtypeStruct((3, 32, D), F32),
        in_specs=[hbm] * 7,
        out_specs=vmem,
        scratch_shapes=[
            pltpu.SMEM((1, 2), jnp.int32),
            pltpu.VMEM((32, D), BF),
            pltpu.VMEM((1, 32), F32),
            pltpu.VMEM((1, 128), F32),
            pltpu.VMEM((TOK, D), BF),
            pltpu.VMEM((TOK, HALF), BF),
            pltpu.VMEM((2, TOK, D), BF),
            pltpu.VMEM((HALF, 2 * TOK), BF),
            pltpu.VMEM((4, NX, ZL, 64, 256), BF),
            pltpu.VMEM((4, NX, ZL, 64, 256), BF),
            pltpu.VMEM((CHUNKS, NX, 128, CW), F32),
            pltpu.VMEM((CHUNKS, 2, 2, 64, CW), BF),
            pltpu.VMEM((CHUNKS, 2, 2, 64, CW), BF),
            pltpu.VMEM((CHUNKS, 2, 64, CW), BF),
            pltpu.VMEM((CHUNKS, 2, 64, CW), BF),
            pltpu.VMEM((CHUNKS, NZ, 16, CW), BF),
            pltpu.VMEM((CHUNKS, 7, 16, CW), BF),
            pltpu.VMEM((CHUNKS, 16, CW), BF),
            pltpu.VMEM((CHUNKS, 7, 16, CW), BF),
            pltpu.VMEM((2 * NX, NZ, 16, 128), BF),
            pltpu.VMEM((128, D), F32),
            pltpu.VMEM((NY, 32, 128), BF),
            pltpu.VMEM((8, 128), F32),
            pltpu.VMEM((16, 128), F32),
            pltpu.VMEM((NX, ZL, 2, 3, 16, 128), BF),
            pltpu.VMEM((2, 16, 128), F32),
            pltpu.VMEM((NX, ZL, 2, 2, 16, 128), BF),
            pltpu.VMEM((2 * NX * ZL * 16, 128), F32),
            pltpu.VMEM((8, 64, 128), BF),
            pltpu.VMEM((128, D), F32),
            pltpu.VMEM((NY, 2, 32, 128), BF),
            pltpu.VMEM((7, 2, 32, 128), BF),
            pltpu.VMEM((2, 32, 128), F32),
            pltpu.VMEM((2, 32, 128), F32),
            pltpu.VMEM((NY, 2, 32, 128), BF),
            pltpu.SemaphoreType.DMA((12,)),
            pltpu.SemaphoreType.DMA((copies,)),
            pltpu.SemaphoreType.DMA((copies,)),
        ],
        compiler_params=pltpu.CompilerParams(
            collective_id=0, has_side_effects=True, vmem_limit_bytes=63 * 1024 * 1024
        ),
        cost_estimate=pl.CostEstimate(
            flops=4 * TOK * D * D, bytes_accessed=4 * TOK * D, transcendentals=0
        ),
    )(
        sample_index.reshape(1, 2), acts, out_grads, act_basis, grad_basis,
        act_eigs.reshape(1, 32), grad_eigs.reshape(1, D),
    )
    device_count = lax.axis_size("grp") * lax.axis_size("dev")
    total_samples = device_count * sample_index.shape[0]
    total_tokens = device_count * acts.shape[0]
    return pl.pallas_call(
        functools.partial(
            finish,
            act_scale=0.25 / total_samples,
            grad_scale=0.25 * total_tokens / total_samples,
        ),
        out_shape=(jax.ShapeDtypeStruct((32, D), F32),) * 3,
        in_specs=[vmem] * 3,
        out_specs=(vmem,) * 3,
    )(result, old_act_factor, old_grad_factor)


def solution(mesh):
    return jax.shard_map(
        local,
        mesh=mesh,
        in_specs=(
            P(("grp", "dev"), None),
            P(("grp", "dev"), None),
            P("dev", None),
            P("dev", None),
            P("dev", None),
            P("dev", None),
            P("dev"),
            P(),
            P(("grp", "dev")),
        ),
        out_specs=(P("dev", None), P("dev", None), P("dev", None)),
        check_vma=False,
    )
```

```python
import functools

import jax
import jax.numpy as jnp
from jax import lax
from jax.experimental import pallas as pl
from jax.experimental.pallas import tpu as pltpu
from jax.sharding import PartitionSpec as P

NX, NY, NZ, ZL = 4, 8, 8, 4
D, TOK = 1024, 512
HALF = D // 2
CHUNKS, CW = 4, 256
BF, F32 = jnp.bfloat16, jnp.float32
DX = (2, 1, 3)
DY = (4, 3, 5, 2, 6, 1, 7)
DZ = (4, 3, 5, 2, 6, 1, 7)
DZL = (2, 1, 7)
DXC = tuple((dx, dc) for dx in (2, 1, 3, 0) for dc in (1, 0) if (dx, dc) != (0, 0))
NT = (((1,), (1,)), ((), ()))


def dot(left, right, dims=(((1,), (0,)), ((), ()))):
    return lax.dot_general(left, right, dims, preferred_element_type=F32)


def column(row):
    sub = lax.broadcasted_iota(jnp.int32, (128, 128), 0)
    lane = lax.broadcasted_iota(jnp.int32, (128, 128), 1)
    return jnp.sum(jnp.where(sub == lane, row, 0.0), axis=1, keepdims=True)


def kernel(
    idx_hbm, acts_hbm, grads_hbm, a_hbm, b_hbm, aeig_hbm, geig_hbm,
    out_ref,
    idx_ref, a_ref, aeig_ref, geig_ref,
    acts_v, acts_sv, grads_v, actst, abuf, bbuf,
    tbuf, sendx1, recvx1, sendx2, recvx2, sendz, recvz, sendy, recvy,
    gbuf, recip, qbuf,
    shifted, parts, ebuf, picks, pbuf, pwide, xbuf, sfull, ssend, srecv, szsend, szrecv, sout,
    lsem, ssem, rsem,
):
    grp, dev = lax.axis_index("grp"), lax.axis_index("dev")
    y, zh = grp // 2, grp % 2
    x, zl, c = dev // 8, (dev // 2) % 4, dev % 2
    z = zh * ZL + zl

    def at(px, py, pz, pc):
        return {"grp": py * 2 + pz // ZL, "dev": px * 8 + (pz % ZL) * 2 + pc}

    def to_x(step):
        return at((x + step) % NX, y, z, c)

    def to_y(step):
        return at(x, (y + step) % NY, z, c)

    def to_z(step):
        return at(x, y, (z + step) % NZ, c)

    def to_xc(step):
        return at((x + step[0]) % NX, y, z, (c + step[1]) % 2)

    sibling = at(x, y, z, 1 - c)

    counter = [0]
    pending = []

    def send(moves, like):
        n = counter[0]
        counter[0] += 1

        def copy(src, dst, target):
            return pltpu.make_async_remote_copy(
                src_ref=src, dst_ref=dst, send_sem=ssem.at[n], recv_sem=rsem.at[n],
                device_id=target, device_id_type=pl.DeviceIdType.MESH,
            )

        for move in moves:
            copy(*move).start()
        whole = copy(like, like, sibling)
        pending.append(whole)
        return whole

    def gather(ref, targets, like):
        return send([(ref, ref, target) for target in targets], like)

    def drain():
        for copy in pending:
            copy.wait_send()
        pending.clear()

    all_x = [to_x(s) for s in DX]
    all_y = [to_y(s) for s in DY]
    all_z = [to_z(s) for s in DZ]
    all_zl = [to_z(s) for s in DZL]
    all_xc = [to_xc(s) for s in DXC]
    x_up, x_down, x_far = (x + 1) % NX, (x + 3) % NX, (x + 2) % NX
    zl_up, zl_down = (zl + 1) % ZL, (zl + 3) % ZL

    barrier = pltpu.get_barrier_semaphore()
    partners = all_xc + all_y + all_z
    for partner in partners:
        pl.semaphore_signal(
            barrier, inc=1, device_id=partner, device_id_type=pl.DeviceIdType.MESH
        )

    my_rows = pl.ds(pl.multiple_of(c * 32, 32), 32)
    my_cols = pl.ds(pl.multiple_of(y * 128, 128), 128)

    def half(ref, side):
        return ref.at[:, pl.ds(pl.multiple_of(side * HALF, HALF), HALF)]

    def quarter(ref, side, h):
        return ref.at[:, pl.ds(pl.multiple_of(side * HALF + h * 256, 256), 256)]

    moves = [
        (aeig_hbm, aeig_ref),
        (b_hbm.at[pl.ds(0, 16), my_cols], ebuf.at[x, zl, c, 1]),
        (b_hbm.at[pl.ds(16, 16), my_cols], ebuf.at[x, zl, c, 2]),
        (acts_hbm, acts_v), (grads_hbm, grads_v.at[0]), (idx_hbm, idx_ref),
        (geig_hbm.at[:, my_cols], geig_ref), (a_hbm, a_ref),
    ]
    for source, whole in ((a_hbm, abuf), (b_hbm, bbuf)):
        for h in range(2):
            moves.append((quarter(source, c, h), whole.at[2 * c + h, x, zl, my_rows]))
    own = [pltpu.make_async_copy(src, dst, lsem.at[i]) for i, (src, dst) in enumerate(moves)]
    pl.semaphore_wait(barrier, len(partners))

    basis_sib = []
    for source, whole in ((a_hbm, abuf), (b_hbm, bbuf)):
        basis_sib.append(send(
            [
                (quarter(source, 1 - c, h), whole.at[2 * (1 - c) + h, x, zl, my_rows], sibling)
                for h in range(2)
            ],
            whole.at[pl.ds(0, 2), 0, 0, pl.ds(0, 32)],
        ))

    acts_sib = send([(half(acts_hbm, 1 - c), acts_sv, sibling)], acts_sv)
    grads_sib = []
    for j in range(CHUNKS):
        piece = grads_v.at[1, :, pl.ds(CW * j, CW)]
        grads_sib.append(send([(grads_hbm.at[:, pl.ds(CW * j, CW)], piece, sibling)], piece))
    for copy in own:
        copy.start()

    own[0].wait()
    shifted[...] = jnp.zeros((8, 128), F32)
    shifted[0:1, 0:32] = aeig_ref[...]
    eigs = pltpu.roll(shifted[...], (dev % 4) * 32, 1)[0:1, :]
    high = eigs.astype(BF).astype(F32)
    middle = (eigs - high).astype(BF).astype(F32)
    parts[...] = jnp.zeros((16, 128), F32)
    parts[0:1, :] = high
    parts[1:2, :] = middle
    parts[2:3, :] = eigs - high - middle
    ebuf[x, zl, c, 0] = parts[...].astype(BF)
    for copy in own[1:3]:
        copy.wait()
    ez = gather(ebuf.at[x, zl, c], all_zl, ebuf.at[0, pl.ds(0, 3), 0])

    own[3].wait()
    mine = acts_v[:, pl.ds(pl.multiple_of(c * HALF, HALF), HALF)]
    for k in range(2):
        for t in range(2):
            actst[256 * k:256 * k + 256, 256 * t:256 * t + 256] = (
                mine[256 * t:256 * t + 256, 256 * k:256 * k + 256].T
            )

    def first(whole):
        return (
            gather(whole.at[2 * c, x, zl], all_zl, whole.at[0, 0, pl.ds(0, 3)]),
            gather(whole.at[2 * c + 1, x, zl], all_x, whole.at[0, 0, pl.ds(0, 3)]),
        )

    def near_x(whole):
        mine = whole.at[2 * c, x]
        return [send([(mine, mine, to_x(s))], mine) for s in (1, 3)]

    def near_z(whole):
        mine = whole.at[2 * c + 1, :, zl]
        return [send([(mine, mine, to_z(s))], mine) for s in (1, 7)]

    def onward(whole, over_x, over_z):
        out = []
        for block, target, copy in (
            (whole.at[2 * c, x_down, pl.ds(0, 2)], to_x(1), over_x[0]),
            (whole.at[2 * c, x_up, pl.ds(2, 2)], to_x(3), over_x[1]),
            (whole.at[2 * c + 1, pl.ds(0, 2), zl_down], to_z(1), over_z[0]),
            (whole.at[2 * c + 1, pl.ds(2, 2), zl_up], to_z(7), over_z[1]),
        ):
            copy.wait_recv()
            out.append(send([(block, block, target)], block))
        return out

    def third(whole, stage):
        for copy in stage:
            copy.wait_recv()
        mine = whole.at[pl.ds(2 * c, 2)]
        return gather(mine, [sibling], mine)

    for copy in own[4:]:
        copy.wait()
    basis_sib[0].wait_recv()
    a_first = first(abuf)

    def term(slot, j):
        part = dot(
            actst[:, slot * TOK:slot * TOK + TOK], grads_v[slot, :, CW * j:CW * j + CW]
        )
        return part.reshape(NX, 128, CW)

    for j in range(CHUNKS):
        tbuf[j] = term(0, j)
    acts_sib.wait_recv()
    for k in range(2):
        for t in range(2):
            actst[256 * k:256 * k + 256, TOK + 256 * t:TOK + 256 * t + 256] = (
                acts_sv[256 * t:256 * t + 256, 256 * k:256 * k + 256].T
            )

    def pick():
        row = lax.broadcasted_iota(jnp.int32, (16, TOK), 0)
        col = lax.broadcasted_iota(jnp.int32, (16, TOK), 1)
        wanted = jnp.where(row == 0, idx_ref[0, 0], jnp.where(row == 1, idx_ref[0, 1], -1))
        hot = jnp.where(col == wanted, 1.0, 0.0).astype(BF)
        for i, source in enumerate((acts_v[...], grads_v[0])):
            rows = dot(hot, source)
            for s in range(2):
                for k in range(8):
                    picks[i, s * 8 + k:s * 8 + k + 1, :] = rows[s:s + 1, 128 * k:128 * k + 128]
        pbuf[x, zl, c] = picks[...].astype(BF)
        return gather(pbuf.at[x, zl, c], all_zl, pbuf.at[0, pl.ds(0, 3), 0])

    r1, r2 = {}, {}

    def forward(j):
        r1[j][0].wait_recv()
        sendx2[j, 0] = (tbuf[j, x_up, 0:64, :] + recvx1[j, 0, 0].astype(F32)).astype(BF)
        up = send([(sendx2.at[j, 0], recvx2.at[j, 0], to_x(1))], recvx2.at[j, 0])
        r1[j][1].wait_recv()
        sendx2[j, 1] = (tbuf[j, x_down, 64:128, :] + recvx1[j, 1, 0].astype(F32)).astype(BF)
        down = send([(sendx2.at[j, 1], recvx2.at[j, 1], to_x(3))], recvx2.at[j, 1])
        r2[j] = (up, down)

    for j in range(CHUNKS):
        grads_sib[j].wait_recv()
        tbuf[j] = tbuf[j] + term(1, j)
        sendx1[j, 0, 0] = tbuf[j, x_far, 0:64, :].astype(BF)
        sendx1[j, 0, 1] = tbuf[j, x_up, 64:128, :].astype(BF)
        sendx1[j, 1, 0] = tbuf[j, x_far, 64:128, :].astype(BF)
        sendx1[j, 1, 1] = tbuf[j, x_down, 0:64, :].astype(BF)
        r1[j] = [
            send([(sendx1.at[j, i], recvx1.at[j, i], to_x(s))], recvx1.at[j, i])
            for i, s in enumerate((1, 3))
        ]
        if j == 2:
            a_first[1].wait_recv()
            a_over_z = near_z(abuf)
            pz = pick()
        if j > 1:
            forward(j - 2)
    forward(CHUNKS - 2)
    forward(CHUNKS - 1)
    ez.wait_recv()
    ex = gather(ebuf.at[x, :, c], all_x, ebuf.at[pl.ds(0, 3), :, 0])
    pz.wait_recv()
    px = gather(pbuf.at[x, :, c], all_x, pbuf.at[pl.ds(0, 3), :, 0])
    a_first[0].wait_recv()
    a_over_x = near_x(abuf)
    basis_sib[1].wait_recv()
    b_first = first(bbuf)

    rz, ry = {}, {}

    def sum_x(j):
        r2[j][0].wait_recv()
        r2[j][1].wait_recv()
        top = tbuf[j, x, 0:64, :] + recvx1[j, 1, 1].astype(F32) + recvx2[j, 0].astype(F32)
        low = tbuf[j, x, 64:128, :] + recvx1[j, 0, 1].astype(F32) + recvx2[j, 1].astype(F32)
        sendz[j, 0:4] = top.astype(BF).reshape(4, 16, CW)
        sendz[j, 4:8] = low.astype(BF).reshape(4, 16, CW)
        rz[j] = send(
            [(sendz.at[j, (z + s) % NZ], recvz.at[j, i], to_z(s)) for i, s in enumerate(DZ)],
            recvz.at[j],
        )

    def sum_z(j):
        rz[j].wait_recv()
        total = sendz[j, z].astype(F32)
        for i in range(len(DZ)):
            total = total + recvz[j, i].astype(F32)
        sendy[j] = total.astype(BF)
        ry[j] = send(
            [(sendy.at[j], recvy.at[j, i], to_y(s)) for i, s in enumerate(DY)], recvy.at[j]
        )

    sum_x(0)
    sum_x(1)
    sum_z(0)
    sum_x(2)
    sum_z(1)
    sum_x(3)
    sum_z(2)
    ex.wait_recv()
    esib = gather(ebuf.at[:, :, c], [sibling], ebuf.at[:, :, c])
    sum_z(3)
    for copy in b_first:
        copy.wait_recv()
    a_onward = onward(abuf, a_over_x, a_over_z)
    b_over_x, b_over_z = near_x(bbuf), near_z(bbuf)
    px.wait_recv()
    psib = gather(pbuf.at[:, :, c], [sibling], pbuf.at[:, :, c])

    esib.wait_recv()
    geig = column(geig_ref[...])
    for m in range(8):
        block = ebuf[m // 2, 2 * (m % 2):2 * (m % 2) + 2, :, 0].astype(F32)
        block = block[0, 0] + block[0, 1] + block[1, 0] + block[1, 1]
        eig_row = block[0:1] + block[1:2] + block[2:3]
        recip[:, 128 * m:128 * m + 128] = 1.0 / (geig * eig_row + 0.1)

    high_parts, low_parts = [], []
    for j in range(CHUNKS):
        ry[j].wait_recv()
        total = sendy[j].astype(F32)
        for i in range(len(DY)):
            total = total + recvy[j, i].astype(F32)
        high_parts.append(total.astype(BF))
        low_parts.append((total - total.astype(BF).astype(F32)).astype(BF))
    columns = ebuf[:, :, :, 1:3].reshape(D, 128)
    product = dot(
        jnp.concatenate(
            [jnp.concatenate(high_parts, axis=1), jnp.concatenate(low_parts, axis=1)], axis=0
        ),
        columns,
    )
    gbuf[c * NX + x, z] = (product[0:16] + product[16:32]).astype(BF)
    mine = gbuf.at[c * NX + x]
    gz = gather(mine.at[z], all_z, gbuf.at[0, pl.ds(0, 7)])

    psib.wait_recv()
    for i in range(2):
        pwide[...] = pbuf[:, :, :, i].reshape(2 * NX * ZL * 16, 128).astype(F32)
        for k in range(8):
            part = jnp.concatenate(
                [pwide[pl.ds(s * 8 + k, 2 * NX * ZL, stride=16), :] for s in range(2)], axis=0
            )
            xbuf[k] = part.astype(BF)
        wide = jnp.concatenate([xbuf[k] for k in range(8)], axis=1)
        sfull[...] = dot(xbuf[dev // 4], wide, (((0,), (0,)), ((), ())))
        rows = sfull[pl.ds(pl.multiple_of((dev % 4) * 32, 32), 32), :]
        for k in range(8):
            ssend[k, i] = rows[:, 128 * k:128 * k + 128].astype(BF)
    sy = send([(ssend.at[(y + s) % NY], srecv.at[i], to_y(s)) for i, s in enumerate(DY)], srecv)

    b_onward = onward(bbuf, b_over_x, b_over_z)
    gz.wait_recv()
    gxc = gather(mine, all_xc, gbuf.at[pl.ds(0, 7)])
    a_third = third(abuf, a_onward)

    sy.wait_recv()
    stat = ssend[y].astype(F32)
    for i in range(len(DY)):
        stat = stat + srecv[i].astype(F32)
    szsend[...] = stat
    sz = send([(szsend, szrecv, to_z(4))], szrecv)

    gxc.wait_recv()
    turned = gbuf[...].reshape(D, 128).T
    a_third.wait_recv()
    total = jnp.zeros((32, 128), F32)
    for q in range(4):
        cols = slice(256 * q, 256 * q + 256)
        scaled = (dot(turned, abuf[q].reshape(D, 256)) * recip[:, cols]).astype(BF)
        total = total + dot(a_ref[:, cols], scaled, NT)
    qbuf[y] = total.astype(BF)
    qy = gather(qbuf.at[y], all_y, qbuf.at[pl.ds(0, 7)])
    b_third = third(bbuf, b_onward)

    sz.wait_recv()
    sout[y] = (szsend[...] + szrecv[...]).astype(BF)
    so = gather(sout.at[y], all_y, sout.at[pl.ds(0, 7)])
    drain()

    qy.wait_recv()
    left = jnp.concatenate([qbuf[k] for k in range(8)], axis=1)
    b_third.wait_recv()
    total = dot(left[:, 0:256], bbuf[0].reshape(D, 256), NT)
    for q in range(1, 4):
        total = total + dot(left[:, 256 * q:256 * q + 256], bbuf[q].reshape(D, 256), NT)
    out_ref[0] = total
    so.wait_recv()
    for i in range(2):
        for k in range(8):
            out_ref[1 + i, :, 128 * k:128 * k + 128] = sout[k, i].astype(F32)


def finish(result_ref, old_act_ref, old_grad_ref, pre_ref, act_ref, grad_ref, *, act_scale, grad_scale):
    pre_ref[...] = result_ref[0]
    act_ref[...] = 0.75 * old_act_ref[...] + act_scale * result_ref[1]
    grad_ref[...] = 0.75 * old_grad_ref[...] + grad_scale * result_ref[2]


def local(
    acts,
    out_grads,
    old_act_factor,
    old_grad_factor,
    act_basis,
    grad_basis,
    act_eigs,
    grad_eigs,
    sample_index,
):
    vmem = pl.BlockSpec(memory_space=pltpu.VMEM)
    hbm = pl.BlockSpec(memory_space=pl.ANY)
    copies = 96
    result = pl.pallas_call(
        kernel,
        out_shape=jax.ShapeDtypeStruct((3, 32, D), F32),
        in_specs=[hbm] * 7,
        out_specs=vmem,
        scratch_shapes=[
            pltpu.SMEM((1, 2), jnp.int32),
            pltpu.VMEM((32, D), BF),
            pltpu.VMEM((1, 32), F32),
            pltpu.VMEM((1, 128), F32),
            pltpu.VMEM((TOK, D), BF),
            pltpu.VMEM((TOK, HALF), BF),
            pltpu.VMEM((2, TOK, D), BF),
            pltpu.VMEM((HALF, 2 * TOK), BF),
            pltpu.VMEM((4, NX, ZL, 64, 256), BF),
            pltpu.VMEM((4, NX, ZL, 64, 256), BF),
            pltpu.VMEM((CHUNKS, NX, 128, CW), F32),
            pltpu.VMEM((CHUNKS, 2, 2, 64, CW), BF),
            pltpu.VMEM((CHUNKS, 2, 2, 64, CW), BF),
            pltpu.VMEM((CHUNKS, 2, 64, CW), BF),
            pltpu.VMEM((CHUNKS, 2, 64, CW), BF),
            pltpu.VMEM((CHUNKS, NZ, 16, CW), BF),
            pltpu.VMEM((CHUNKS, 7, 16, CW), BF),
            pltpu.VMEM((CHUNKS, 16, CW), BF),
            pltpu.VMEM((CHUNKS, 7, 16, CW), BF),
            pltpu.VMEM((2 * NX, NZ, 16, 128), BF),
            pltpu.VMEM((128, D), F32),
            pltpu.VMEM((NY, 32, 128), BF),
            pltpu.VMEM((8, 128), F32),
            pltpu.VMEM((16, 128), F32),
            pltpu.VMEM((NX, ZL, 2, 3, 16, 128), BF),
            pltpu.VMEM((2, 16, 128), F32),
            pltpu.VMEM((NX, ZL, 2, 2, 16, 128), BF),
            pltpu.VMEM((2 * NX * ZL * 16, 128), F32),
            pltpu.VMEM((8, 64, 128), BF),
            pltpu.VMEM((128, D), F32),
            pltpu.VMEM((NY, 2, 32, 128), BF),
            pltpu.VMEM((7, 2, 32, 128), BF),
            pltpu.VMEM((2, 32, 128), F32),
            pltpu.VMEM((2, 32, 128), F32),
            pltpu.VMEM((NY, 2, 32, 128), BF),
            pltpu.SemaphoreType.DMA((12,)),
            pltpu.SemaphoreType.DMA((copies,)),
            pltpu.SemaphoreType.DMA((copies,)),
        ],
        compiler_params=pltpu.CompilerParams(
            collective_id=0, has_side_effects=True, vmem_limit_bytes=63 * 1024 * 1024
        ),
        cost_estimate=pl.CostEstimate(
            flops=4 * TOK * D * D, bytes_accessed=4 * TOK * D, transcendentals=0
        ),
    )(
        sample_index.reshape(1, 2), acts, out_grads, act_basis, grad_basis,
        act_eigs.reshape(1, 32), grad_eigs.reshape(1, D),
    )
    device_count = lax.axis_size("grp") * lax.axis_size("dev")
    total_samples = device_count * sample_index.shape[0]
    total_tokens = device_count * acts.shape[0]
    return pl.pallas_call(
        functools.partial(
            finish,
            act_scale=0.25 / total_samples,
            grad_scale=0.25 * total_tokens / total_samples,
        ),
        out_shape=(jax.ShapeDtypeStruct((32, D), F32),) * 3,
        in_specs=[vmem] * 3,
        out_specs=(vmem,) * 3,
    )(result, old_act_factor, old_grad_factor)


def solution(mesh):
    return jax.shard_map(
        local,
        mesh=mesh,
        in_specs=(
            P(("grp", "dev"), None),
            P(("grp", "dev"), None),
            P("dev", None),
            P("dev", None),
            P("dev", None),
            P("dev", None),
            P("dev"),
            P(),
            P(("grp", "dev")),
        ),
        out_specs=(P("dev", None), P("dev", None), P("dev", None)),
        check_vma=False,
    )
```

```python
import functools

import jax
import jax.numpy as jnp
from jax import lax
from jax.experimental import pallas as pl
from jax.experimental.pallas import tpu as pltpu
from jax.sharding import PartitionSpec as P

NX, NY, NZ, ZL = 4, 8, 8, 4
D, TOK = 1024, 512
HALF = D // 2
WIDTHS = (384, 256, 256, 128)
STARTS = (0, 384, 640, 896)
CHUNKS = len(WIDTHS)
BF, F32 = jnp.bfloat16, jnp.float32
DX = (2, 1, 3)
DY = (4, 3, 5, 2, 6, 1, 7)
DZ = (4, 3, 5, 2, 6, 1, 7)
DZL = (2, 1, 7)
DXC = tuple((dx, dc) for dx in (2, 1, 3, 0) for dc in (1, 0) if (dx, dc) != (0, 0))
NT = (((1,), (1,)), ((), ()))


def dot(left, right, dims=(((1,), (0,)), ((), ()))):
    return lax.dot_general(left, right, dims, preferred_element_type=F32)


def column(row):
    sub = lax.broadcasted_iota(jnp.int32, (128, 128), 0)
    lane = lax.broadcasted_iota(jnp.int32, (128, 128), 1)
    return jnp.sum(jnp.where(sub == lane, row, 0.0), axis=1, keepdims=True)


def kernel(
    idx_hbm, acts_hbm, grads_hbm, a_hbm, b_hbm, aeig_hbm, geig_hbm,
    out_ref,
    idx_ref, a_ref, aeig_ref, geig_ref,
    acts_v, acts_sv, grads_v, actst, abuf, bbuf,
    tbuf, sendx1, recvx1, sendx2, recvx2, sendz, recvz, sendy, recvy,
    gbuf, recip, qbuf,
    shifted, parts, ebuf, picks, pbuf, pwide, xbuf, sfull, ssend, srecv, szsend, szrecv, sout,
    lsem, ssem, rsem,
):
    grp, dev = lax.axis_index("grp"), lax.axis_index("dev")
    y, zh = grp // 2, grp % 2
    x, zl, c = dev // 8, (dev // 2) % 4, dev % 2
    z = zh * ZL + zl

    def at(px, py, pz, pc):
        return {"grp": py * 2 + pz // ZL, "dev": px * 8 + (pz % ZL) * 2 + pc}

    def to_x(step):
        return at((x + step) % NX, y, z, c)

    def to_y(step):
        return at(x, (y + step) % NY, z, c)

    def to_z(step):
        return at(x, y, (z + step) % NZ, c)

    def to_xc(step):
        return at((x + step[0]) % NX, y, z, (c + step[1]) % 2)

    sibling = at(x, y, z, 1 - c)

    counter = [0]
    pending = []

    def send(moves, like):
        n = counter[0]
        counter[0] += 1

        def copy(src, dst, target):
            return pltpu.make_async_remote_copy(
                src_ref=src, dst_ref=dst, send_sem=ssem.at[n], recv_sem=rsem.at[n],
                device_id=target, device_id_type=pl.DeviceIdType.MESH,
            )

        for move in moves:
            copy(*move).start()
        whole = copy(like, like, sibling)
        pending.append(whole)
        return whole

    def gather(ref, targets, like):
        return send([(ref, ref, target) for target in targets], like)

    def drain():
        for copy in pending:
            copy.wait_send()
        pending.clear()

    all_x = [to_x(s) for s in DX]
    all_y = [to_y(s) for s in DY]
    all_z = [to_z(s) for s in DZ]
    all_zl = [to_z(s) for s in DZL]
    all_xc = [to_xc(s) for s in DXC]
    x_up, x_down, x_far = (x + 1) % NX, (x + 3) % NX, (x + 2) % NX
    zl_up, zl_down = (zl + 1) % ZL, (zl + 3) % ZL

    barrier = pltpu.get_barrier_semaphore()
    partners = all_xc + all_y + all_z
    for partner in partners:
        pl.semaphore_signal(
            barrier, inc=1, device_id=partner, device_id_type=pl.DeviceIdType.MESH
        )

    my_rows = pl.ds(pl.multiple_of(c * 32, 32), 32)
    my_cols = pl.ds(pl.multiple_of(y * 128, 128), 128)

    def half(ref, side):
        return ref.at[:, pl.ds(pl.multiple_of(side * HALF, HALF), HALF)]

    def quarter(ref, side, h):
        return ref.at[:, pl.ds(pl.multiple_of(side * HALF + h * 256, 256), 256)]

    moves = [
        (aeig_hbm, aeig_ref),
        (b_hbm.at[pl.ds(0, 16), my_cols], ebuf.at[x, zl, c, 1]),
        (b_hbm.at[pl.ds(16, 16), my_cols], ebuf.at[x, zl, c, 2]),
        (acts_hbm, acts_v), (grads_hbm, grads_v.at[0]), (idx_hbm, idx_ref),
        (geig_hbm.at[:, my_cols], geig_ref), (a_hbm, a_ref),
    ]
    for source, whole in ((a_hbm, abuf), (b_hbm, bbuf)):
        for h in range(2):
            moves.append((quarter(source, c, h), whole.at[2 * c + h, x, zl, my_rows]))
    own = [pltpu.make_async_copy(src, dst, lsem.at[i]) for i, (src, dst) in enumerate(moves)]
    pl.semaphore_wait(barrier, len(partners))

    basis_sib = []
    for source, whole in ((a_hbm, abuf), (b_hbm, bbuf)):
        basis_sib.append(send(
            [
                (quarter(source, 1 - c, h), whole.at[2 * (1 - c) + h, x, zl, my_rows], sibling)
                for h in range(2)
            ],
            whole.at[pl.ds(0, 2), 0, 0, pl.ds(0, 32)],
        ))

    acts_sib = send([(half(acts_hbm, 1 - c), acts_sv, sibling)], acts_sv)
    grads_sib = []
    for j in range(CHUNKS):
        piece = grads_v.at[1, :, pl.ds(STARTS[j], WIDTHS[j])]
        grads_sib.append(send([(grads_hbm.at[:, pl.ds(STARTS[j], WIDTHS[j])], piece, sibling)], piece))
    for copy in own:
        copy.start()

    own[0].wait()
    shifted[...] = jnp.zeros((8, 128), F32)
    shifted[0:1, 0:32] = aeig_ref[...]
    eigs = pltpu.roll(shifted[...], (dev % 4) * 32, 1)[0:1, :]
    high = eigs.astype(BF).astype(F32)
    middle = (eigs - high).astype(BF).astype(F32)
    parts[...] = jnp.zeros((16, 128), F32)
    parts[0:1, :] = high
    parts[1:2, :] = middle
    parts[2:3, :] = eigs - high - middle
    ebuf[x, zl, c, 0] = parts[...].astype(BF)
    for copy in own[1:3]:
        copy.wait()
    ez = gather(ebuf.at[x, zl, c], all_zl, ebuf.at[0, pl.ds(0, 3), 0])

    own[3].wait()
    mine = acts_v[:, pl.ds(pl.multiple_of(c * HALF, HALF), HALF)]
    for k in range(2):
        for t in range(2):
            actst[256 * k:256 * k + 256, 256 * t:256 * t + 256] = (
                mine[256 * t:256 * t + 256, 256 * k:256 * k + 256].T
            )

    def first(whole):
        return (
            gather(whole.at[2 * c, x, zl], all_zl, whole.at[0, 0, pl.ds(0, 3)]),
            gather(whole.at[2 * c + 1, x, zl], all_x, whole.at[0, 0, pl.ds(0, 3)]),
        )

    def near_x(whole):
        mine = whole.at[2 * c, x]
        return [send([(mine, mine, to_x(s))], mine) for s in (1, 3)]

    def near_z(whole):
        mine = whole.at[2 * c + 1, :, zl]
        return [send([(mine, mine, to_z(s))], mine) for s in (1, 7)]

    def onward(whole, over_x, over_z):
        out = []
        for block, target, copy in (
            (whole.at[2 * c, x_down, pl.ds(0, 2)], to_x(1), over_x[0]),
            (whole.at[2 * c, x_up, pl.ds(2, 2)], to_x(3), over_x[1]),
            (whole.at[2 * c + 1, pl.ds(0, 2), zl_down], to_z(1), over_z[0]),
            (whole.at[2 * c + 1, pl.ds(2, 2), zl_up], to_z(7), over_z[1]),
        ):
            copy.wait_recv()
            out.append(send([(block, block, target)], block))
        return out

    def third(whole, stage):
        for copy in stage:
            copy.wait_recv()
        mine = whole.at[pl.ds(2 * c, 2)]
        return gather(mine, [sibling], mine)

    for copy in own[4:]:
        copy.wait()
    basis_sib[0].wait_recv()
    a_first = first(abuf)

    def term(slot, j):
        part = dot(
            actst[:, slot * TOK:slot * TOK + TOK], grads_v[slot, :, STARTS[j]:STARTS[j] + WIDTHS[j]]
        )
        return part.reshape(NX, 128, WIDTHS[j])

    for j in range(CHUNKS):
        tbuf[j][...] = term(0, j)
    acts_sib.wait_recv()
    for k in range(2):
        for t in range(2):
            actst[256 * k:256 * k + 256, TOK + 256 * t:TOK + 256 * t + 256] = (
                acts_sv[256 * t:256 * t + 256, 256 * k:256 * k + 256].T
            )

    def pick():
        row = lax.broadcasted_iota(jnp.int32, (16, TOK), 0)
        col = lax.broadcasted_iota(jnp.int32, (16, TOK), 1)
        wanted = jnp.where(row == 0, idx_ref[0, 0], jnp.where(row == 1, idx_ref[0, 1], -1))
        hot = jnp.where(col == wanted, 1.0, 0.0).astype(BF)
        for i, source in enumerate((acts_v[...], grads_v[0])):
            rows = dot(hot, source)
            for s in range(2):
                for k in range(8):
                    picks[i, s * 8 + k:s * 8 + k + 1, :] = rows[s:s + 1, 128 * k:128 * k + 128]
        pbuf[x, zl, c] = picks[...].astype(BF)
        return gather(pbuf.at[x, zl, c], all_zl, pbuf.at[0, pl.ds(0, 3), 0])

    r1, r2 = {}, {}

    def forward(j):
        r1[j][0].wait_recv()
        sendx2[j][0] = (tbuf[j][x_up, 0:64, :] + recvx1[j][0, 0].astype(F32)).astype(BF)
        up = send([(sendx2[j].at[0], recvx2[j].at[0], to_x(1))], recvx2[j].at[0])
        r1[j][1].wait_recv()
        sendx2[j][1] = (tbuf[j][x_down, 64:128, :] + recvx1[j][1, 0].astype(F32)).astype(BF)
        down = send([(sendx2[j].at[1], recvx2[j].at[1], to_x(3))], recvx2[j].at[1])
        r2[j] = (up, down)

    for j in range(CHUNKS):
        grads_sib[j].wait_recv()
        tbuf[j][...] = tbuf[j][...] + term(1, j)
        sendx1[j][0, 0] = tbuf[j][x_far, 0:64, :].astype(BF)
        sendx1[j][0, 1] = tbuf[j][x_up, 64:128, :].astype(BF)
        sendx1[j][1, 0] = tbuf[j][x_far, 64:128, :].astype(BF)
        sendx1[j][1, 1] = tbuf[j][x_down, 0:64, :].astype(BF)
        r1[j] = [
            send([(sendx1[j].at[i], recvx1[j].at[i], to_x(s))], recvx1[j].at[i])
            for i, s in enumerate((1, 3))
        ]
        if j == 2:
            a_first[1].wait_recv()
            a_over_z = near_z(abuf)
            pz = pick()
        if j > 1:
            forward(j - 2)
    forward(CHUNKS - 2)
    forward(CHUNKS - 1)
    ez.wait_recv()
    ex = gather(ebuf.at[x, :, c], all_x, ebuf.at[pl.ds(0, 3), :, 0])
    pz.wait_recv()
    px = gather(pbuf.at[x, :, c], all_x, pbuf.at[pl.ds(0, 3), :, 0])
    a_first[0].wait_recv()
    a_over_x = near_x(abuf)
    basis_sib[1].wait_recv()
    b_first = first(bbuf)

    rz, ry = {}, {}

    def sum_x(j):
        r2[j][0].wait_recv()
        r2[j][1].wait_recv()
        top = tbuf[j][x, 0:64, :] + recvx1[j][1, 1].astype(F32) + recvx2[j][0].astype(F32)
        low = tbuf[j][x, 64:128, :] + recvx1[j][0, 1].astype(F32) + recvx2[j][1].astype(F32)
        sendz[j][0:4] = top.astype(BF).reshape(4, 16, WIDTHS[j])
        sendz[j][4:8] = low.astype(BF).reshape(4, 16, WIDTHS[j])
        rz[j] = send(
            [(sendz[j].at[(z + s) % NZ], recvz[j].at[i], to_z(s)) for i, s in enumerate(DZ)],
            recvz[j],
        )

    def sum_z(j):
        rz[j].wait_recv()
        total = sendz[j][z].astype(F32)
        for i in range(len(DZ)):
            total = total + recvz[j][i].astype(F32)
        sendy[j][...] = total.astype(BF)
        ry[j] = send(
            [(sendy[j], recvy[j].at[i], to_y(s)) for i, s in enumerate(DY)], recvy[j]
        )

    sum_x(0)
    sum_x(1)
    sum_z(0)
    sum_x(2)
    sum_z(1)
    sum_x(3)
    sum_z(2)
    ex.wait_recv()
    esib = gather(ebuf.at[:, :, c], [sibling], ebuf.at[:, :, c])
    sum_z(3)
    for copy in b_first:
        copy.wait_recv()
    a_onward = onward(abuf, a_over_x, a_over_z)
    b_over_x, b_over_z = near_x(bbuf), near_z(bbuf)
    px.wait_recv()
    psib = gather(pbuf.at[:, :, c], [sibling], pbuf.at[:, :, c])

    esib.wait_recv()
    geig = column(geig_ref[...])
    for m in range(8):
        block = ebuf[m // 2, 2 * (m % 2):2 * (m % 2) + 2, :, 0].astype(F32)
        block = block[0, 0] + block[0, 1] + block[1, 0] + block[1, 1]
        eig_row = block[0:1] + block[1:2] + block[2:3]
        recip[:, 128 * m:128 * m + 128] = 1.0 / (geig * eig_row + 0.1)

    high_parts, low_parts = [], []
    for j in range(CHUNKS):
        ry[j].wait_recv()
        total = sendy[j][...].astype(F32)
        for i in range(len(DY)):
            total = total + recvy[j][i].astype(F32)
        high_parts.append(total.astype(BF))
        low_parts.append((total - total.astype(BF).astype(F32)).astype(BF))
    columns = ebuf[:, :, :, 1:3].reshape(D, 128)
    product = dot(
        jnp.concatenate(
            [jnp.concatenate(high_parts, axis=1), jnp.concatenate(low_parts, axis=1)], axis=0
        ),
        columns,
    )
    gbuf[c * NX + x, z] = (product[0:16] + product[16:32]).astype(BF)
    mine = gbuf.at[c * NX + x]
    gz = gather(mine.at[z], all_z, gbuf.at[0, pl.ds(0, 7)])
    a_third = third(abuf, a_onward)

    psib.wait_recv()
    for i in range(2):
        pwide[...] = pbuf[:, :, :, i].reshape(2 * NX * ZL * 16, 128).astype(F32)
        for k in range(8):
            part = jnp.concatenate(
                [pwide[pl.ds(s * 8 + k, 2 * NX * ZL, stride=16), :] for s in range(2)], axis=0
            )
            xbuf[k] = part.astype(BF)
        wide = jnp.concatenate([xbuf[k] for k in range(8)], axis=1)
        sfull[...] = dot(xbuf[dev // 4], wide, (((0,), (0,)), ((), ())))
        rows = sfull[pl.ds(pl.multiple_of((dev % 4) * 32, 32), 32), :]
        for k in range(8):
            ssend[k, i] = rows[:, 128 * k:128 * k + 128].astype(BF)
    sy = send([(ssend.at[(y + s) % NY], srecv.at[i], to_y(s)) for i, s in enumerate(DY)], srecv)

    b_onward = onward(bbuf, b_over_x, b_over_z)
    gz.wait_recv()
    gxc = gather(mine, all_xc, gbuf.at[pl.ds(0, 7)])
    b_third = third(bbuf, b_onward)

    sy.wait_recv()
    stat = ssend[y].astype(F32)
    for i in range(len(DY)):
        stat = stat + srecv[i].astype(F32)
    szsend[...] = stat
    sz = send([(szsend, szrecv, to_z(4))], szrecv)

    gxc.wait_recv()
    turned = gbuf[...].reshape(D, 128).T
    a_third.wait_recv()
    total = jnp.zeros((32, 128), F32)
    for q in range(4):
        cols = slice(256 * q, 256 * q + 256)
        scaled = (dot(turned, abuf[q].reshape(D, 256)) * recip[:, cols]).astype(BF)
        total = total + dot(a_ref[:, cols], scaled, NT)
    qbuf[y] = total.astype(BF)
    qy = gather(qbuf.at[y], all_y, qbuf.at[pl.ds(0, 7)])

    sz.wait_recv()
    sout[y] = (szsend[...] + szrecv[...]).astype(BF)
    so = gather(sout.at[y], all_y, sout.at[pl.ds(0, 7)])
    drain()

    qy.wait_recv()
    left = jnp.concatenate([qbuf[k] for k in range(8)], axis=1)
    b_third.wait_recv()
    total = dot(left[:, 0:256], bbuf[0].reshape(D, 256), NT)
    for q in range(1, 4):
        total = total + dot(left[:, 256 * q:256 * q + 256], bbuf[q].reshape(D, 256), NT)
    out_ref[0] = total
    so.wait_recv()
    for i in range(2):
        for k in range(8):
            out_ref[1 + i, :, 128 * k:128 * k + 128] = sout[k, i].astype(F32)


def finish(result_ref, old_act_ref, old_grad_ref, pre_ref, act_ref, grad_ref, *, act_scale, grad_scale):
    pre_ref[...] = result_ref[0]
    act_ref[...] = 0.75 * old_act_ref[...] + act_scale * result_ref[1]
    grad_ref[...] = 0.75 * old_grad_ref[...] + grad_scale * result_ref[2]


def local(
    acts,
    out_grads,
    old_act_factor,
    old_grad_factor,
    act_basis,
    grad_basis,
    act_eigs,
    grad_eigs,
    sample_index,
):
    vmem = pl.BlockSpec(memory_space=pltpu.VMEM)
    hbm = pl.BlockSpec(memory_space=pl.ANY)
    copies = 96
    result = pl.pallas_call(
        kernel,
        out_shape=jax.ShapeDtypeStruct((3, 32, D), F32),
        in_specs=[hbm] * 7,
        out_specs=vmem,
        scratch_shapes=[
            pltpu.SMEM((1, 2), jnp.int32),
            pltpu.VMEM((32, D), BF),
            pltpu.VMEM((1, 32), F32),
            pltpu.VMEM((1, 128), F32),
            pltpu.VMEM((TOK, D), BF),
            pltpu.VMEM((TOK, HALF), BF),
            pltpu.VMEM((2, TOK, D), BF),
            pltpu.VMEM((HALF, 2 * TOK), BF),
            pltpu.VMEM((4, NX, ZL, 64, 256), BF),
            pltpu.VMEM((4, NX, ZL, 64, 256), BF),
            [pltpu.VMEM((NX, 128, w), F32) for w in WIDTHS],
            [pltpu.VMEM((2, 2, 64, w), BF) for w in WIDTHS],
            [pltpu.VMEM((2, 2, 64, w), BF) for w in WIDTHS],
            [pltpu.VMEM((2, 64, w), BF) for w in WIDTHS],
            [pltpu.VMEM((2, 64, w), BF) for w in WIDTHS],
            [pltpu.VMEM((NZ, 16, w), BF) for w in WIDTHS],
            [pltpu.VMEM((7, 16, w), BF) for w in WIDTHS],
            [pltpu.VMEM((16, w), BF) for w in WIDTHS],
            [pltpu.VMEM((7, 16, w), BF) for w in WIDTHS],
            pltpu.VMEM((2 * NX, NZ, 16, 128), BF),
            pltpu.VMEM((128, D), F32),
            pltpu.VMEM((NY, 32, 128), BF),
            pltpu.VMEM((8, 128), F32),
            pltpu.VMEM((16, 128), F32),
            pltpu.VMEM((NX, ZL, 2, 3, 16, 128), BF),
            pltpu.VMEM((2, 16, 128), F32),
            pltpu.VMEM((NX, ZL, 2, 2, 16, 128), BF),
            pltpu.VMEM((2 * NX * ZL * 16, 128), F32),
            pltpu.VMEM((8, 64, 128), BF),
            pltpu.VMEM((128, D), F32),
            pltpu.VMEM((NY, 2, 32, 128), BF),
            pltpu.VMEM((7, 2, 32, 128), BF),
            pltpu.VMEM((2, 32, 128), F32),
            pltpu.VMEM((2, 32, 128), F32),
            pltpu.VMEM((NY, 2, 32, 128), BF),
            pltpu.SemaphoreType.DMA((12,)),
            pltpu.SemaphoreType.DMA((copies,)),
            pltpu.SemaphoreType.DMA((copies,)),
        ],
        compiler_params=pltpu.CompilerParams(
            collective_id=0, has_side_effects=True, vmem_limit_bytes=63 * 1024 * 1024
        ),
        cost_estimate=pl.CostEstimate(
            flops=4 * TOK * D * D, bytes_accessed=4 * TOK * D, transcendentals=0
        ),
    )(
        sample_index.reshape(1, 2), acts, out_grads, act_basis, grad_basis,
        act_eigs.reshape(1, 32), grad_eigs.reshape(1, D),
    )
    device_count = lax.axis_size("grp") * lax.axis_size("dev")
    total_samples = device_count * sample_index.shape[0]
    total_tokens = device_count * acts.shape[0]
    return pl.pallas_call(
        functools.partial(
            finish,
            act_scale=0.25 / total_samples,
            grad_scale=0.25 * total_tokens / total_samples,
        ),
        out_shape=(jax.ShapeDtypeStruct((32, D), F32),) * 3,
        in_specs=[vmem] * 3,
        out_specs=(vmem,) * 3,
    )(result, old_act_factor, old_grad_factor)


def solution(mesh):
    return jax.shard_map(
        local,
        mesh=mesh,
        in_specs=(
            P(("grp", "dev"), None),
            P(("grp", "dev"), None),
            P("dev", None),
            P("dev", None),
            P("dev", None),
            P("dev", None),
            P("dev"),
            P(),
            P(("grp", "dev")),
        ),
        out_specs=(P("dev", None), P("dev", None), P("dev", None)),
        check_vma=False,
    )
```

```python
import functools

import jax
import jax.numpy as jnp
from jax import lax
from jax.experimental import pallas as pl
from jax.experimental.pallas import tpu as pltpu
from jax.sharding import PartitionSpec as P

NX, NY, NZ, ZL = 4, 8, 8, 4
D, TOK = 1024, 512
HALF = D // 2
CHUNKS, CW = 4, 256
BF, F32 = jnp.bfloat16, jnp.float32
DX = (2, 1, 3)
DY = (4, 3, 5, 2, 6, 1, 7)
DZ = (4, 3, 5, 2, 6, 1, 7)
DZL = (2, 1, 7)
DXC = tuple((dx, dc) for dx in (2, 1, 3, 0) for dc in (1, 0) if (dx, dc) != (0, 0))
NT = (((1,), (1,)), ((), ()))


def dot(left, right, dims=(((1,), (0,)), ((), ()))):
    return lax.dot_general(left, right, dims, preferred_element_type=F32)


def column(row):
    sub = lax.broadcasted_iota(jnp.int32, (128, 128), 0)
    lane = lax.broadcasted_iota(jnp.int32, (128, 128), 1)
    return jnp.sum(jnp.where(sub == lane, row, 0.0), axis=1, keepdims=True)


def kernel(
    idx_hbm, acts_hbm, grads_hbm, a_hbm, b_hbm, aeig_hbm, geig_hbm,
    out_ref,
    idx_ref, a_ref, aeig_ref, geig_ref,
    acts_v, acts_sv, grads_v, actst, abuf,
    tbuf, sendx1, recvx1, sendx2, recvx2, sendz, recvz, sendy, recvy,
    gbuf, recip, qsend, qrecv, qbuf,
    shifted, parts, ebuf, picks, pbuf, pwide, xbuf, sfull, ssend, srecv, szsend, szrecv, sout,
    lsem, ssem, rsem,
):
    grp, dev = lax.axis_index("grp"), lax.axis_index("dev")
    y, zh = grp // 2, grp % 2
    x, zl, c = dev // 8, (dev // 2) % 4, dev % 2
    z = zh * ZL + zl

    def at(px, py, pz, pc):
        return {"grp": py * 2 + pz // ZL, "dev": px * 8 + (pz % ZL) * 2 + pc}

    def to_x(step):
        return at((x + step) % NX, y, z, c)

    def to_y(step):
        return at(x, (y + step) % NY, z, c)

    def to_z(step):
        return at(x, y, (z + step) % NZ, c)

    def to_xc(step):
        return at((x + step[0]) % NX, y, z, (c + step[1]) % 2)

    sibling = at(x, y, z, 1 - c)

    counter = [0]
    pending = []

    def send(moves, like):
        n = counter[0]
        counter[0] += 1

        def copy(src, dst, target):
            return pltpu.make_async_remote_copy(
                src_ref=src, dst_ref=dst, send_sem=ssem.at[n], recv_sem=rsem.at[n],
                device_id=target, device_id_type=pl.DeviceIdType.MESH,
            )

        for move in moves:
            copy(*move).start()
        whole = copy(like, like, sibling)
        pending.append(whole)
        return whole

    def gather(ref, targets, like):
        return send([(ref, ref, target) for target in targets], like)

    def drain():
        for copy in pending:
            copy.wait_send()
        pending.clear()

    all_x = [to_x(s) for s in DX]
    all_y = [to_y(s) for s in DY]
    all_z = [to_z(s) for s in DZ]
    all_zl = [to_z(s) for s in DZL]
    all_xc = [to_xc(s) for s in DXC]
    x_up, x_down, x_far = (x + 1) % NX, (x + 3) % NX, (x + 2) % NX
    zl_up, zl_down = (zl + 1) % ZL, (zl + 3) % ZL

    barrier = pltpu.get_barrier_semaphore()
    partners = all_xc + all_y + all_z
    for partner in partners:
        pl.semaphore_signal(
            barrier, inc=1, device_id=partner, device_id_type=pl.DeviceIdType.MESH
        )

    my_rows = pl.ds(pl.multiple_of(c * 32, 32), 32)
    my_cols = pl.ds(pl.multiple_of(y * 128, 128), 128)

    def half(ref, side):
        return ref.at[:, pl.ds(pl.multiple_of(side * HALF, HALF), HALF)]

    def quarter(ref, side, h):
        return ref.at[:, pl.ds(pl.multiple_of(side * HALF + h * 256, 256), 256)]

    moves = [
        (aeig_hbm, aeig_ref),
        (b_hbm.at[pl.ds(0, 16), my_cols], ebuf.at[x, zl, c, 1]),
        (b_hbm.at[pl.ds(16, 16), my_cols], ebuf.at[x, zl, c, 2]),
        (acts_hbm, acts_v), (grads_hbm, grads_v.at[0]), (idx_hbm, idx_ref),
        (geig_hbm.at[:, my_cols], geig_ref), (a_hbm, a_ref),
    ]
    for h in range(2):
        moves.append((quarter(a_hbm, c, h), abuf.at[2 * c + h, x, zl, my_rows]))
    own = [pltpu.make_async_copy(src, dst, lsem.at[i]) for i, (src, dst) in enumerate(moves)]
    pl.semaphore_wait(barrier, len(partners))

    basis_sib = send(
        [
            (quarter(a_hbm, 1 - c, h), abuf.at[2 * (1 - c) + h, x, zl, my_rows], sibling)
            for h in range(2)
        ],
        abuf.at[pl.ds(0, 2), 0, 0, pl.ds(0, 32)],
    )
    acts_sib = send([(half(acts_hbm, 1 - c), acts_sv, sibling)], acts_sv)
    grads_sib = []
    for j in range(CHUNKS):
        piece = grads_v.at[1, :, pl.ds(CW * j, CW)]
        grads_sib.append(send([(grads_hbm.at[:, pl.ds(CW * j, CW)], piece, sibling)], piece))
    for copy in own:
        copy.start()

    own[0].wait()
    shifted[...] = jnp.zeros((8, 128), F32)
    shifted[0:1, 0:32] = aeig_ref[...]
    eigs = pltpu.roll(shifted[...], (dev % 4) * 32, 1)[0:1, :]
    high = eigs.astype(BF).astype(F32)
    middle = (eigs - high).astype(BF).astype(F32)
    parts[...] = jnp.zeros((16, 128), F32)
    parts[0:1, :] = high
    parts[1:2, :] = middle
    parts[2:3, :] = eigs - high - middle
    ebuf[x, zl, c, 0] = parts[...].astype(BF)
    for copy in own[1:3]:
        copy.wait()
    ez = gather(ebuf.at[x, zl, c], all_zl, ebuf.at[0, pl.ds(0, 3), 0])

    own[3].wait()
    mine = acts_v[:, pl.ds(pl.multiple_of(c * HALF, HALF), HALF)]
    for k in range(2):
        for t in range(2):
            actst[256 * k:256 * k + 256, 256 * t:256 * t + 256] = (
                mine[256 * t:256 * t + 256, 256 * k:256 * k + 256].T
            )

    def first(whole):
        return (
            gather(whole.at[2 * c, x, zl], all_zl, whole.at[0, 0, pl.ds(0, 3)]),
            gather(whole.at[2 * c + 1, x, zl], all_x, whole.at[0, 0, pl.ds(0, 3)]),
        )

    def near_x(whole):
        mine = whole.at[2 * c, x]
        return [send([(mine, mine, to_x(s))], mine) for s in (1, 3)]

    def near_z(whole):
        mine = whole.at[2 * c + 1, :, zl]
        return [send([(mine, mine, to_z(s))], mine) for s in (1, 7)]

    def onward(whole, over_x, over_z):
        out = []
        for block, target, copy in (
            (whole.at[2 * c, x_down, pl.ds(0, 2)], to_x(1), over_x[0]),
            (whole.at[2 * c, x_up, pl.ds(2, 2)], to_x(3), over_x[1]),
            (whole.at[2 * c + 1, pl.ds(0, 2), zl_down], to_z(1), over_z[0]),
            (whole.at[2 * c + 1, pl.ds(2, 2), zl_up], to_z(7), over_z[1]),
        ):
            copy.wait_recv()
            out.append(send([(block, block, target)], block))
        return out

    def third(whole, stage):
        for copy in stage:
            copy.wait_recv()
        mine = whole.at[pl.ds(2 * c, 2)]
        return gather(mine, [sibling], mine)

    for copy in own[4:]:
        copy.wait()
    basis_sib.wait_recv()
    a_first = first(abuf)

    def term(slot, j):
        part = dot(
            actst[:, slot * TOK:slot * TOK + TOK], grads_v[slot, :, CW * j:CW * j + CW]
        )
        return part.reshape(NX, 128, CW)

    for j in range(CHUNKS):
        tbuf[j] = term(0, j)
    acts_sib.wait_recv()
    for k in range(2):
        for t in range(2):
            actst[256 * k:256 * k + 256, TOK + 256 * t:TOK + 256 * t + 256] = (
                acts_sv[256 * t:256 * t + 256, 256 * k:256 * k + 256].T
            )

    def pick():
        row = lax.broadcasted_iota(jnp.int32, (16, TOK), 0)
        col = lax.broadcasted_iota(jnp.int32, (16, TOK), 1)
        wanted = jnp.where(row == 0, idx_ref[0, 0], jnp.where(row == 1, idx_ref[0, 1], -1))
        hot = jnp.where(col == wanted, 1.0, 0.0).astype(BF)
        for i, source in enumerate((acts_v[...], grads_v[0])):
            rows = dot(hot, source)
            for s in range(2):
                for k in range(8):
                    picks[i, s * 8 + k:s * 8 + k + 1, :] = rows[s:s + 1, 128 * k:128 * k + 128]
        pbuf[x, zl, c] = picks[...].astype(BF)
        return gather(pbuf.at[x, zl, c], all_zl, pbuf.at[0, pl.ds(0, 3), 0])

    r1, r2 = {}, {}

    def forward(j):
        r1[j][0].wait_recv()
        sendx2[j, 0] = (tbuf[j, x_up, 0:64, :] + recvx1[j, 0, 0].astype(F32)).astype(BF)
        up = send([(sendx2.at[j, 0], recvx2.at[j, 0], to_x(1))], recvx2.at[j, 0])
        r1[j][1].wait_recv()
        sendx2[j, 1] = (tbuf[j, x_down, 64:128, :] + recvx1[j, 1, 0].astype(F32)).astype(BF)
        down = send([(sendx2.at[j, 1], recvx2.at[j, 1], to_x(3))], recvx2.at[j, 1])
        r2[j] = (up, down)

    for j in range(CHUNKS):
        grads_sib[j].wait_recv()
        tbuf[j] = tbuf[j] + term(1, j)
        sendx1[j, 0, 0] = tbuf[j, x_far, 0:64, :].astype(BF)
        sendx1[j, 0, 1] = tbuf[j, x_up, 64:128, :].astype(BF)
        sendx1[j, 1, 0] = tbuf[j, x_far, 64:128, :].astype(BF)
        sendx1[j, 1, 1] = tbuf[j, x_down, 0:64, :].astype(BF)
        r1[j] = [
            send([(sendx1.at[j, i], recvx1.at[j, i], to_x(s))], recvx1.at[j, i])
            for i, s in enumerate((1, 3))
        ]
        if j == 2:
            a_first[1].wait_recv()
            a_over_z = near_z(abuf)
            pz = pick()
        if j > 1:
            forward(j - 2)
    forward(CHUNKS - 2)
    forward(CHUNKS - 1)
    ez.wait_recv()
    ex = gather(ebuf.at[x, :, c], all_x, ebuf.at[pl.ds(0, 3), :, 0])
    pz.wait_recv()
    px = gather(pbuf.at[x, :, c], all_x, pbuf.at[pl.ds(0, 3), :, 0])
    a_first[0].wait_recv()
    a_over_x = near_x(abuf)

    rz, ry = {}, {}

    def sum_x(j):
        r2[j][0].wait_recv()
        r2[j][1].wait_recv()
        top = tbuf[j, x, 0:64, :] + recvx1[j, 1, 1].astype(F32) + recvx2[j, 0].astype(F32)
        low = tbuf[j, x, 64:128, :] + recvx1[j, 0, 1].astype(F32) + recvx2[j, 1].astype(F32)
        sendz[j, 0:4] = top.astype(BF).reshape(4, 16, CW)
        sendz[j, 4:8] = low.astype(BF).reshape(4, 16, CW)
        rz[j] = send(
            [(sendz.at[j, (z + s) % NZ], recvz.at[j, i], to_z(s)) for i, s in enumerate(DZ)],
            recvz.at[j],
        )

    def sum_z(j):
        rz[j].wait_recv()
        total = sendz[j, z].astype(F32)
        for i in range(len(DZ)):
            total = total + recvz[j, i].astype(F32)
        sendy[j] = total.astype(BF)
        ry[j] = send(
            [(sendy.at[j], recvy.at[j, i], to_y(s)) for i, s in enumerate(DY)], recvy.at[j]
        )

    sum_x(0)
    sum_x(1)
    sum_z(0)
    sum_x(2)
    sum_z(1)
    sum_x(3)
    sum_z(2)
    ex.wait_recv()
    esib = gather(ebuf.at[:, :, c], [sibling], ebuf.at[:, :, c])
    sum_z(3)
    a_onward = onward(abuf, a_over_x, a_over_z)
    px.wait_recv()
    psib = gather(pbuf.at[:, :, c], [sibling], pbuf.at[:, :, c])

    esib.wait_recv()
    geig = column(geig_ref[...])
    for m in range(8):
        block = ebuf[m // 2, 2 * (m % 2):2 * (m % 2) + 2, :, 0].astype(F32)
        block = block[0, 0] + block[0, 1] + block[1, 0] + block[1, 1]
        eig_row = block[0:1] + block[1:2] + block[2:3]
        recip[:, 128 * m:128 * m + 128] = 1.0 / (geig * eig_row + 0.1)

    high_parts, low_parts = [], []
    for j in range(CHUNKS):
        ry[j].wait_recv()
        total = sendy[j].astype(F32)
        for i in range(len(DY)):
            total = total + recvy[j, i].astype(F32)
        high_parts.append(total.astype(BF))
        low_parts.append((total - total.astype(BF).astype(F32)).astype(BF))
    columns = ebuf[:, :, :, 1:3].reshape(D, 128)
    product = dot(
        jnp.concatenate(
            [jnp.concatenate(high_parts, axis=1), jnp.concatenate(low_parts, axis=1)], axis=0
        ),
        columns,
    )
    gbuf[c * NX + x, z] = (product[0:16] + product[16:32]).astype(BF)
    mine = gbuf.at[c * NX + x]
    gz = gather(mine.at[z], all_z, gbuf.at[0, pl.ds(0, 7)])

    psib.wait_recv()
    for i in range(2):
        pwide[...] = pbuf[:, :, :, i].reshape(2 * NX * ZL * 16, 128).astype(F32)
        for k in range(8):
            part = jnp.concatenate(
                [pwide[pl.ds(s * 8 + k, 2 * NX * ZL, stride=16), :] for s in range(2)], axis=0
            )
            xbuf[k] = part.astype(BF)
        wide = jnp.concatenate([xbuf[k] for k in range(8)], axis=1)
        sfull[...] = dot(xbuf[dev // 4], wide, (((0,), (0,)), ((), ())))
        rows = sfull[pl.ds(pl.multiple_of((dev % 4) * 32, 32), 32), :]
        for k in range(8):
            ssend[k, i] = rows[:, 128 * k:128 * k + 128].astype(BF)
    sy = send([(ssend.at[(y + s) % NY], srecv.at[i], to_y(s)) for i, s in enumerate(DY)], srecv)

    gz.wait_recv()
    gxc = gather(mine, all_xc, gbuf.at[pl.ds(0, 7)])
    a_third = third(abuf, a_onward)

    sy.wait_recv()
    stat = ssend[y].astype(F32)
    for i in range(len(DY)):
        stat = stat + srecv[i].astype(F32)
    szsend[...] = stat
    sz = send([(szsend, szrecv, to_z(4))], szrecv)

    gxc.wait_recv()
    turned = gbuf[...].reshape(D, 128).T
    a_third.wait_recv()
    total = jnp.zeros((32, 128), F32)
    for q in range(4):
        cols = slice(256 * q, 256 * q + 256)
        scaled = (dot(turned, abuf[q].reshape(D, 256)) * recip[:, cols]).astype(BF)
        total = total + dot(a_ref[:, cols], scaled, NT)
    high = total.astype(BF)
    low = (total - high.astype(F32)).astype(BF)
    partial = dot(jnp.concatenate([high, low], axis=0), columns, NT)
    partial = partial[0:32] + partial[32:64]
    for k in range(8):
        qsend[k] = partial[:, 128 * k:128 * k + 128].astype(BF)
    qr = send([(qsend.at[(y + s) % NY], qrecv.at[i], to_y(s)) for i, s in enumerate(DY)], qrecv)

    sz.wait_recv()
    sout[y] = (szsend[...] + szrecv[...]).astype(BF)
    so = gather(sout.at[y], all_y, sout.at[pl.ds(0, 7)])
    qr.wait_recv()
    total = qsend[y].astype(F32)
    for i in range(len(DY)):
        total = total + qrecv[i].astype(F32)
    qbuf[y] = total.astype(BF)
    qy = gather(qbuf.at[y], all_y, qbuf.at[pl.ds(0, 7)])
    drain()
    so.wait_recv()
    for i in range(2):
        for k in range(8):
            out_ref[1 + i, :, 128 * k:128 * k + 128] = sout[k, i]
    qy.wait_recv()
    for k in range(8):
        out_ref[0, :, 128 * k:128 * k + 128] = qbuf[k]


def finish(result_ref, old_act_ref, old_grad_ref, pre_ref, act_ref, grad_ref, *, act_scale, grad_scale):
    pre_ref[...] = result_ref[0].astype(F32)
    act_ref[...] = 0.75 * old_act_ref[...] + act_scale * result_ref[1].astype(F32)
    grad_ref[...] = 0.75 * old_grad_ref[...] + grad_scale * result_ref[2].astype(F32)


def local(
    acts,
    out_grads,
    old_act_factor,
    old_grad_factor,
    act_basis,
    grad_basis,
    act_eigs,
    grad_eigs,
    sample_index,
):
    vmem = pl.BlockSpec(memory_space=pltpu.VMEM)
    hbm = pl.BlockSpec(memory_space=pl.ANY)
    copies = 96
    result = pl.pallas_call(
        kernel,
        out_shape=jax.ShapeDtypeStruct((3, 32, D), BF),
        in_specs=[hbm] * 7,
        out_specs=vmem,
        scratch_shapes=[
            pltpu.SMEM((1, 2), jnp.int32),
            pltpu.VMEM((32, D), BF),
            pltpu.VMEM((1, 32), F32),
            pltpu.VMEM((1, 128), F32),
            pltpu.VMEM((TOK, D), BF),
            pltpu.VMEM((TOK, HALF), BF),
            pltpu.VMEM((2, TOK, D), BF),
            pltpu.VMEM((HALF, 2 * TOK), BF),
            pltpu.VMEM((4, NX, ZL, 64, 256), BF),
            pltpu.VMEM((CHUNKS, NX, 128, CW), F32),
            pltpu.VMEM((CHUNKS, 2, 2, 64, CW), BF),
            pltpu.VMEM((CHUNKS, 2, 2, 64, CW), BF),
            pltpu.VMEM((CHUNKS, 2, 64, CW), BF),
            pltpu.VMEM((CHUNKS, 2, 64, CW), BF),
            pltpu.VMEM((CHUNKS, NZ, 16, CW), BF),
            pltpu.VMEM((CHUNKS, 7, 16, CW), BF),
            pltpu.VMEM((CHUNKS, 16, CW), BF),
            pltpu.VMEM((CHUNKS, 7, 16, CW), BF),
            pltpu.VMEM((2 * NX, NZ, 16, 128), BF),
            pltpu.VMEM((128, D), F32),
            pltpu.VMEM((NY, 32, 128), BF),
            pltpu.VMEM((7, 32, 128), BF),
            pltpu.VMEM((NY, 32, 128), BF),
            pltpu.VMEM((8, 128), F32),
            pltpu.VMEM((16, 128), F32),
            pltpu.VMEM((NX, ZL, 2, 3, 16, 128), BF),
            pltpu.VMEM((2, 16, 128), F32),
            pltpu.VMEM((NX, ZL, 2, 2, 16, 128), BF),
            pltpu.VMEM((2 * NX * ZL * 16, 128), F32),
            pltpu.VMEM((8, 64, 128), BF),
            pltpu.VMEM((128, D), F32),
            pltpu.VMEM((NY, 2, 32, 128), BF),
            pltpu.VMEM((7, 2, 32, 128), BF),
            pltpu.VMEM((2, 32, 128), F32),
            pltpu.VMEM((2, 32, 128), F32),
            pltpu.VMEM((NY, 2, 32, 128), BF),
            pltpu.SemaphoreType.DMA((12,)),
            pltpu.SemaphoreType.DMA((copies,)),
            pltpu.SemaphoreType.DMA((copies,)),
        ],
        compiler_params=pltpu.CompilerParams(
            collective_id=0, has_side_effects=True, vmem_limit_bytes=63 * 1024 * 1024
        ),
        cost_estimate=pl.CostEstimate(
            flops=4 * TOK * D * D, bytes_accessed=4 * TOK * D, transcendentals=0
        ),
    )(
        sample_index.reshape(1, 2), acts, out_grads, act_basis, grad_basis,
        act_eigs.reshape(1, 32), grad_eigs.reshape(1, D),
    )
    device_count = lax.axis_size("grp") * lax.axis_size("dev")
    total_samples = device_count * sample_index.shape[0]
    total_tokens = device_count * acts.shape[0]
    return pl.pallas_call(
        functools.partial(
            finish,
            act_scale=0.25 / total_samples,
            grad_scale=0.25 * total_tokens / total_samples,
        ),
        out_shape=(jax.ShapeDtypeStruct((32, D), F32),) * 3,
        in_specs=[vmem] * 3,
        out_specs=(vmem,) * 3,
    )(result, old_act_factor, old_grad_factor)


def solution(mesh):
    return jax.shard_map(
        local,
        mesh=mesh,
        in_specs=(
            P(("grp", "dev"), None),
            P(("grp", "dev"), None),
            P("dev", None),
            P("dev", None),
            P("dev", None),
            P("dev", None),
            P("dev"),
            P(),
            P(("grp", "dev")),
        ),
        out_specs=(P("dev", None), P("dev", None), P("dev", None)),
        check_vma=False,
    )
```

```python
import functools

import jax
import jax.numpy as jnp
from jax import lax
from jax.experimental import pallas as pl
from jax.experimental.pallas import tpu as pltpu
from jax.sharding import PartitionSpec as P

NX, NY, NZ, ZL = 4, 8, 8, 4
D, TOK = 1024, 512
HALF = D // 2
CHUNKS, CW = 4, 256
BF, F32 = jnp.bfloat16, jnp.float32
DX = (2, 1, 3)
DY = (4, 3, 5, 2, 6, 1, 7)
DZ = (4, 3, 5, 2, 6, 1, 7)
DZL = (2, 1, 7)
DXC = tuple((dx, dc) for dx in (2, 1, 3, 0) for dc in (1, 0) if (dx, dc) != (0, 0))
NT = (((1,), (1,)), ((), ()))


def dot(left, right, dims=(((1,), (0,)), ((), ()))):
    return lax.dot_general(left, right, dims, preferred_element_type=F32)


def column(row):
    sub = lax.broadcasted_iota(jnp.int32, (128, 128), 0)
    lane = lax.broadcasted_iota(jnp.int32, (128, 128), 1)
    return jnp.sum(jnp.where(sub == lane, row, 0.0), axis=1, keepdims=True)


def kernel(
    idx_hbm, acts_hbm, grads_hbm, a_hbm, b_hbm, aeig_hbm, geig_hbm,
    out_ref,
    idx_ref, a_ref, aeig_ref, geig_ref,
    acts_v, acts_sv, grads_v, actst, abuf,
    tbuf, sendx1, recvx1, sendx2, recvx2, sendz, recvz, sendy, recvy,
    gbuf, recip, qsend, qrecv, qbuf,
    shifted, parts, ebuf, picks, pbuf, pwide, xbuf, sfull, ssend, srecv, szsend, szrecv, sout,
    lsem, ssem, rsem,
):
    grp, dev = lax.axis_index("grp"), lax.axis_index("dev")
    y, zh = grp // 2, grp % 2
    x, zl, c = dev // 8, (dev // 2) % 4, dev % 2
    z = zh * ZL + zl

    def at(px, py, pz, pc):
        return {"grp": py * 2 + pz // ZL, "dev": px * 8 + (pz % ZL) * 2 + pc}

    def to_x(step):
        return at((x + step) % NX, y, z, c)

    def to_y(step):
        return at(x, (y + step) % NY, z, c)

    def to_z(step):
        return at(x, y, (z + step) % NZ, c)

    def to_xc(step):
        return at((x + step[0]) % NX, y, z, (c + step[1]) % 2)

    sibling = at(x, y, z, 1 - c)

    counter = [0]
    pending = []

    def send(moves, like):
        n = counter[0]
        counter[0] += 1

        def copy(src, dst, target):
            return pltpu.make_async_remote_copy(
                src_ref=src, dst_ref=dst, send_sem=ssem.at[n], recv_sem=rsem.at[n],
                device_id=target, device_id_type=pl.DeviceIdType.MESH,
            )

        for move in moves:
            copy(*move).start()
        whole = copy(like, like, sibling)
        pending.append(whole)
        return whole

    def gather(ref, targets, like):
        return send([(ref, ref, target) for target in targets], like)

    def drain():
        for copy in pending:
            copy.wait_send()
        pending.clear()

    all_x = [to_x(s) for s in DX]
    all_y = [to_y(s) for s in DY]
    all_z = [to_z(s) for s in DZ]
    all_zl = [to_z(s) for s in DZL]
    all_xc = [to_xc(s) for s in DXC]
    x_up, x_down, x_far = (x + 1) % NX, (x + 3) % NX, (x + 2) % NX
    zl_up, zl_down = (zl + 1) % ZL, (zl + 3) % ZL

    my_rows = pl.ds(pl.multiple_of(c * 32, 32), 32)
    my_cols = pl.ds(pl.multiple_of(y * 128, 128), 128)

    def half(ref, side):
        return ref.at[:, pl.ds(pl.multiple_of(side * HALF, HALF), HALF)]

    def quarter(ref, side, h):
        return ref.at[:, pl.ds(pl.multiple_of(side * HALF + h * 256, 256), 256)]

    moves = [
        (aeig_hbm, aeig_ref),
        (b_hbm.at[pl.ds(0, 16), my_cols], ebuf.at[x, zl, c, 1]),
        (b_hbm.at[pl.ds(16, 16), my_cols], ebuf.at[x, zl, c, 2]),
        (acts_hbm, acts_v), (grads_hbm, grads_v.at[0]), (idx_hbm, idx_ref),
        (geig_hbm.at[:, my_cols], geig_ref), (a_hbm, a_ref),
    ]
    for h in range(2):
        moves.append((quarter(a_hbm, c, h), abuf.at[2 * c + h, x, zl, my_rows]))
    own = [pltpu.make_async_copy(src, dst, lsem.at[i]) for i, (src, dst) in enumerate(moves)]
    for copy in own[3:5]:
        copy.start()

    barrier = pltpu.get_barrier_semaphore()
    partners = all_xc + all_y + all_z
    for partner in partners:
        pl.semaphore_signal(
            barrier, inc=1, device_id=partner, device_id_type=pl.DeviceIdType.MESH
        )

    pl.semaphore_wait(barrier, len(partners))

    basis_sib = send(
        [
            (quarter(a_hbm, 1 - c, h), abuf.at[2 * (1 - c) + h, x, zl, my_rows], sibling)
            for h in range(2)
        ],
        abuf.at[pl.ds(0, 2), 0, 0, pl.ds(0, 32)],
    )
    acts_sib = send([(half(acts_hbm, 1 - c), acts_sv, sibling)], acts_sv)
    grads_sib = []
    for j in range(CHUNKS):
        piece = grads_v.at[1, :, pl.ds(CW * j, CW)]
        grads_sib.append(send([(grads_hbm.at[:, pl.ds(CW * j, CW)], piece, sibling)], piece))
    for copy in own[:3] + own[5:]:
        copy.start()

    own[3].wait()
    mine = acts_v[:, pl.ds(pl.multiple_of(c * HALF, HALF), HALF)]
    for k in range(2):
        for t in range(2):
            actst[256 * k:256 * k + 256, 256 * t:256 * t + 256] = (
                mine[256 * t:256 * t + 256, 256 * k:256 * k + 256].T
            )

    own[0].wait()
    shifted[...] = jnp.zeros((8, 128), F32)
    shifted[0:1, 0:32] = aeig_ref[...]
    eigs = pltpu.roll(shifted[...], (dev % 4) * 32, 1)[0:1, :]
    high = eigs.astype(BF).astype(F32)
    middle = (eigs - high).astype(BF).astype(F32)
    parts[...] = jnp.zeros((16, 128), F32)
    parts[0:1, :] = high
    parts[1:2, :] = middle
    parts[2:3, :] = eigs - high - middle
    ebuf[x, zl, c, 0] = parts[...].astype(BF)
    for copy in own[1:3]:
        copy.wait()
    ez = gather(ebuf.at[x, zl, c], all_zl, ebuf.at[0, pl.ds(0, 3), 0])

    def first(whole):
        return (
            gather(whole.at[2 * c, x, zl], all_zl, whole.at[0, 0, pl.ds(0, 3)]),
            gather(whole.at[2 * c + 1, x, zl], all_x, whole.at[0, 0, pl.ds(0, 3)]),
        )

    def near_x(whole):
        mine = whole.at[2 * c, x]
        return [send([(mine, mine, to_x(s))], mine) for s in (1, 3)]

    def near_z(whole):
        mine = whole.at[2 * c + 1, :, zl]
        return [send([(mine, mine, to_z(s))], mine) for s in (1, 7)]

    def onward(whole, over_x, over_z):
        out = []
        for block, target, copy in (
            (whole.at[2 * c, x_down, pl.ds(0, 2)], to_x(1), over_x[0]),
            (whole.at[2 * c, x_up, pl.ds(2, 2)], to_x(3), over_x[1]),
            (whole.at[2 * c + 1, pl.ds(0, 2), zl_down], to_z(1), over_z[0]),
            (whole.at[2 * c + 1, pl.ds(2, 2), zl_up], to_z(7), over_z[1]),
        ):
            copy.wait_recv()
            out.append(send([(block, block, target)], block))
        return out

    def third(whole, stage):
        for copy in stage:
            copy.wait_recv()
        mine = whole.at[pl.ds(2 * c, 2)]
        return gather(mine, [sibling], mine)

    for copy in own[4:]:
        copy.wait()
    basis_sib.wait_recv()
    a_first = first(abuf)

    def term(slot, j):
        part = dot(
            actst[:, slot * TOK:slot * TOK + TOK], grads_v[slot, :, CW * j:CW * j + CW]
        )
        return part.reshape(NX, 128, CW)

    for j in range(CHUNKS):
        tbuf[j] = term(0, j)
    acts_sib.wait_recv()
    for k in range(2):
        for t in range(2):
            actst[256 * k:256 * k + 256, TOK + 256 * t:TOK + 256 * t + 256] = (
                acts_sv[256 * t:256 * t + 256, 256 * k:256 * k + 256].T
            )

    def pick():
        row = lax.broadcasted_iota(jnp.int32, (16, TOK), 0)
        col = lax.broadcasted_iota(jnp.int32, (16, TOK), 1)
        wanted = jnp.where(row == 0, idx_ref[0, 0], jnp.where(row == 1, idx_ref[0, 1], -1))
        hot = jnp.where(col == wanted, 1.0, 0.0).astype(BF)
        for i, source in enumerate((acts_v[...], grads_v[0])):
            rows = dot(hot, source)
            for s in range(2):
                for k in range(8):
                    picks[i, s * 8 + k:s * 8 + k + 1, :] = rows[s:s + 1, 128 * k:128 * k + 128]
        pbuf[x, zl, c] = picks[...].astype(BF)
        return gather(pbuf.at[x, zl, c], all_zl, pbuf.at[0, pl.ds(0, 3), 0])

    r1, r2 = {}, {}

    def forward(j):
        r1[j][0].wait_recv()
        sendx2[j, 0] = (tbuf[j, x_up, 0:64, :] + recvx1[j, 0, 0].astype(F32)).astype(BF)
        up = send([(sendx2.at[j, 0], recvx2.at[j, 0], to_x(1))], recvx2.at[j, 0])
        r1[j][1].wait_recv()
        sendx2[j, 1] = (tbuf[j, x_down, 64:128, :] + recvx1[j, 1, 0].astype(F32)).astype(BF)
        down = send([(sendx2.at[j, 1], recvx2.at[j, 1], to_x(3))], recvx2.at[j, 1])
        r2[j] = (up, down)

    for j in range(CHUNKS):
        grads_sib[j].wait_recv()
        tbuf[j] = tbuf[j] + term(1, j)
        sendx1[j, 0, 0] = tbuf[j, x_far, 0:64, :].astype(BF)
        sendx1[j, 0, 1] = tbuf[j, x_up, 64:128, :].astype(BF)
        sendx1[j, 1, 0] = tbuf[j, x_far, 64:128, :].astype(BF)
        sendx1[j, 1, 1] = tbuf[j, x_down, 0:64, :].astype(BF)
        r1[j] = [
            send([(sendx1.at[j, i], recvx1.at[j, i], to_x(s))], recvx1.at[j, i])
            for i, s in enumerate((1, 3))
        ]
        if j == 2:
            a_first[1].wait_recv()
            a_over_z = near_z(abuf)
            pz = pick()
        if j > 1:
            forward(j - 2)
    forward(CHUNKS - 2)
    forward(CHUNKS - 1)
    ez.wait_recv()
    ex = gather(ebuf.at[x, :, c], all_x, ebuf.at[pl.ds(0, 3), :, 0])
    pz.wait_recv()
    px = gather(pbuf.at[x, :, c], all_x, pbuf.at[pl.ds(0, 3), :, 0])
    a_first[0].wait_recv()
    a_over_x = near_x(abuf)

    rz, ry = {}, {}

    def sum_x(j):
        r2[j][0].wait_recv()
        r2[j][1].wait_recv()
        top = tbuf[j, x, 0:64, :] + recvx1[j, 1, 1].astype(F32) + recvx2[j, 0].astype(F32)
        low = tbuf[j, x, 64:128, :] + recvx1[j, 0, 1].astype(F32) + recvx2[j, 1].astype(F32)
        sendz[j, 0:4] = top.astype(BF).reshape(4, 16, CW)
        sendz[j, 4:8] = low.astype(BF).reshape(4, 16, CW)
        rz[j] = send(
            [(sendz.at[j, (z + s) % NZ], recvz.at[j, i], to_z(s)) for i, s in enumerate(DZ)],
            recvz.at[j],
        )

    def sum_z(j):
        rz[j].wait_recv()
        total = sendz[j, z].astype(F32)
        for i in range(len(DZ)):
            total = total + recvz[j, i].astype(F32)
        sendy[j] = total.astype(BF)
        ry[j] = send(
            [(sendy.at[j], recvy.at[j, i], to_y(s)) for i, s in enumerate(DY)], recvy.at[j]
        )

    sum_x(0)
    sum_x(1)
    sum_z(0)
    sum_x(2)
    sum_z(1)
    sum_x(3)
    sum_z(2)
    ex.wait_recv()
    esib = gather(ebuf.at[:, :, c], [sibling], ebuf.at[:, :, c])
    px.wait_recv()
    psib = gather(pbuf.at[:, :, c], [sibling], pbuf.at[:, :, c])
    sum_z(3)
    a_onward = onward(abuf, a_over_x, a_over_z)
    esib.wait_recv()
    geig = column(geig_ref[...])
    for m in range(8):
        block = ebuf[m // 2, 2 * (m % 2):2 * (m % 2) + 2, :, 0].astype(F32)
        block = block[0, 0] + block[0, 1] + block[1, 0] + block[1, 1]
        eig_row = block[0:1] + block[1:2] + block[2:3]
        recip[:, 128 * m:128 * m + 128] = 1.0 / (geig * eig_row + 0.1)

    psib.wait_recv()
    for i in range(2):
        pwide[...] = pbuf[:, :, :, i].reshape(2 * NX * ZL * 16, 128).astype(F32)
        for k in range(8):
            part = jnp.concatenate(
                [pwide[pl.ds(s * 8 + k, 2 * NX * ZL, stride=16), :] for s in range(2)], axis=0
            )
            xbuf[k] = part.astype(BF)
        wide = jnp.concatenate([xbuf[k] for k in range(8)], axis=1)
        sfull[...] = dot(xbuf[dev // 4], wide, (((0,), (0,)), ((), ())))
        rows = sfull[pl.ds(pl.multiple_of((dev % 4) * 32, 32), 32), :]
        for k in range(8):
            ssend[k, i] = rows[:, 128 * k:128 * k + 128].astype(BF)
    sy = send([(ssend.at[(y + s) % NY], srecv.at[i], to_y(s)) for i, s in enumerate(DY)], srecv)

    high_parts, low_parts = [], []
    for j in range(CHUNKS):
        ry[j].wait_recv()
        total = sendy[j].astype(F32)
        for i in range(len(DY)):
            total = total + recvy[j, i].astype(F32)
        high_parts.append(total.astype(BF))
        low_parts.append((total - total.astype(BF).astype(F32)).astype(BF))
    columns = ebuf[:, :, :, 1:3].reshape(D, 128)
    product = dot(
        jnp.concatenate(
            [jnp.concatenate(high_parts, axis=1), jnp.concatenate(low_parts, axis=1)], axis=0
        ),
        columns,
    )
    gbuf[c * NX + x, z] = (product[0:16] + product[16:32]).astype(BF)
    mine = gbuf.at[c * NX + x]
    gz = gather(mine.at[z], all_z, gbuf.at[0, pl.ds(0, 7)])

    a_third = third(abuf, a_onward)

    sy.wait_recv()
    stat = ssend[y].astype(F32)
    for i in range(len(DY)):
        stat = stat + srecv[i].astype(F32)
    szsend[...] = stat
    sz = send([(szsend, szrecv, to_z(4))], szrecv)

    gz.wait_recv()
    gxc = gather(mine, all_xc, gbuf.at[pl.ds(0, 7)])

    sz.wait_recv()
    sout[y] = (szsend[...] + szrecv[...]).astype(BF)
    so = gather(sout.at[y], all_y, sout.at[pl.ds(0, 7)])

    gxc.wait_recv()
    turned = gbuf[...].reshape(D, 128).T
    a_third.wait_recv()
    total = jnp.zeros((32, 128), F32)
    for q in range(4):
        cols = slice(256 * q, 256 * q + 256)
        scaled = (dot(turned, abuf[q].reshape(D, 256)) * recip[:, cols]).astype(BF)
        total = total + dot(a_ref[:, cols], scaled, NT)
    high = total.astype(BF)
    low = (total - high.astype(F32)).astype(BF)
    partial = dot(jnp.concatenate([high, low], axis=0), columns, NT)
    partial = partial[0:32] + partial[32:64]
    for k in range(8):
        qsend[k] = partial[:, 128 * k:128 * k + 128].astype(BF)
    qr = send([(qsend.at[(y + s) % NY], qrecv.at[i], to_y(s)) for i, s in enumerate(DY)], qrecv)

    qr.wait_recv()
    total = qsend[y].astype(F32)
    for i in range(len(DY)):
        total = total + qrecv[i].astype(F32)
    qbuf[y] = total.astype(BF)
    qy = gather(qbuf.at[y], all_y, qbuf.at[pl.ds(0, 7)])
    drain()
    so.wait_recv()
    for i in range(2):
        for k in range(8):
            out_ref[1 + i, :, 128 * k:128 * k + 128] = sout[k, i]
    qy.wait_recv()
    for k in range(8):
        out_ref[0, :, 128 * k:128 * k + 128] = qbuf[k]


def finish(result_ref, old_act_ref, old_grad_ref, pre_ref, act_ref, grad_ref, *, act_scale, grad_scale):
    pre_ref[...] = result_ref[0].astype(F32)
    act_ref[...] = 0.75 * old_act_ref[...] + act_scale * result_ref[1].astype(F32)
    grad_ref[...] = 0.75 * old_grad_ref[...] + grad_scale * result_ref[2].astype(F32)


def local(
    acts,
    out_grads,
    old_act_factor,
    old_grad_factor,
    act_basis,
    grad_basis,
    act_eigs,
    grad_eigs,
    sample_index,
):
    vmem = pl.BlockSpec(memory_space=pltpu.VMEM)
    hbm = pl.BlockSpec(memory_space=pl.ANY)
    copies = 96
    result = pl.pallas_call(
        kernel,
        out_shape=jax.ShapeDtypeStruct((3, 32, D), BF),
        in_specs=[hbm] * 7,
        out_specs=vmem,
        scratch_shapes=[
            pltpu.SMEM((1, 2), jnp.int32),
            pltpu.VMEM((32, D), BF),
            pltpu.VMEM((1, 32), F32),
            pltpu.VMEM((1, 128), F32),
            pltpu.VMEM((TOK, D), BF),
            pltpu.VMEM((TOK, HALF), BF),
            pltpu.VMEM((2, TOK, D), BF),
            pltpu.VMEM((HALF, 2 * TOK), BF),
            pltpu.VMEM((4, NX, ZL, 64, 256), BF),
            pltpu.VMEM((CHUNKS, NX, 128, CW), F32),
            pltpu.VMEM((CHUNKS, 2, 2, 64, CW), BF),
            pltpu.VMEM((CHUNKS, 2, 2, 64, CW), BF),
            pltpu.VMEM((CHUNKS, 2, 64, CW), BF),
            pltpu.VMEM((CHUNKS, 2, 64, CW), BF),
            pltpu.VMEM((CHUNKS, NZ, 16, CW), BF),
            pltpu.VMEM((CHUNKS, 7, 16, CW), BF),
            pltpu.VMEM((CHUNKS, 16, CW), BF),
            pltpu.VMEM((CHUNKS, 7, 16, CW), BF),
            pltpu.VMEM((2 * NX, NZ, 16, 128), BF),
            pltpu.VMEM((128, D), F32),
            pltpu.VMEM((NY, 32, 128), BF),
            pltpu.VMEM((7, 32, 128), BF),
            pltpu.VMEM((NY, 32, 128), BF),
            pltpu.VMEM((8, 128), F32),
            pltpu.VMEM((16, 128), F32),
            pltpu.VMEM((NX, ZL, 2, 3, 16, 128), BF),
            pltpu.VMEM((2, 16, 128), F32),
            pltpu.VMEM((NX, ZL, 2, 2, 16, 128), BF),
            pltpu.VMEM((2 * NX * ZL * 16, 128), F32),
            pltpu.VMEM((8, 64, 128), BF),
            pltpu.VMEM((128, D), F32),
            pltpu.VMEM((NY, 2, 32, 128), BF),
            pltpu.VMEM((7, 2, 32, 128), BF),
            pltpu.VMEM((2, 32, 128), F32),
            pltpu.VMEM((2, 32, 128), F32),
            pltpu.VMEM((NY, 2, 32, 128), BF),
            pltpu.SemaphoreType.DMA((12,)),
            pltpu.SemaphoreType.DMA((copies,)),
            pltpu.SemaphoreType.DMA((copies,)),
        ],
        compiler_params=pltpu.CompilerParams(
            collective_id=0, has_side_effects=True, vmem_limit_bytes=63 * 1024 * 1024
        ),
        cost_estimate=pl.CostEstimate(
            flops=4 * TOK * D * D, bytes_accessed=4 * TOK * D, transcendentals=0
        ),
    )(
        sample_index.reshape(1, 2), acts, out_grads, act_basis, grad_basis,
        act_eigs.reshape(1, 32), grad_eigs.reshape(1, D),
    )
    device_count = lax.axis_size("grp") * lax.axis_size("dev")
    total_samples = device_count * sample_index.shape[0]
    total_tokens = device_count * acts.shape[0]
    return pl.pallas_call(
        functools.partial(
            finish,
            act_scale=0.25 / total_samples,
            grad_scale=0.25 * total_tokens / total_samples,
        ),
        out_shape=(jax.ShapeDtypeStruct((32, D), F32),) * 3,
        in_specs=[vmem] * 3,
        out_specs=(vmem,) * 3,
    )(result, old_act_factor, old_grad_factor)


def solution(mesh):
    return jax.shard_map(
        local,
        mesh=mesh,
        in_specs=(
            P(("grp", "dev"), None),
            P(("grp", "dev"), None),
            P("dev", None),
            P("dev", None),
            P("dev", None),
            P("dev", None),
            P("dev"),
            P(),
            P(("grp", "dev")),
        ),
        out_specs=(P("dev", None), P("dev", None), P("dev", None)),
        check_vma=False,
    )
```

```python
import functools

import jax
import jax.numpy as jnp
from jax import lax
from jax.experimental import pallas as pl
from jax.experimental.pallas import tpu as pltpu
from jax.sharding import PartitionSpec as P

NX, NY, NZ, ZL = 4, 8, 8, 4
D, TOK = 1024, 512
HALF = D // 2
CHUNKS, CW = 2, 512
BF, F32 = jnp.bfloat16, jnp.float32
DX = (2, 1, 3)
DY = (4, 3, 5, 2, 6, 1, 7)
DZ = (4, 3, 5, 2, 6, 1, 7)
DZL = (2, 1, 7)
DXC = tuple((dx, dc) for dx in (2, 1, 3, 0) for dc in (1, 0) if (dx, dc) != (0, 0))
NT = (((1,), (1,)), ((), ()))


def dot(left, right, dims=(((1,), (0,)), ((), ()))):
    return lax.dot_general(left, right, dims, preferred_element_type=F32)


def column(row):
    sub = lax.broadcasted_iota(jnp.int32, (128, 128), 0)
    lane = lax.broadcasted_iota(jnp.int32, (128, 128), 1)
    return jnp.sum(jnp.where(sub == lane, row, 0.0), axis=1, keepdims=True)


def kernel(
    idx_hbm, acts_hbm, grads_hbm, a_hbm, b_hbm, aeig_hbm, geig_hbm,
    out_ref,
    idx_ref, a_ref, aeig_ref, geig_ref,
    acts_v, acts_sv, grads_v, actst, abuf,
    tbuf, sendx1, recvx1, sendx2, recvx2, sendz, recvz, sendy, recvy,
    gbuf, recip, qsend, qrecv, qbuf,
    shifted, parts, ebuf, picks, pbuf, pwide, xbuf, sfull, ssend, srecv, szsend, szrecv, sout,
    lsem, ssem, rsem,
):
    grp, dev = lax.axis_index("grp"), lax.axis_index("dev")
    y, zh = grp // 2, grp % 2
    x, zl, c = dev // 8, (dev // 2) % 4, dev % 2
    z = zh * ZL + zl

    def at(px, py, pz, pc):
        return {"grp": py * 2 + pz // ZL, "dev": px * 8 + (pz % ZL) * 2 + pc}

    def to_x(step):
        return at((x + step) % NX, y, z, c)

    def to_y(step):
        return at(x, (y + step) % NY, z, c)

    def to_z(step):
        return at(x, y, (z + step) % NZ, c)

    def to_xc(step):
        return at((x + step[0]) % NX, y, z, (c + step[1]) % 2)

    sibling = at(x, y, z, 1 - c)

    counter = [0]
    pending = []

    def send(moves, like):
        n = counter[0]
        counter[0] += 1

        def copy(src, dst, target):
            return pltpu.make_async_remote_copy(
                src_ref=src, dst_ref=dst, send_sem=ssem.at[n], recv_sem=rsem.at[n],
                device_id=target, device_id_type=pl.DeviceIdType.MESH,
            )

        for move in moves:
            copy(*move).start()
        whole = copy(like, like, sibling)
        pending.append(whole)
        return whole

    def gather(ref, targets, like):
        return send([(ref, ref, target) for target in targets], like)

    def drain():
        for copy in pending:
            copy.wait_send()
        pending.clear()

    all_x = [to_x(s) for s in DX]
    all_y = [to_y(s) for s in DY]
    all_z = [to_z(s) for s in DZ]
    all_zl = [to_z(s) for s in DZL]
    all_xc = [to_xc(s) for s in DXC]
    x_up, x_down, x_far = (x + 1) % NX, (x + 3) % NX, (x + 2) % NX
    zl_up, zl_down = (zl + 1) % ZL, (zl + 3) % ZL

    my_rows = pl.ds(pl.multiple_of(c * 32, 32), 32)
    my_cols = pl.ds(pl.multiple_of(y * 128, 128), 128)

    def half(ref, side):
        return ref.at[:, pl.ds(pl.multiple_of(side * HALF, HALF), HALF)]

    def quarter(ref, side, h):
        return ref.at[:, pl.ds(pl.multiple_of(side * HALF + h * 256, 256), 256)]

    moves = [
        (aeig_hbm, aeig_ref),
        (b_hbm.at[pl.ds(0, 16), my_cols], ebuf.at[x, zl, c, 1]),
        (b_hbm.at[pl.ds(16, 16), my_cols], ebuf.at[x, zl, c, 2]),
        (acts_hbm, acts_v), (grads_hbm, grads_v.at[0]), (idx_hbm, idx_ref),
        (geig_hbm.at[:, my_cols], geig_ref), (a_hbm, a_ref),
    ]
    for h in range(2):
        moves.append((quarter(a_hbm, c, h), abuf.at[2 * c + h, x, zl, my_rows]))
    own = [pltpu.make_async_copy(src, dst, lsem.at[i]) for i, (src, dst) in enumerate(moves)]
    for copy in own[3:5]:
        copy.start()

    barrier = pltpu.get_barrier_semaphore()
    partners = all_xc + all_y + all_z
    for partner in partners:
        pl.semaphore_signal(
            barrier, inc=1, device_id=partner, device_id_type=pl.DeviceIdType.MESH
        )

    pl.semaphore_wait(barrier, len(partners))

    basis_sib = send(
        [
            (quarter(a_hbm, 1 - c, h), abuf.at[2 * (1 - c) + h, x, zl, my_rows], sibling)
            for h in range(2)
        ],
        abuf.at[pl.ds(0, 2), 0, 0, pl.ds(0, 32)],
    )
    acts_sib = send([(half(acts_hbm, 1 - c), acts_sv, sibling)], acts_sv)
    grads_sib = []
    for j in range(CHUNKS):
        piece = grads_v.at[1, :, pl.ds(CW * j, CW)]
        grads_sib.append(send([(grads_hbm.at[:, pl.ds(CW * j, CW)], piece, sibling)], piece))
    for copy in own[:3] + own[5:]:
        copy.start()

    own[3].wait()
    mine = acts_v[:, pl.ds(pl.multiple_of(c * HALF, HALF), HALF)]
    for k in range(2):
        for t in range(2):
            actst[256 * k:256 * k + 256, 256 * t:256 * t + 256] = (
                mine[256 * t:256 * t + 256, 256 * k:256 * k + 256].T
            )

    own[0].wait()
    shifted[...] = jnp.zeros((8, 128), F32)
    shifted[0:1, 0:32] = aeig_ref[...]
    eigs = pltpu.roll(shifted[...], (dev % 4) * 32, 1)[0:1, :]
    high = eigs.astype(BF).astype(F32)
    middle = (eigs - high).astype(BF).astype(F32)
    parts[...] = jnp.zeros((16, 128), F32)
    parts[0:1, :] = high
    parts[1:2, :] = middle
    parts[2:3, :] = eigs - high - middle
    ebuf[x, zl, c, 0] = parts[...].astype(BF)
    for copy in own[1:3]:
        copy.wait()
    ez = gather(ebuf.at[x, zl, c], all_zl, ebuf.at[0, pl.ds(0, 3), 0])

    def first(whole):
        return (
            gather(whole.at[2 * c, x, zl], all_zl, whole.at[0, 0, pl.ds(0, 3)]),
            gather(whole.at[2 * c + 1, x, zl], all_x, whole.at[0, 0, pl.ds(0, 3)]),
        )

    def near_x(whole):
        mine = whole.at[2 * c, x]
        return [send([(mine, mine, to_x(s))], mine) for s in (1, 3)]

    def near_z(whole):
        mine = whole.at[2 * c + 1, :, zl]
        return [send([(mine, mine, to_z(s))], mine) for s in (1, 7)]

    def onward(whole, over_x, over_z):
        out = []
        for block, target, copy in (
            (whole.at[2 * c, x_down, pl.ds(0, 2)], to_x(1), over_x[0]),
            (whole.at[2 * c, x_up, pl.ds(2, 2)], to_x(3), over_x[1]),
            (whole.at[2 * c + 1, pl.ds(0, 2), zl_down], to_z(1), over_z[0]),
            (whole.at[2 * c + 1, pl.ds(2, 2), zl_up], to_z(7), over_z[1]),
        ):
            copy.wait_recv()
            out.append(send([(block, block, target)], block))
        return out

    def third(whole, stage):
        for copy in stage:
            copy.wait_recv()
        mine = whole.at[pl.ds(2 * c, 2)]
        return gather(mine, [sibling], mine)

    for copy in own[4:]:
        copy.wait()
    basis_sib.wait_recv()
    a_first = first(abuf)

    def term(slot, j):
        part = dot(
            actst[:, slot * TOK:slot * TOK + TOK], grads_v[slot, :, CW * j:CW * j + CW]
        )
        return part.reshape(NX, 128, CW)

    for j in range(CHUNKS):
        tbuf[j] = term(0, j)
    acts_sib.wait_recv()
    for k in range(2):
        for t in range(2):
            actst[256 * k:256 * k + 256, TOK + 256 * t:TOK + 256 * t + 256] = (
                acts_sv[256 * t:256 * t + 256, 256 * k:256 * k + 256].T
            )

    def pick():
        row = lax.broadcasted_iota(jnp.int32, (16, TOK), 0)
        col = lax.broadcasted_iota(jnp.int32, (16, TOK), 1)
        wanted = jnp.where(row == 0, idx_ref[0, 0], jnp.where(row == 1, idx_ref[0, 1], -1))
        hot = jnp.where(col == wanted, 1.0, 0.0).astype(BF)
        for i, source in enumerate((acts_v[...], grads_v[0])):
            rows = dot(hot, source)
            for s in range(2):
                for k in range(8):
                    picks[i, s * 8 + k:s * 8 + k + 1, :] = rows[s:s + 1, 128 * k:128 * k + 128]
        pbuf[x, zl, c] = picks[...].astype(BF)
        return gather(pbuf.at[x, zl, c], all_zl, pbuf.at[0, pl.ds(0, 3), 0])

    r1, r2 = {}, {}

    def forward(j):
        r1[j][0].wait_recv()
        sendx2[j, 0] = (tbuf[j, x_up, 0:64, :] + recvx1[j, 0, 0].astype(F32)).astype(BF)
        up = send([(sendx2.at[j, 0], recvx2.at[j, 0], to_x(1))], recvx2.at[j, 0])
        r1[j][1].wait_recv()
        sendx2[j, 1] = (tbuf[j, x_down, 64:128, :] + recvx1[j, 1, 0].astype(F32)).astype(BF)
        down = send([(sendx2.at[j, 1], recvx2.at[j, 1], to_x(3))], recvx2.at[j, 1])
        r2[j] = (up, down)

    for j in range(CHUNKS):
        grads_sib[j].wait_recv()
        tbuf[j] = tbuf[j] + term(1, j)
        sendx1[j, 0, 0] = tbuf[j, x_far, 0:64, :].astype(BF)
        sendx1[j, 0, 1] = tbuf[j, x_up, 64:128, :].astype(BF)
        sendx1[j, 1, 0] = tbuf[j, x_far, 64:128, :].astype(BF)
        sendx1[j, 1, 1] = tbuf[j, x_down, 0:64, :].astype(BF)
        r1[j] = [
            send([(sendx1.at[j, i], recvx1.at[j, i], to_x(s))], recvx1.at[j, i])
            for i, s in enumerate((1, 3))
        ]
    a_first[1].wait_recv()
    a_over_z = near_z(abuf)
    pz = pick()
    for j in range(CHUNKS):
        forward(j)
    ez.wait_recv()
    ex = gather(ebuf.at[x, :, c], all_x, ebuf.at[pl.ds(0, 3), :, 0])
    pz.wait_recv()
    px = gather(pbuf.at[x, :, c], all_x, pbuf.at[pl.ds(0, 3), :, 0])
    a_first[0].wait_recv()
    a_over_x = near_x(abuf)

    rz, ry = {}, {}

    def sum_x(j):
        r2[j][0].wait_recv()
        r2[j][1].wait_recv()
        top = tbuf[j, x, 0:64, :] + recvx1[j, 1, 1].astype(F32) + recvx2[j, 0].astype(F32)
        low = tbuf[j, x, 64:128, :] + recvx1[j, 0, 1].astype(F32) + recvx2[j, 1].astype(F32)
        sendz[j, 0:4] = top.astype(BF).reshape(4, 16, CW)
        sendz[j, 4:8] = low.astype(BF).reshape(4, 16, CW)
        rz[j] = send(
            [(sendz.at[j, (z + s) % NZ], recvz.at[j, i], to_z(s)) for i, s in enumerate(DZ)],
            recvz.at[j],
        )

    def sum_z(j):
        rz[j].wait_recv()
        total = sendz[j, z].astype(F32)
        for i in range(len(DZ)):
            total = total + recvz[j, i].astype(F32)
        sendy[j] = total.astype(BF)
        ry[j] = send(
            [(sendy.at[j], recvy.at[j, i], to_y(s)) for i, s in enumerate(DY)], recvy.at[j]
        )

    sum_x(0)
    sum_x(1)
    sum_z(0)
    ex.wait_recv()
    esib = gather(ebuf.at[:, :, c], [sibling], ebuf.at[:, :, c])
    px.wait_recv()
    psib = gather(pbuf.at[:, :, c], [sibling], pbuf.at[:, :, c])
    sum_z(1)
    a_onward = onward(abuf, a_over_x, a_over_z)
    esib.wait_recv()
    geig = column(geig_ref[...])
    for m in range(8):
        block = ebuf[m // 2, 2 * (m % 2):2 * (m % 2) + 2, :, 0].astype(F32)
        block = block[0, 0] + block[0, 1] + block[1, 0] + block[1, 1]
        eig_row = block[0:1] + block[1:2] + block[2:3]
        recip[:, 128 * m:128 * m + 128] = 1.0 / (geig * eig_row + 0.1)

    psib.wait_recv()
    for i in range(2):
        pwide[...] = pbuf[:, :, :, i].reshape(2 * NX * ZL * 16, 128).astype(F32)
        for k in range(8):
            part = jnp.concatenate(
                [pwide[pl.ds(s * 8 + k, 2 * NX * ZL, stride=16), :] for s in range(2)], axis=0
            )
            xbuf[k] = part.astype(BF)
        wide = jnp.concatenate([xbuf[k] for k in range(8)], axis=1)
        sfull[...] = dot(xbuf[dev // 4], wide, (((0,), (0,)), ((), ())))
        rows = sfull[pl.ds(pl.multiple_of((dev % 4) * 32, 32), 32), :]
        for k in range(8):
            ssend[k, i] = rows[:, 128 * k:128 * k + 128].astype(BF)
    sy = send([(ssend.at[(y + s) % NY], srecv.at[i], to_y(s)) for i, s in enumerate(DY)], srecv)

    high_parts, low_parts = [], []
    for j in range(CHUNKS):
        ry[j].wait_recv()
        total = sendy[j].astype(F32)
        for i in range(len(DY)):
            total = total + recvy[j, i].astype(F32)
        high_parts.append(total.astype(BF))
        low_parts.append((total - total.astype(BF).astype(F32)).astype(BF))
    columns = ebuf[:, :, :, 1:3].reshape(D, 128)
    product = dot(
        jnp.concatenate(
            [jnp.concatenate(high_parts, axis=1), jnp.concatenate(low_parts, axis=1)], axis=0
        ),
        columns,
    )
    gbuf[c * NX + x, z] = (product[0:16] + product[16:32]).astype(BF)
    mine = gbuf.at[c * NX + x]
    gz = gather(mine.at[z], all_z, gbuf.at[0, pl.ds(0, 7)])

    a_third = third(abuf, a_onward)

    sy.wait_recv()
    stat = ssend[y].astype(F32)
    for i in range(len(DY)):
        stat = stat + srecv[i].astype(F32)
    szsend[...] = stat
    sz = send([(szsend, szrecv, to_z(4))], szrecv)

    gz.wait_recv()
    gxc = gather(mine, all_xc, gbuf.at[pl.ds(0, 7)])

    sz.wait_recv()
    sout[y] = (szsend[...] + szrecv[...]).astype(BF)
    so = gather(sout.at[y], all_y, sout.at[pl.ds(0, 7)])

    gxc.wait_recv()
    turned = gbuf[...].reshape(D, 128).T
    a_third.wait_recv()
    total = jnp.zeros((32, 128), F32)
    for q in range(4):
        cols = slice(256 * q, 256 * q + 256)
        scaled = (dot(turned, abuf[q].reshape(D, 256)) * recip[:, cols]).astype(BF)
        total = total + dot(a_ref[:, cols], scaled, NT)
    high = total.astype(BF)
    low = (total - high.astype(F32)).astype(BF)
    partial = dot(jnp.concatenate([high, low], axis=0), columns, NT)
    partial = partial[0:32] + partial[32:64]
    for k in range(8):
        qsend[k] = partial[:, 128 * k:128 * k + 128].astype(BF)
    qr = send([(qsend.at[(y + s) % NY], qrecv.at[i], to_y(s)) for i, s in enumerate(DY)], qrecv)

    qr.wait_recv()
    total = qsend[y].astype(F32)
    for i in range(len(DY)):
        total = total + qrecv[i].astype(F32)
    qbuf[y] = total.astype(BF)
    qy = gather(qbuf.at[y], all_y, qbuf.at[pl.ds(0, 7)])
    drain()
    so.wait_recv()
    for i in range(2):
        for k in range(8):
            out_ref[1 + i, :, 128 * k:128 * k + 128] = sout[k, i]
    qy.wait_recv()
    for k in range(8):
        out_ref[0, :, 128 * k:128 * k + 128] = qbuf[k]


def finish(result_ref, old_act_ref, old_grad_ref, pre_ref, act_ref, grad_ref, *, act_scale, grad_scale):
    pre_ref[...] = result_ref[0].astype(F32)
    act_ref[...] = 0.75 * old_act_ref[...] + act_scale * result_ref[1].astype(F32)
    grad_ref[...] = 0.75 * old_grad_ref[...] + grad_scale * result_ref[2].astype(F32)


def local(
    acts,
    out_grads,
    old_act_factor,
    old_grad_factor,
    act_basis,
    grad_basis,
    act_eigs,
    grad_eigs,
    sample_index,
):
    vmem = pl.BlockSpec(memory_space=pltpu.VMEM)
    hbm = pl.BlockSpec(memory_space=pl.ANY)
    copies = 96
    result = pl.pallas_call(
        kernel,
        out_shape=jax.ShapeDtypeStruct((3, 32, D), BF),
        in_specs=[hbm] * 7,
        out_specs=vmem,
        scratch_shapes=[
            pltpu.SMEM((1, 2), jnp.int32),
            pltpu.VMEM((32, D), BF),
            pltpu.VMEM((1, 32), F32),
            pltpu.VMEM((1, 128), F32),
            pltpu.VMEM((TOK, D), BF),
            pltpu.VMEM((TOK, HALF), BF),
            pltpu.VMEM((2, TOK, D), BF),
            pltpu.VMEM((HALF, 2 * TOK), BF),
            pltpu.VMEM((4, NX, ZL, 64, 256), BF),
            pltpu.VMEM((CHUNKS, NX, 128, CW), F32),
            pltpu.VMEM((CHUNKS, 2, 2, 64, CW), BF),
            pltpu.VMEM((CHUNKS, 2, 2, 64, CW), BF),
            pltpu.VMEM((CHUNKS, 2, 64, CW), BF),
            pltpu.VMEM((CHUNKS, 2, 64, CW), BF),
            pltpu.VMEM((CHUNKS, NZ, 16, CW), BF),
            pltpu.VMEM((CHUNKS, 7, 16, CW), BF),
            pltpu.VMEM((CHUNKS, 16, CW), BF),
            pltpu.VMEM((CHUNKS, 7, 16, CW), BF),
            pltpu.VMEM((2 * NX, NZ, 16, 128), BF),
            pltpu.VMEM((128, D), F32),
            pltpu.VMEM((NY, 32, 128), BF),
            pltpu.VMEM((7, 32, 128), BF),
            pltpu.VMEM((NY, 32, 128), BF),
            pltpu.VMEM((8, 128), F32),
            pltpu.VMEM((16, 128), F32),
            pltpu.VMEM((NX, ZL, 2, 3, 16, 128), BF),
            pltpu.VMEM((2, 16, 128), F32),
            pltpu.VMEM((NX, ZL, 2, 2, 16, 128), BF),
            pltpu.VMEM((2 * NX * ZL * 16, 128), F32),
            pltpu.VMEM((8, 64, 128), BF),
            pltpu.VMEM((128, D), F32),
            pltpu.VMEM((NY, 2, 32, 128), BF),
            pltpu.VMEM((7, 2, 32, 128), BF),
            pltpu.VMEM((2, 32, 128), F32),
            pltpu.VMEM((2, 32, 128), F32),
            pltpu.VMEM((NY, 2, 32, 128), BF),
            pltpu.SemaphoreType.DMA((12,)),
            pltpu.SemaphoreType.DMA((copies,)),
            pltpu.SemaphoreType.DMA((copies,)),
        ],
        compiler_params=pltpu.CompilerParams(
            collective_id=0, has_side_effects=True, vmem_limit_bytes=63 * 1024 * 1024
        ),
        cost_estimate=pl.CostEstimate(
            flops=4 * TOK * D * D, bytes_accessed=4 * TOK * D, transcendentals=0
        ),
    )(
        sample_index.reshape(1, 2), acts, out_grads, act_basis, grad_basis,
        act_eigs.reshape(1, 32), grad_eigs.reshape(1, D),
    )
    device_count = lax.axis_size("grp") * lax.axis_size("dev")
    total_samples = device_count * sample_index.shape[0]
    total_tokens = device_count * acts.shape[0]
    return pl.pallas_call(
        functools.partial(
            finish,
            act_scale=0.25 / total_samples,
            grad_scale=0.25 * total_tokens / total_samples,
        ),
        out_shape=(jax.ShapeDtypeStruct((32, D), F32),) * 3,
        in_specs=[vmem] * 3,
        out_specs=(vmem,) * 3,
    )(result, old_act_factor, old_grad_factor)


def solution(mesh):
    return jax.shard_map(
        local,
        mesh=mesh,
        in_specs=(
            P(("grp", "dev"), None),
            P(("grp", "dev"), None),
            P("dev", None),
            P("dev", None),
            P("dev", None),
            P("dev", None),
            P("dev"),
            P(),
            P(("grp", "dev")),
        ),
        out_specs=(P("dev", None), P("dev", None), P("dev", None)),
        check_vma=False,
    )
```

```python
import functools

import jax
import jax.numpy as jnp
from jax import lax
from jax.experimental import pallas as pl
from jax.experimental.pallas import tpu as pltpu
from jax.sharding import PartitionSpec as P

NX, NY, NZ, ZL = 4, 8, 8, 4
D, TOK = 1024, 512
HALF = D // 2
CHUNKS, CW = 4, 256
BF, F32 = jnp.bfloat16, jnp.float32
DX = (2, 1, 3)
DY = (4, 3, 5, 2, 6, 1, 7)
DZ = (4, 3, 5, 2, 6, 1, 7)
DZL = (2, 1, 7)
DXC = tuple((dx, dc) for dx in (2, 1, 3, 0) for dc in (1, 0) if (dx, dc) != (0, 0))
NT = (((1,), (1,)), ((), ()))


def dot(left, right, dims=(((1,), (0,)), ((), ()))):
    return lax.dot_general(left, right, dims, preferred_element_type=F32)


def column(row):
    sub = lax.broadcasted_iota(jnp.int32, (128, 128), 0)
    lane = lax.broadcasted_iota(jnp.int32, (128, 128), 1)
    return jnp.sum(jnp.where(sub == lane, row, 0.0), axis=1, keepdims=True)


def kernel(
    idx_hbm, acts_hbm, grads_hbm, a_hbm, b_hbm, aeig_hbm, geig_hbm,
    out_ref,
    idx_ref, a_ref, aeig_ref, geig_ref,
    acts_v, grads_v, actst, sendc, recvc, abuf,
    tbuf, sendx1, recvx1, sendx2, recvx2, sendz, recvz, sendy, recvy,
    gbuf, recip, qsend, qrecv, qbuf,
    shifted, parts, ebuf, picks, pbuf, pwide, xbuf, sfull, ssend, srecv, szsend, szrecv, sout,
    lsem, ssem, rsem,
):
    grp, dev = lax.axis_index("grp"), lax.axis_index("dev")
    y, zh = grp // 2, grp % 2
    x, zl, c = dev // 8, (dev // 2) % 4, dev % 2
    z = zh * ZL + zl

    def at(px, py, pz, pc):
        return {"grp": py * 2 + pz // ZL, "dev": px * 8 + (pz % ZL) * 2 + pc}

    def to_x(step):
        return at((x + step) % NX, y, z, c)

    def to_y(step):
        return at(x, (y + step) % NY, z, c)

    def to_z(step):
        return at(x, y, (z + step) % NZ, c)

    def to_xc(step):
        return at((x + step[0]) % NX, y, z, (c + step[1]) % 2)

    sibling = at(x, y, z, 1 - c)

    counter = [0]
    pending = []

    def send(moves, like):
        n = counter[0]
        counter[0] += 1

        def copy(src, dst, target):
            return pltpu.make_async_remote_copy(
                src_ref=src, dst_ref=dst, send_sem=ssem.at[n], recv_sem=rsem.at[n],
                device_id=target, device_id_type=pl.DeviceIdType.MESH,
            )

        for move in moves:
            copy(*move).start()
        whole = copy(like, like, sibling)
        pending.append(whole)
        return whole

    def gather(ref, targets, like):
        return send([(ref, ref, target) for target in targets], like)

    def drain():
        for copy in pending:
            copy.wait_send()
        pending.clear()

    all_x = [to_x(s) for s in DX]
    all_y = [to_y(s) for s in DY]
    all_z = [to_z(s) for s in DZ]
    all_zl = [to_z(s) for s in DZL]
    all_xc = [to_xc(s) for s in DXC]
    x_up, x_down, x_far = (x + 1) % NX, (x + 3) % NX, (x + 2) % NX
    zl_up, zl_down = (zl + 1) % ZL, (zl + 3) % ZL

    my_rows = pl.ds(pl.multiple_of(c * 32, 32), 32)
    my_cols = pl.ds(pl.multiple_of(y * 128, 128), 128)

    def quarter(ref, side, h):
        return ref.at[:, pl.ds(pl.multiple_of(side * HALF + h * 256, 256), 256)]

    moves = [
        (aeig_hbm, aeig_ref),
        (b_hbm.at[pl.ds(0, 16), my_cols], ebuf.at[x, zl, c, 1]),
        (b_hbm.at[pl.ds(16, 16), my_cols], ebuf.at[x, zl, c, 2]),
        (acts_hbm, acts_v), (grads_hbm, grads_v), (idx_hbm, idx_ref),
        (geig_hbm.at[:, my_cols], geig_ref), (a_hbm, a_ref),
    ]
    for h in range(2):
        moves.append((quarter(a_hbm, c, h), abuf.at[2 * c + h, x, zl, my_rows]))
    own = [pltpu.make_async_copy(src, dst, lsem.at[i]) for i, (src, dst) in enumerate(moves)]
    for copy in own[3:5]:
        copy.start()

    barrier = pltpu.get_barrier_semaphore()
    partners = all_xc + all_y + all_z
    for partner in partners:
        pl.semaphore_signal(
            barrier, inc=1, device_id=partner, device_id_type=pl.DeviceIdType.MESH
        )

    for copy in own[:3] + own[5:]:
        copy.start()

    def turn(side):
        mine = acts_v[:, pl.ds(pl.multiple_of(side * HALF, HALF), HALF)]
        for k in range(2):
            for t in range(2):
                actst[256 * k:256 * k + 256, 256 * t:256 * t + 256] = (
                    mine[256 * t:256 * t + 256, 256 * k:256 * k + 256].T
                )

    def term(j):
        return dot(actst[...], grads_v[:, CW * j:CW * j + CW])

    own[3].wait()
    turn(1 - c)
    own[4].wait()

    pl.semaphore_wait(barrier, len(partners))

    basis_sib = send(
        [
            (quarter(a_hbm, 1 - c, h), abuf.at[2 * (1 - c) + h, x, zl, my_rows], sibling)
            for h in range(2)
        ],
        abuf.at[pl.ds(0, 2), 0, 0, pl.ds(0, 32)],
    )
    rc = []
    for j in range(CHUNKS):
        sendc[j] = term(j).astype(BF)
        rc.append(send([(sendc.at[j], recvc.at[j], sibling)], recvc.at[j]))
    turn(c)

    own[0].wait()
    shifted[...] = jnp.zeros((8, 128), F32)
    shifted[0:1, 0:32] = aeig_ref[...]
    eigs = pltpu.roll(shifted[...], (dev % 4) * 32, 1)[0:1, :]
    high = eigs.astype(BF).astype(F32)
    middle = (eigs - high).astype(BF).astype(F32)
    parts[...] = jnp.zeros((16, 128), F32)
    parts[0:1, :] = high
    parts[1:2, :] = middle
    parts[2:3, :] = eigs - high - middle
    ebuf[x, zl, c, 0] = parts[...].astype(BF)
    for copy in own[1:3]:
        copy.wait()
    ez = gather(ebuf.at[x, zl, c], all_zl, ebuf.at[0, pl.ds(0, 3), 0])

    def first(whole):
        return (
            gather(whole.at[2 * c, x, zl], all_zl, whole.at[0, 0, pl.ds(0, 3)]),
            gather(whole.at[2 * c + 1, x, zl], all_x, whole.at[0, 0, pl.ds(0, 3)]),
        )

    def near_x(whole):
        mine = whole.at[2 * c, x]
        return [send([(mine, mine, to_x(s))], mine) for s in (1, 3)]

    def near_z(whole):
        mine = whole.at[2 * c + 1, :, zl]
        return [send([(mine, mine, to_z(s))], mine) for s in (1, 7)]

    def onward(whole, over_x, over_z):
        out = []
        for block, target, copy in (
            (whole.at[2 * c, x_down, pl.ds(0, 2)], to_x(1), over_x[0]),
            (whole.at[2 * c, x_up, pl.ds(2, 2)], to_x(3), over_x[1]),
            (whole.at[2 * c + 1, pl.ds(0, 2), zl_down], to_z(1), over_z[0]),
            (whole.at[2 * c + 1, pl.ds(2, 2), zl_up], to_z(7), over_z[1]),
        ):
            copy.wait_recv()
            out.append(send([(block, block, target)], block))
        return out

    def third(whole, stage):
        for copy in stage:
            copy.wait_recv()
        mine = whole.at[pl.ds(2 * c, 2)]
        return gather(mine, [sibling], mine)

    for copy in own[5:]:
        copy.wait()
    basis_sib.wait_recv()
    a_first = first(abuf)

    def pick():
        row = lax.broadcasted_iota(jnp.int32, (16, TOK), 0)
        col = lax.broadcasted_iota(jnp.int32, (16, TOK), 1)
        wanted = jnp.where(row == 0, idx_ref[0, 0], jnp.where(row == 1, idx_ref[0, 1], -1))
        hot = jnp.where(col == wanted, 1.0, 0.0).astype(BF)
        for i, source in enumerate((acts_v[...], grads_v[...])):
            rows = dot(hot, source)
            for s in range(2):
                for k in range(8):
                    picks[i, s * 8 + k:s * 8 + k + 1, :] = rows[s:s + 1, 128 * k:128 * k + 128]
        pbuf[x, zl, c] = picks[...].astype(BF)
        return gather(pbuf.at[x, zl, c], all_zl, pbuf.at[0, pl.ds(0, 3), 0])

    r1, r2 = {}, {}

    def forward(j):
        r1[j][0].wait_recv()
        sendx2[j, 0] = (tbuf[j, x_up, 0:64, :] + recvx1[j, 0, 0].astype(F32)).astype(BF)
        up = send([(sendx2.at[j, 0], recvx2.at[j, 0], to_x(1))], recvx2.at[j, 0])
        r1[j][1].wait_recv()
        sendx2[j, 1] = (tbuf[j, x_down, 64:128, :] + recvx1[j, 1, 0].astype(F32)).astype(BF)
        down = send([(sendx2.at[j, 1], recvx2.at[j, 1], to_x(3))], recvx2.at[j, 1])
        r2[j] = (up, down)

    for j in range(CHUNKS):
        mine = term(j)
        rc[j].wait_recv()
        tbuf[j] = (mine + recvc[j].astype(F32)).reshape(NX, 128, CW)
        sendx1[j, 0, 0] = tbuf[j, x_far, 0:64, :].astype(BF)
        sendx1[j, 0, 1] = tbuf[j, x_up, 64:128, :].astype(BF)
        sendx1[j, 1, 0] = tbuf[j, x_far, 64:128, :].astype(BF)
        sendx1[j, 1, 1] = tbuf[j, x_down, 0:64, :].astype(BF)
        r1[j] = [
            send([(sendx1.at[j, i], recvx1.at[j, i], to_x(s))], recvx1.at[j, i])
            for i, s in enumerate((1, 3))
        ]
        if j == 2:
            a_first[1].wait_recv()
            a_over_z = near_z(abuf)
            pz = pick()
        if j > 1:
            forward(j - 2)
    forward(CHUNKS - 2)
    forward(CHUNKS - 1)
    ez.wait_recv()
    ex = gather(ebuf.at[x, :, c], all_x, ebuf.at[pl.ds(0, 3), :, 0])
    pz.wait_recv()
    px = gather(pbuf.at[x, :, c], all_x, pbuf.at[pl.ds(0, 3), :, 0])
    a_first[0].wait_recv()
    a_over_x = near_x(abuf)

    rz, ry = {}, {}

    def sum_x(j):
        r2[j][0].wait_recv()
        r2[j][1].wait_recv()
        top = tbuf[j, x, 0:64, :] + recvx1[j, 1, 1].astype(F32) + recvx2[j, 0].astype(F32)
        low = tbuf[j, x, 64:128, :] + recvx1[j, 0, 1].astype(F32) + recvx2[j, 1].astype(F32)
        sendz[j, 0:4] = top.astype(BF).reshape(4, 16, CW)
        sendz[j, 4:8] = low.astype(BF).reshape(4, 16, CW)
        rz[j] = send(
            [(sendz.at[j, (z + s) % NZ], recvz.at[j, i], to_z(s)) for i, s in enumerate(DZ)],
            recvz.at[j],
        )

    def sum_z(j):
        rz[j].wait_recv()
        total = sendz[j, z].astype(F32)
        for i in range(len(DZ)):
            total = total + recvz[j, i].astype(F32)
        sendy[j] = total.astype(BF)
        ry[j] = send(
            [(sendy.at[j], recvy.at[j, i], to_y(s)) for i, s in enumerate(DY)], recvy.at[j]
        )

    sum_x(0)
    sum_x(1)
    sum_z(0)
    sum_x(2)
    sum_z(1)
    sum_x(3)
    sum_z(2)
    ex.wait_recv()
    esib = gather(ebuf.at[:, :, c], [sibling], ebuf.at[:, :, c])
    px.wait_recv()
    psib = gather(pbuf.at[:, :, c], [sibling], pbuf.at[:, :, c])
    sum_z(3)
    a_onward = onward(abuf, a_over_x, a_over_z)
    esib.wait_recv()
    geig = column(geig_ref[...])
    for m in range(8):
        block = ebuf[m // 2, 2 * (m % 2):2 * (m % 2) + 2, :, 0].astype(F32)
        block = block[0, 0] + block[0, 1] + block[1, 0] + block[1, 1]
        eig_row = block[0:1] + block[1:2] + block[2:3]
        recip[:, 128 * m:128 * m + 128] = 1.0 / (geig * eig_row + 0.1)

    psib.wait_recv()
    for i in range(2):
        pwide[...] = pbuf[:, :, :, i].reshape(2 * NX * ZL * 16, 128).astype(F32)
        for k in range(8):
            part = jnp.concatenate(
                [pwide[pl.ds(s * 8 + k, 2 * NX * ZL, stride=16), :] for s in range(2)], axis=0
            )
            xbuf[k] = part.astype(BF)
        wide = jnp.concatenate([xbuf[k] for k in range(8)], axis=1)
        sfull[...] = dot(xbuf[dev // 4], wide, (((0,), (0,)), ((), ())))
        rows = sfull[pl.ds(pl.multiple_of((dev % 4) * 32, 32), 32), :]
        for k in range(8):
            ssend[k, i] = rows[:, 128 * k:128 * k + 128].astype(BF)
    sy = send([(ssend.at[(y + s) % NY], srecv.at[i], to_y(s)) for i, s in enumerate(DY)], srecv)

    high_parts, low_parts = [], []
    for j in range(CHUNKS):
        ry[j].wait_recv()
        total = sendy[j].astype(F32)
        for i in range(len(DY)):
            total = total + recvy[j, i].astype(F32)
        high_parts.append(total.astype(BF))
        low_parts.append((total - total.astype(BF).astype(F32)).astype(BF))
    columns = ebuf[:, :, :, 1:3].reshape(D, 128)
    product = dot(
        jnp.concatenate(
            [jnp.concatenate(high_parts, axis=1), jnp.concatenate(low_parts, axis=1)], axis=0
        ),
        columns,
    )
    gbuf[c * NX + x, z] = (product[0:16] + product[16:32]).astype(BF)
    mine = gbuf.at[c * NX + x]
    gz = gather(mine.at[z], all_z, gbuf.at[0, pl.ds(0, 7)])

    a_third = third(abuf, a_onward)

    sy.wait_recv()
    stat = ssend[y].astype(F32)
    for i in range(len(DY)):
        stat = stat + srecv[i].astype(F32)
    szsend[...] = stat
    sz = send([(szsend, szrecv, to_z(4))], szrecv)

    gz.wait_recv()
    gxc = gather(mine, all_xc, gbuf.at[pl.ds(0, 7)])

    sz.wait_recv()
    sout[y] = (szsend[...] + szrecv[...]).astype(BF)
    so = gather(sout.at[y], all_y, sout.at[pl.ds(0, 7)])

    gxc.wait_recv()
    turned = gbuf[...].reshape(D, 128).T
    a_third.wait_recv()
    total = jnp.zeros((32, 128), F32)
    for q in range(4):
        cols = slice(256 * q, 256 * q + 256)
        scaled = (dot(turned, abuf[q].reshape(D, 256)) * recip[:, cols]).astype(BF)
        total = total + dot(a_ref[:, cols], scaled, NT)
    high = total.astype(BF)
    low = (total - high.astype(F32)).astype(BF)
    partial = dot(jnp.concatenate([high, low], axis=0), columns, NT)
    partial = partial[0:32] + partial[32:64]
    for k in range(8):
        qsend[k] = partial[:, 128 * k:128 * k + 128].astype(BF)
    qr = send([(qsend.at[(y + s) % NY], qrecv.at[i], to_y(s)) for i, s in enumerate(DY)], qrecv)

    qr.wait_recv()
    total = qsend[y].astype(F32)
    for i in range(len(DY)):
        total = total + qrecv[i].astype(F32)
    qbuf[y] = total.astype(BF)
    qy = gather(qbuf.at[y], all_y, qbuf.at[pl.ds(0, 7)])
    drain()
    so.wait_recv()
    for i in range(2):
        for k in range(8):
            out_ref[1 + i, :, 128 * k:128 * k + 128] = sout[k, i]
    qy.wait_recv()
    for k in range(8):
        out_ref[0, :, 128 * k:128 * k + 128] = qbuf[k]


def finish(result_ref, old_act_ref, old_grad_ref, pre_ref, act_ref, grad_ref, *, act_scale, grad_scale):
    pre_ref[...] = result_ref[0].astype(F32)
    act_ref[...] = 0.75 * old_act_ref[...] + act_scale * result_ref[1].astype(F32)
    grad_ref[...] = 0.75 * old_grad_ref[...] + grad_scale * result_ref[2].astype(F32)


def local(
    acts,
    out_grads,
    old_act_factor,
    old_grad_factor,
    act_basis,
    grad_basis,
    act_eigs,
    grad_eigs,
    sample_index,
):
    vmem = pl.BlockSpec(memory_space=pltpu.VMEM)
    hbm = pl.BlockSpec(memory_space=pl.ANY)
    copies = 96
    result = pl.pallas_call(
        kernel,
        out_shape=jax.ShapeDtypeStruct((3, 32, D), BF),
        in_specs=[hbm] * 7,
        out_specs=vmem,
        scratch_shapes=[
            pltpu.SMEM((1, 2), jnp.int32),
            pltpu.VMEM((32, D), BF),
            pltpu.VMEM((1, 32), F32),
            pltpu.VMEM((1, 128), F32),
            pltpu.VMEM((TOK, D), BF),
            pltpu.VMEM((TOK, D), BF),
            pltpu.VMEM((HALF, TOK), BF),
            pltpu.VMEM((CHUNKS, HALF, CW), BF),
            pltpu.VMEM((CHUNKS, HALF, CW), BF),
            pltpu.VMEM((4, NX, ZL, 64, 256), BF),
            pltpu.VMEM((CHUNKS, NX, 128, CW), F32),
            pltpu.VMEM((CHUNKS, 2, 2, 64, CW), BF),
            pltpu.VMEM((CHUNKS, 2, 2, 64, CW), BF),
            pltpu.VMEM((CHUNKS, 2, 64, CW), BF),
            pltpu.VMEM((CHUNKS, 2, 64, CW), BF),
            pltpu.VMEM((CHUNKS, NZ, 16, CW), BF),
            pltpu.VMEM((CHUNKS, 7, 16, CW), BF),
            pltpu.VMEM((CHUNKS, 16, CW), BF),
            pltpu.VMEM((CHUNKS, 7, 16, CW), BF),
            pltpu.VMEM((2 * NX, NZ, 16, 128), BF),
            pltpu.VMEM((128, D), F32),
            pltpu.VMEM((NY, 32, 128), BF),
            pltpu.VMEM((7, 32, 128), BF),
            pltpu.VMEM((NY, 32, 128), BF),
            pltpu.VMEM((8, 128), F32),
            pltpu.VMEM((16, 128), F32),
            pltpu.VMEM((NX, ZL, 2, 3, 16, 128), BF),
            pltpu.VMEM((2, 16, 128), F32),
            pltpu.VMEM((NX, ZL, 2, 2, 16, 128), BF),
            pltpu.VMEM((2 * NX * ZL * 16, 128), F32),
            pltpu.VMEM((8, 64, 128), BF),
            pltpu.VMEM((128, D), F32),
            pltpu.VMEM((NY, 2, 32, 128), BF),
            pltpu.VMEM((7, 2, 32, 128), BF),
            pltpu.VMEM((2, 32, 128), F32),
            pltpu.VMEM((2, 32, 128), F32),
            pltpu.VMEM((NY, 2, 32, 128), BF),
            pltpu.SemaphoreType.DMA((12,)),
            pltpu.SemaphoreType.DMA((copies,)),
            pltpu.SemaphoreType.DMA((copies,)),
        ],
        compiler_params=pltpu.CompilerParams(
            collective_id=0, has_side_effects=True, vmem_limit_bytes=63 * 1024 * 1024
        ),
        cost_estimate=pl.CostEstimate(
            flops=4 * TOK * D * D, bytes_accessed=4 * TOK * D, transcendentals=0
        ),
    )(
        sample_index.reshape(1, 2), acts, out_grads, act_basis, grad_basis,
        act_eigs.reshape(1, 32), grad_eigs.reshape(1, D),
    )
    device_count = lax.axis_size("grp") * lax.axis_size("dev")
    total_samples = device_count * sample_index.shape[0]
    total_tokens = device_count * acts.shape[0]
    return pl.pallas_call(
        functools.partial(
            finish,
            act_scale=0.25 / total_samples,
            grad_scale=0.25 * total_tokens / total_samples,
        ),
        out_shape=(jax.ShapeDtypeStruct((32, D), F32),) * 3,
        in_specs=[vmem] * 3,
        out_specs=(vmem,) * 3,
    )(result, old_act_factor, old_grad_factor)


def solution(mesh):
    return jax.shard_map(
        local,
        mesh=mesh,
        in_specs=(
            P(("grp", "dev"), None),
            P(("grp", "dev"), None),
            P("dev", None),
            P("dev", None),
            P("dev", None),
            P("dev", None),
            P("dev"),
            P(),
            P(("grp", "dev")),
        ),
        out_specs=(P("dev", None), P("dev", None), P("dev", None)),
        check_vma=False,
    )
```

```python
import functools

import jax
import jax.numpy as jnp
from jax import lax
from jax.experimental import pallas as pl
from jax.experimental.pallas import tpu as pltpu
from jax.sharding import PartitionSpec as P

NX, NY, NZ, ZL = 4, 8, 8, 4
D, TOK = 1024, 512
HALF = D // 2
CHUNKS, CW = 4, 256
BF, F32 = jnp.bfloat16, jnp.float32
DX = (2, 1, 3)
DY = (4, 3, 5, 2, 6, 1, 7)
DZ = (4, 3, 5, 2, 6, 1, 7)
DZL = (2, 1, 7)
DXC = tuple((dx, dc) for dx in (2, 1, 3, 0) for dc in (1, 0) if (dx, dc) != (0, 0))
NT = (((1,), (1,)), ((), ()))


def dot(left, right, dims=(((1,), (0,)), ((), ()))):
    return lax.dot_general(left, right, dims, preferred_element_type=F32)


def column(row):
    sub = lax.broadcasted_iota(jnp.int32, (128, 128), 0)
    lane = lax.broadcasted_iota(jnp.int32, (128, 128), 1)
    return jnp.sum(jnp.where(sub == lane, row, 0.0), axis=1, keepdims=True)


def kernel(
    idx_hbm, acts_hbm, grads_hbm, a_hbm, b_hbm, aeig_hbm, geig_hbm,
    out_ref,
    idx_ref, a_ref, aeig_ref, geig_ref,
    acts_v, acts_sv, grads_v, actst, abuf, bbuf,
    tbuf, sendx1, recvx1, sendx2, recvx2, sendz, recvz, sendy, recvy,
    gbuf, recip, qbuf,
    shifted, parts, ebuf, picks, pbuf, pwide, xbuf, sfull, ssend, srecv, szsend, szrecv, sout,
    lsem, ssem, rsem,
):
    grp, dev = lax.axis_index("grp"), lax.axis_index("dev")
    y, zh = grp // 2, grp % 2
    x, zl, c = dev // 8, (dev // 2) % 4, dev % 2
    z = zh * ZL + zl

    def at(px, py, pz, pc):
        return {"grp": py * 2 + pz // ZL, "dev": px * 8 + (pz % ZL) * 2 + pc}

    def to_x(step):
        return at((x + step) % NX, y, z, c)

    def to_y(step):
        return at(x, (y + step) % NY, z, c)

    def to_z(step):
        return at(x, y, (z + step) % NZ, c)

    def to_xc(step):
        return at((x + step[0]) % NX, y, z, (c + step[1]) % 2)

    sibling = at(x, y, z, 1 - c)

    counter = [0]
    pending = []

    def send(moves, like):
        n = counter[0]
        counter[0] += 1

        def copy(src, dst, target):
            return pltpu.make_async_remote_copy(
                src_ref=src, dst_ref=dst, send_sem=ssem.at[n], recv_sem=rsem.at[n],
                device_id=target, device_id_type=pl.DeviceIdType.MESH,
            )

        for move in moves:
            copy(*move).start()
        whole = copy(like, like, sibling)
        pending.append(whole)
        return whole

    def gather(ref, targets, like):
        return send([(ref, ref, target) for target in targets], like)

    def drain(keep=0):
        for copy in pending[:len(pending) - keep]:
            copy.wait_send()
        del pending[:len(pending) - keep]

    all_x = [to_x(s) for s in DX]
    all_y = [to_y(s) for s in DY]
    all_z = [to_z(s) for s in DZ]
    all_zl = [to_z(s) for s in DZL]
    all_xc = [to_xc(s) for s in DXC]
    x_up, x_down, x_far = (x + 1) % NX, (x + 3) % NX, (x + 2) % NX
    zl_up, zl_down = (zl + 1) % ZL, (zl + 3) % ZL

    barrier = pltpu.get_barrier_semaphore()
    partners = all_xc + all_y + all_z
    for partner in partners:
        pl.semaphore_signal(
            barrier, inc=1, device_id=partner, device_id_type=pl.DeviceIdType.MESH
        )

    my_rows = pl.ds(pl.multiple_of(c * 32, 32), 32)
    my_cols = pl.ds(pl.multiple_of(y * 128, 128), 128)

    def half(ref, side):
        return ref.at[:, pl.ds(pl.multiple_of(side * HALF, HALF), HALF)]

    def quarter(ref, side, h):
        return ref.at[:, pl.ds(pl.multiple_of(side * HALF + h * 256, 256), 256)]

    moves = [
        (aeig_hbm, aeig_ref),
        (b_hbm.at[pl.ds(0, 16), my_cols], ebuf.at[x, zl, c, 1]),
        (b_hbm.at[pl.ds(16, 16), my_cols], ebuf.at[x, zl, c, 2]),
        (acts_hbm, acts_v), (grads_hbm, grads_v.at[0]), (idx_hbm, idx_ref),
        (geig_hbm.at[:, my_cols], geig_ref), (a_hbm, a_ref),
    ]
    for source, whole in ((a_hbm, abuf), (b_hbm, bbuf)):
        for h in range(2):
            moves.append((quarter(source, c, h), whole.at[2 * c + h, x, zl, my_rows]))
    own = [pltpu.make_async_copy(src, dst, lsem.at[i]) for i, (src, dst) in enumerate(moves)]
    for copy in own[3:5]:
        copy.start()
    own[3].wait()
    mine = acts_v[:, pl.ds(pl.multiple_of(c * HALF, HALF), HALF)]
    for k in range(2):
        for t in range(2):
            actst[256 * k:256 * k + 256, 256 * t:256 * t + 256] = (
                mine[256 * t:256 * t + 256, 256 * k:256 * k + 256].T
            )

    pl.semaphore_wait(barrier, len(partners))

    basis_sib = []
    for source, whole in ((a_hbm, abuf), (b_hbm, bbuf)):
        basis_sib.append(send(
            [
                (quarter(source, 1 - c, h), whole.at[2 * (1 - c) + h, x, zl, my_rows], sibling)
                for h in range(2)
            ],
            whole.at[pl.ds(0, 2), 0, 0, pl.ds(0, 32)],
        ))

    acts_sib = send([(half(acts_hbm, 1 - c), acts_sv, sibling)], acts_sv)
    grads_sib = []
    for j in range(CHUNKS):
        piece = grads_v.at[1, :, pl.ds(CW * j, CW)]
        grads_sib.append(send([(grads_hbm.at[:, pl.ds(CW * j, CW)], piece, sibling)], piece))
    for copy in own[:3] + own[5:]:
        copy.start()

    own[0].wait()
    shifted[...] = jnp.zeros((8, 128), F32)
    shifted[0:1, 0:32] = aeig_ref[...]
    eigs = pltpu.roll(shifted[...], (dev % 4) * 32, 1)[0:1, :]
    high = eigs.astype(BF).astype(F32)
    middle = (eigs - high).astype(BF).astype(F32)
    parts[...] = jnp.zeros((16, 128), F32)
    parts[0:1, :] = high
    parts[1:2, :] = middle
    parts[2:3, :] = eigs - high - middle
    ebuf[x, zl, c, 0] = parts[...].astype(BF)
    for copy in own[1:3]:
        copy.wait()
    ez = gather(ebuf.at[x, zl, c], all_zl, ebuf.at[0, pl.ds(0, 3), 0])

    def first(whole):
        return (
            gather(whole.at[2 * c, x, zl], all_zl, whole.at[0, 0, pl.ds(0, 3)]),
            gather(whole.at[2 * c + 1, x, zl], all_x, whole.at[0, 0, pl.ds(0, 3)]),
        )

    def near_x(whole):
        mine = whole.at[2 * c, x]
        return [send([(mine, mine, to_x(s))], mine) for s in (1, 3)]

    def near_z(whole):
        mine = whole.at[2 * c + 1, :, zl]
        return [send([(mine, mine, to_z(s))], mine) for s in (1, 7)]

    def onward(whole, over_x, over_z):
        out = []
        for block, target, copy in (
            (whole.at[2 * c, x_down, pl.ds(0, 2)], to_x(1), over_x[0]),
            (whole.at[2 * c, x_up, pl.ds(2, 2)], to_x(3), over_x[1]),
            (whole.at[2 * c + 1, pl.ds(0, 2), zl_down], to_z(1), over_z[0]),
            (whole.at[2 * c + 1, pl.ds(2, 2), zl_up], to_z(7), over_z[1]),
        ):
            copy.wait_recv()
            out.append(send([(block, block, target)], block))
        return out

    def third(whole, stage):
        for copy in stage:
            copy.wait_recv()
        mine = whole.at[pl.ds(2 * c, 2)]
        return gather(mine, [sibling], mine)

    for copy in own[4:]:
        copy.wait()
    basis_sib[0].wait_recv()
    a_first = first(abuf)

    def term(slot, j):
        part = dot(
            actst[:, slot * TOK:slot * TOK + TOK], grads_v[slot, :, CW * j:CW * j + CW]
        )
        return part.reshape(NX, 128, CW)

    for j in range(CHUNKS):
        tbuf[j] = term(0, j)
    acts_sib.wait_recv()
    for k in range(2):
        for t in range(2):
            actst[256 * k:256 * k + 256, TOK + 256 * t:TOK + 256 * t + 256] = (
                acts_sv[256 * t:256 * t + 256, 256 * k:256 * k + 256].T
            )

    def pick():
        row = lax.broadcasted_iota(jnp.int32, (16, TOK), 0)
        col = lax.broadcasted_iota(jnp.int32, (16, TOK), 1)
        wanted = jnp.where(row == 0, idx_ref[0, 0], jnp.where(row == 1, idx_ref[0, 1], -1))
        hot = jnp.where(col == wanted, 1.0, 0.0).astype(BF)
        for i, source in enumerate((acts_v[...], grads_v[0])):
            rows = dot(hot, source)
            for s in range(2):
                for k in range(8):
                    picks[i, s * 8 + k:s * 8 + k + 1, :] = rows[s:s + 1, 128 * k:128 * k + 128]
        pbuf[x, zl, c] = picks[...].astype(BF)
        return gather(pbuf.at[x, zl, c], all_zl, pbuf.at[0, pl.ds(0, 3), 0])

    r1, r2 = {}, {}

    def forward(j):
        r1[j][0].wait_recv()
        sendx2[j, 0] = (tbuf[j, x_up, 0:64, :] + recvx1[j, 0, 0].astype(F32)).astype(BF)
        up = send([(sendx2.at[j, 0], recvx2.at[j, 0], to_x(1))], recvx2.at[j, 0])
        r1[j][1].wait_recv()
        sendx2[j, 1] = (tbuf[j, x_down, 64:128, :] + recvx1[j, 1, 0].astype(F32)).astype(BF)
        down = send([(sendx2.at[j, 1], recvx2.at[j, 1], to_x(3))], recvx2.at[j, 1])
        r2[j] = (up, down)

    for j in range(CHUNKS):
        grads_sib[j].wait_recv()
        tbuf[j] = tbuf[j] + term(1, j)
        sendx1[j, 0, 0] = tbuf[j, x_far, 0:64, :].astype(BF)
        sendx1[j, 0, 1] = tbuf[j, x_up, 64:128, :].astype(BF)
        sendx1[j, 1, 0] = tbuf[j, x_far, 64:128, :].astype(BF)
        sendx1[j, 1, 1] = tbuf[j, x_down, 0:64, :].astype(BF)
        r1[j] = [
            send([(sendx1.at[j, i], recvx1.at[j, i], to_x(s))], recvx1.at[j, i])
            for i, s in enumerate((1, 3))
        ]
        if j == 2:
            a_first[1].wait_recv()
            a_over_z = near_z(abuf)
            pz = pick()
        if j > 1:
            forward(j - 2)
    forward(CHUNKS - 2)
    forward(CHUNKS - 1)
    ez.wait_recv()
    ex = gather(ebuf.at[x, :, c], all_x, ebuf.at[pl.ds(0, 3), :, 0])
    pz.wait_recv()
    px = gather(pbuf.at[x, :, c], all_x, pbuf.at[pl.ds(0, 3), :, 0])
    a_first[0].wait_recv()
    a_over_x = near_x(abuf)
    basis_sib[1].wait_recv()
    b_first = first(bbuf)

    rz, ry = {}, {}

    def sum_x(j):
        r2[j][0].wait_recv()
        r2[j][1].wait_recv()
        top = tbuf[j, x, 0:64, :] + recvx1[j, 1, 1].astype(F32) + recvx2[j, 0].astype(F32)
        low = tbuf[j, x, 64:128, :] + recvx1[j, 0, 1].astype(F32) + recvx2[j, 1].astype(F32)
        sendz[j, 0:4] = top.astype(BF).reshape(4, 16, CW)
        sendz[j, 4:8] = low.astype(BF).reshape(4, 16, CW)
        rz[j] = send(
            [(sendz.at[j, (z + s) % NZ], recvz.at[j, i], to_z(s)) for i, s in enumerate(DZ)],
            recvz.at[j],
        )

    def sum_z(j):
        rz[j].wait_recv()
        total = sendz[j, z].astype(F32)
        for i in range(len(DZ)):
            total = total + recvz[j, i].astype(F32)
        sendy[j] = total.astype(BF)
        ry[j] = send(
            [(sendy.at[j], recvy.at[j, i], to_y(s)) for i, s in enumerate(DY)], recvy.at[j]
        )

    sum_x(0)
    sum_x(1)
    sum_z(0)
    sum_x(2)
    sum_z(1)
    sum_x(3)
    sum_z(2)
    ex.wait_recv()
    esib = gather(ebuf.at[:, :, c], [sibling], ebuf.at[:, :, c])
    sum_z(3)
    for copy in b_first:
        copy.wait_recv()
    a_onward = onward(abuf, a_over_x, a_over_z)
    b_over_x, b_over_z = near_x(bbuf), near_z(bbuf)
    px.wait_recv()
    psib = gather(pbuf.at[:, :, c], [sibling], pbuf.at[:, :, c])

    esib.wait_recv()
    geig = column(geig_ref[...])
    for m in range(8):
        block = ebuf[m // 2, 2 * (m % 2):2 * (m % 2) + 2, :, 0].astype(F32)
        block = block[0, 0] + block[0, 1] + block[1, 0] + block[1, 1]
        eig_row = block[0:1] + block[1:2] + block[2:3]
        recip[:, 128 * m:128 * m + 128] = 1.0 / (geig * eig_row + 0.1)

    high_parts, low_parts = [], []
    for j in range(CHUNKS):
        ry[j].wait_recv()
        total = sendy[j].astype(F32)
        for i in range(len(DY)):
            total = total + recvy[j, i].astype(F32)
        high_parts.append(total.astype(BF))
        low_parts.append((total - total.astype(BF).astype(F32)).astype(BF))
    columns = ebuf[:, :, :, 1:3].reshape(D, 128)
    product = dot(
        jnp.concatenate(
            [jnp.concatenate(high_parts, axis=1), jnp.concatenate(low_parts, axis=1)], axis=0
        ),
        columns,
    )
    gbuf[c * NX + x, z] = (product[0:16] + product[16:32]).astype(BF)
    mine = gbuf.at[c * NX + x]
    gz = gather(mine.at[z], all_z, gbuf.at[0, pl.ds(0, 7)])

    psib.wait_recv()
    for i in range(2):
        pwide[...] = pbuf[:, :, :, i].reshape(2 * NX * ZL * 16, 128).astype(F32)
        for k in range(8):
            part = jnp.concatenate(
                [pwide[pl.ds(s * 8 + k, 2 * NX * ZL, stride=16), :] for s in range(2)], axis=0
            )
            xbuf[k] = part.astype(BF)
        wide = jnp.concatenate([xbuf[k] for k in range(8)], axis=1)
        sfull[...] = dot(xbuf[dev // 4], wide, (((0,), (0,)), ((), ())))
        rows = sfull[pl.ds(pl.multiple_of((dev % 4) * 32, 32), 32), :]
        for k in range(8):
            ssend[k, i] = rows[:, 128 * k:128 * k + 128].astype(BF)
    sy = send([(ssend.at[(y + s) % NY], srecv.at[i], to_y(s)) for i, s in enumerate(DY)], srecv)

    b_onward = onward(bbuf, b_over_x, b_over_z)
    gz.wait_recv()
    gxc = gather(mine, all_xc, gbuf.at[pl.ds(0, 7)])
    a_third = third(abuf, a_onward)

    sy.wait_recv()
    stat = ssend[y].astype(F32)
    for i in range(len(DY)):
        stat = stat + srecv[i].astype(F32)
    szsend[...] = stat
    sz = send([(szsend, szrecv, to_z(4))], szrecv)

    drain(12)
    gxc.wait_recv()
    turned = gbuf[...].reshape(D, 128).T
    a_third.wait_recv()
    total = jnp.zeros((32, 128), F32)
    for q in range(4):
        cols = slice(256 * q, 256 * q + 256)
        scaled = (dot(turned, abuf[q].reshape(D, 256)) * recip[:, cols]).astype(BF)
        total = total + dot(a_ref[:, cols], scaled, NT)
    qbuf[y] = total.astype(BF)
    qy = gather(qbuf.at[y], all_y, qbuf.at[pl.ds(0, 7)])
    b_third = third(bbuf, b_onward)

    sz.wait_recv()
    sout[y] = (szsend[...] + szrecv[...]).astype(BF)
    so = gather(sout.at[y], all_y, sout.at[pl.ds(0, 7)])
    drain()

    qy.wait_recv()
    left = jnp.concatenate([qbuf[k] for k in range(8)], axis=1)
    b_third.wait_recv()
    total = dot(left[:, 0:256], bbuf[0].reshape(D, 256), NT)
    for q in range(1, 4):
        total = total + dot(left[:, 256 * q:256 * q + 256], bbuf[q].reshape(D, 256), NT)
    out_ref[0] = total
    so.wait_recv()
    for i in range(2):
        for k in range(8):
            out_ref[1 + i, :, 128 * k:128 * k + 128] = sout[k, i].astype(F32)


def finish(result_ref, old_act_ref, old_grad_ref, pre_ref, act_ref, grad_ref, *, act_scale, grad_scale):
    pre_ref[...] = result_ref[0]
    act_ref[...] = 0.75 * old_act_ref[...] + act_scale * result_ref[1]
    grad_ref[...] = 0.75 * old_grad_ref[...] + grad_scale * result_ref[2]


def local(
    acts,
    out_grads,
    old_act_factor,
    old_grad_factor,
    act_basis,
    grad_basis,
    act_eigs,
    grad_eigs,
    sample_index,
):
    vmem = pl.BlockSpec(memory_space=pltpu.VMEM)
    hbm = pl.BlockSpec(memory_space=pl.ANY)
    copies = 96
    result = pl.pallas_call(
        kernel,
        out_shape=jax.ShapeDtypeStruct((3, 32, D), F32),
        in_specs=[hbm] * 7,
        out_specs=vmem,
        scratch_shapes=[
            pltpu.SMEM((1, 2), jnp.int32),
            pltpu.VMEM((32, D), BF),
            pltpu.VMEM((1, 32), F32),
            pltpu.VMEM((1, 128), F32),
            pltpu.VMEM((TOK, D), BF),
            pltpu.VMEM((TOK, HALF), BF),
            pltpu.VMEM((2, TOK, D), BF),
            pltpu.VMEM((HALF, 2 * TOK), BF),
            pltpu.VMEM((4, NX, ZL, 64, 256), BF),
            pltpu.VMEM((4, NX, ZL, 64, 256), BF),
            pltpu.VMEM((CHUNKS, NX, 128, CW), F32),
            pltpu.VMEM((CHUNKS, 2, 2, 64, CW), BF),
            pltpu.VMEM((CHUNKS, 2, 2, 64, CW), BF),
            pltpu.VMEM((CHUNKS, 2, 64, CW), BF),
            pltpu.VMEM((CHUNKS, 2, 64, CW), BF),
            pltpu.VMEM((CHUNKS, NZ, 16, CW), BF),
            pltpu.VMEM((CHUNKS, 7, 16, CW), BF),
            pltpu.VMEM((CHUNKS, 16, CW), BF),
            pltpu.VMEM((CHUNKS, 7, 16, CW), BF),
            pltpu.VMEM((2 * NX, NZ, 16, 128), BF),
            pltpu.VMEM((128, D), F32),
            pltpu.VMEM((NY, 32, 128), BF),
            pltpu.VMEM((8, 128), F32),
            pltpu.VMEM((16, 128), F32),
            pltpu.VMEM((NX, ZL, 2, 3, 16, 128), BF),
            pltpu.VMEM((2, 16, 128), F32),
            pltpu.VMEM((NX, ZL, 2, 2, 16, 128), BF),
            pltpu.VMEM((2 * NX * ZL * 16, 128), F32),
            pltpu.VMEM((8, 64, 128), BF),
            pltpu.VMEM((128, D), F32),
            pltpu.VMEM((NY, 2, 32, 128), BF),
            pltpu.VMEM((7, 2, 32, 128), BF),
            pltpu.VMEM((2, 32, 128), F32),
            pltpu.VMEM((2, 32, 128), F32),
            pltpu.VMEM((NY, 2, 32, 128), BF),
            pltpu.SemaphoreType.DMA((12,)),
            pltpu.SemaphoreType.DMA((copies,)),
            pltpu.SemaphoreType.DMA((copies,)),
        ],
        compiler_params=pltpu.CompilerParams(
            collective_id=0, has_side_effects=True, vmem_limit_bytes=63 * 1024 * 1024
        ),
        cost_estimate=pl.CostEstimate(
            flops=4 * TOK * D * D, bytes_accessed=4 * TOK * D, transcendentals=0
        ),
    )(
        sample_index.reshape(1, 2), acts, out_grads, act_basis, grad_basis,
        act_eigs.reshape(1, 32), grad_eigs.reshape(1, D),
    )
    device_count = lax.axis_size("grp") * lax.axis_size("dev")
    total_samples = device_count * sample_index.shape[0]
    total_tokens = device_count * acts.shape[0]
    return pl.pallas_call(
        functools.partial(
            finish,
            act_scale=0.25 / total_samples,
            grad_scale=0.25 * total_tokens / total_samples,
        ),
        out_shape=(jax.ShapeDtypeStruct((32, D), F32),) * 3,
        in_specs=[vmem] * 3,
        out_specs=(vmem,) * 3,
    )(result, old_act_factor, old_grad_factor)


def solution(mesh):
    return jax.shard_map(
        local,
        mesh=mesh,
        in_specs=(
            P(("grp", "dev"), None),
            P(("grp", "dev"), None),
            P("dev", None),
            P("dev", None),
            P("dev", None),
            P("dev", None),
            P("dev"),
            P(),
            P(("grp", "dev")),
        ),
        out_specs=(P("dev", None), P("dev", None), P("dev", None)),
        check_vma=False,
    )
```
